256 devices in a mesh: rep: 8 (over z_hi, x), fsdp: 32 (over y, z_lo, core).
Axes of the slice: x: 4, y: 4, z: 8 (z_hi: 2, z_lo: 4; z = z_hi * 4 + z_lo), core: 2. Of those that a mesh axis runs over, the one named last changes fastest.
Arguments:
- momentum: float32 [8, 2048, 4096], P('rep', 'fsdp'), may hold values from -6 to 6
- gradient: bfloat16 [8, 2048, 4096], P('rep', 'fsdp'), may hold values from -6 to 6
- weight: bfloat16 [2048, 4096], P('fsdp'), may hold values from -0.09375 to 0.09375
- activations: bfloat16 [131072, 4096], P(('rep', 'fsdp')), may hold values from -6 to 6
Outputs:
- new_momentum: float32 [8, 2048, 4096], P('rep', 'fsdp')
- direction: float32 [2048, 4096], P('fsdp')
- projected: bfloat16 [131072, 2048], P(('rep', 'fsdp'))
The draws below stay inside these ranges and needn't reach their ends.
All inputs are finite; a program needn't handle non-finite values.
Results may differ from the reference program's by a relative error of at most 0.012.
Values may be sent and summed in bfloat16 or wider, within the bound.
No kernel may reach another device: no remote copies, remote signals or barrier semaphores. Data moves between devices by JAX's collectives and lax.ppermute only.
A program may use at most 192 MiB of HBM per device.

```python
import math
import jax
import jax.numpy as jnp
from jax import lax

COLS = 4096
TILE = 64
BAND = 16
REP = 8
ROWS = 2048
TOKENS = 131072


def level_of(key, extent, cuts, least, largest):
    level, own = 1.0, jax.random.fold_in(key, 6)
    for dim, parts in cuts:
        steps = jnp.exp(jax.random.uniform(jax.random.fold_in(own, dim), (parts,), jnp.float32, least / len(cuts), largest / len(cuts)))
        level = level * jnp.repeat(steps, extent[dim] // parts).reshape([-1 if axis == dim else 1 for axis in range(len(extent))])
    return level


def bell_draw(own_key, extent, scale, bound, split=(), kind=jnp.bfloat16):
    result = jax.random.normal(own_key, extent, jnp.float32) * scale
    if len(split) > 0:
        result = level_of(own_key, extent, split, -0.22, 0.18) * result
    return jnp.clip(result, min=-bound, max=bound).astype(kind)


def setup_inputs(seed: int = 0) -> dict:
    splits = jax.random.split(jax.random.key(seed), 5)
    return {
        "momentum": bell_draw(splits[0], (REP, ROWS, COLS), 1.0, 6.0, ((0, 8), (1, 32)), jnp.float32),
        "gradient": bell_draw(splits[1], (REP, ROWS, COLS), 1.0, 6.0, ((0, 8), (1, 32))),
        "weight": bell_draw(splits[2], (ROWS, COLS), COLS ** -0.5, 0.09375, ((0, 32),)),
        "activations": bell_draw(splits[3], (TOKENS, COLS), 1.0, 6.0, ((0, 256),)),
    }


highest = lax.Precision.HIGHEST
momentum_decay = 0.9
step_rate = 0.02
soft_width = 0.25

def cosine_rows():
    freq = jnp.arange(BAND, dtype=jnp.float32)[:, None]
    place = jnp.arange(TILE, dtype=jnp.float32)[None, :]
    factor = jnp.where(freq == 0.0, math.sqrt(1.0 / TILE), math.sqrt(2.0 / TILE))
    return factor * jnp.cos(math.pi * (2.0 * place + 1.0) * freq / (2.0 * TILE))

def low_band(field, cosines):
    blocks = field.shape[0] // TILE
    width = field.shape[1]
    row_pass = jnp.einsum('ai,kic->kac', cosines, field.reshape(blocks, TILE, width), precision=highest)
    row_pass = row_pass.reshape(blocks, BAND, width // TILE, TILE)
    coefficients = jnp.einsum('bj,katj->katb', cosines, row_pass, precision=highest)
    return coefficients.reshape(blocks * BAND, width // TILE * BAND)

def restore(coefficients, cosines, width):
    blocks = coefficients.shape[0] // BAND
    tiles = width // TILE
    col_pass = jnp.einsum('katb,bj->katj', coefficients.reshape(blocks, BAND, tiles, BAND), cosines, precision=highest)
    col_pass = col_pass.reshape(blocks, BAND, width)
    return jnp.einsum('ai,kac->kic', cosines, col_pass, precision=highest).reshape(blocks * TILE, width)

def reference(momentum, gradient, weight, activations):
    cosines = cosine_rows()
    mixed = momentum_decay * momentum + gradient.astype(jnp.float32)
    bands = jax.vmap(lambda field: low_band(field, cosines))(mixed)
    new_momentum = mixed - jax.vmap(lambda coef: restore(coef, cosines, COLS))(bands)
    total = lax.optimization_barrier(jnp.sum(bands, axis=0))
    update = restore(total, cosines, COLS)
    direction = update * lax.rsqrt(update * update + soft_width)
    new_weight = (weight.astype(jnp.float32) - step_rate * direction).astype(jnp.bfloat16)
    projected = lax.dot_general(activations, new_weight, (((1,), (1,)), ((), ())), preferred_element_type=jnp.float32)
    return (new_momentum, direction, projected.astype(jnp.bfloat16))
```

```python
import math

import jax
import jax.numpy as jnp
import numpy as np
from jax import lax
from jax.experimental import pallas as pl
from jax.experimental.pallas import tpu as pltpu
from jax.sharding import PartitionSpec as P

TILE = 64
BAND = 16
WIDE = 8
AXES = ("rep", "fsdp")

momentum_decay = 0.9
step_rate = 0.02
soft_width = 0.25

F32 = jnp.float32
BF16 = jnp.bfloat16
NT = (((1,), (1,)), ((), ()))


def cosine_rows():
    freq = np.arange(BAND, dtype=np.float64)[:, None]
    place = np.arange(TILE, dtype=np.float64)[None, :]
    factor = np.where(freq == 0.0, math.sqrt(1.0 / TILE), math.sqrt(2.0 / TILE))
    return factor * np.cos(math.pi * (2.0 * place + 1.0) * freq / (2.0 * TILE))


def halves(array):
    high = np.asarray(array, np.float32).astype(jnp.bfloat16)
    low = (np.asarray(array, np.float64) - high.astype(np.float64)).astype(jnp.bfloat16)
    return high, low


def split(value):
    high = value.astype(BF16)
    return high, (value - high.astype(F32)).astype(BF16)


def dot(a, b):
    return jnp.dot(a, b, preferred_element_type=F32)


def spot(index):
    rep, rest = divmod(index, 32)
    high, x = divmod(rep, 4)
    y, rest = divmod(rest, 8)
    low, core = divmod(rest, 2)
    return x, y, high * 4 + low, core


def place(x, y, z, core):
    x, y, z = x % 4, y % 4, z % 8
    return ((z // 4) * 4 + x) * 32 + y * 8 + (z % 4) * 2 + core


def fetch(value, source):
    return lax.ppermute(value, AXES, [(place(*source(*spot(i))), i) for i in range(256)])


def along(axis, step):
    def source(x, y, z, core):
        if (core + axis) % 2 == 0:
            return x, y + step, z, core
        if step == 2 and z % 2:
            return x, y, z - 2, core
        return x, y, z + step, core

    return source


def along_x(step):
    return lambda x, y, z, core: (x + step, y, z, core)


def far_z(x, y, z, core):
    return x, y, z + 4, core


def sibling(x, y, z, core):
    return x, y, z, 1 - core


def call(kernel, out_shape, inputs, scratch=(), limit=16, flops=0, smem=0):
    specs = [pl.BlockSpec(memory_space=pltpu.SMEM)] * smem
    specs += [pl.BlockSpec(memory_space=pltpu.VMEM)] * (len(inputs) - smem)
    moved = sum(math.prod(v.shape) * v.dtype.itemsize for v in inputs)
    return pl.pallas_call(
        kernel,
        out_shape=out_shape,
        in_specs=specs,
        out_specs=jax.tree.map(lambda _: pl.BlockSpec(memory_space=pltpu.VMEM), out_shape),
        scratch_shapes=list(scratch),
        compiler_params=pltpu.CompilerParams(vmem_limit_bytes=limit << 20),
        cost_estimate=pl.CostEstimate(flops=flops, bytes_accessed=moved, transcendentals=0),
    )(*inputs)


def stacked(value, wide):
    return jnp.concatenate(
        [value[:, k * wide : (k + 1) * wide] for k in range(value.shape[1] // wide)], axis=0
    )


def mixed_of(momentum, gradient):
    return momentum_decay * momentum[0] + gradient[0].astype(F32)


def bands_kernel(momentum, gradient, cols_hi, cols_lo, rows3, exact, rounded):
    high, low = split(mixed_of(momentum, gradient))
    high = stacked(high, WIDE * TILE)
    low = stacked(low, WIDE * TILE)
    narrow = dot(high, cols_hi[...]) + dot(low, cols_hi[...]) + dot(high, cols_lo[...])
    narrow = jnp.concatenate(
        [narrow[k * TILE : (k + 1) * TILE] for k in range(narrow.shape[0] // TILE)], axis=1
    )
    high, low = split(narrow)
    bands = dot(rows3[...], jnp.concatenate([high, low, high], axis=0))
    exact[...] = bands
    rounded[...] = bands.astype(BF16)


def restored(bands, back_rows3, back_hi, back_lo):
    high, low = split(bands)
    tall = dot(back_rows3[...], jnp.concatenate([high, low, high], axis=0))
    high, low = split(stacked(tall, WIDE * BAND))
    return dot(high, back_hi[...]) + dot(low, back_hi[...]) + dot(high, back_lo[...])


def residual_kernel(momentum, gradient, bands, back_rows3, back_hi, back_lo, out):
    mixed = mixed_of(momentum, gradient)
    low = restored(bands[...], back_rows3, back_hi, back_lo)
    wide = WIDE * TILE
    for k in range(mixed.shape[1] // wide):
        cut = slice(k * wide, (k + 1) * wide)
        out[0, :, cut] = mixed[:, cut] - low[k * TILE : (k + 1) * TILE]


def soft_sign(update):
    return update * lax.rsqrt(update * update + soft_width)


def direction_kernel(total, back_rows3, back_hi, back_lo, out):
    sign = soft_sign(restored(total[...], back_rows3, back_hi, back_lo))
    wide = WIDE * TILE
    for k in range(out.shape[1] // wide):
        out[:, k * wide : (k + 1) * wide] = sign[k * TILE : (k + 1) * TILE]


def forward_kernel(parts, first, own, other, back_rows, back_cols, *refs):
    groups = len(parts)
    refs = list(refs)
    bands = [refs.pop(0) for _ in range(groups)]
    weights = [[refs.pop(0) for _ in range(n)] for n in parts]
    outs = [refs.pop(0) for _ in range(2 * groups)]
    tall, fresh, total = refs
    wide = WIDE * TILE
    steps = own.shape[1] // wide
    start = first[0]

    for g in range(groups):
        spread = dot(back_rows[...], bands[g][...]).astype(BF16)
        for k in range(steps):
            tall[k] = spread[:, k * WIDE * BAND : (k + 1) * WIDE * BAND]

        def renew(k, slot, g=g):
            cut = pl.ds(pl.multiple_of(k * wide, wide), wide)
            sign = soft_sign(dot(tall[k], back_cols[...]))
            row = 0
            for ref in weights[g]:
                rows = ref.shape[0]
                for r in range(0, rows, TILE):
                    new = ref[r : r + TILE, cut].astype(F32) - step_rate * sign[row : row + TILE]
                    spot_ = lax.rem(start + row // TILE, 4) * TILE
                    fresh[slot, pl.ds(pl.multiple_of(spot_, TILE), TILE), :] = new.astype(BF16)
                    row += TILE

        def multiply(k, slot):
            cut = pl.ds(pl.multiple_of(k * wide, wide), wide)
            rows = own.shape[0]
            for n, ref in enumerate((own, other)):
                total[n * rows : (n + 1) * rows] += lax.dot_general(
                    ref[:, cut], fresh[slot], NT, preferred_element_type=F32
                )

        total[...] = jnp.zeros_like(total)
        renew(0, 0)

        @pl.loop(0, steps // 2)
        def _(pair):
            k = pair * 2
            multiply(k, 0)
            renew(k + 1, 1)
            multiply(k + 1, 1)
            renew(lax.rem(k + 2, steps), 0)

        rows = own.shape[0]
        outs[2 * g][...] = total[:rows].astype(BF16)
        outs[2 * g + 1][...] = total[rows:].astype(BF16)


def weave_kernel(where, *refs):
    mine, theirs, out, held = refs[:4], refs[4:8], refs[8], refs[9]
    core, my_start, their_start = where[0], where[1], where[2]
    for g in range(4):
        held[core, lax.rem(my_start + g, 4)] = mine[g][...]
        held[1 - core, lax.rem(their_start + g, 4)] = theirs[g][...]
    for y in range(4):
        for z in range(4):
            left = held[0, z, :, y * TILE : (y + 1) * TILE]
            right = held[1, y, :, z * TILE : (z + 1) * TILE]
            j = (y * 4 + z) * 2 * TILE
            out[:, j : j + 2 * TILE] = jnp.concatenate([left, right], axis=1)


def on_device(momentum, gradient, weight, activations):
    cosines = cosine_rows()
    high, low = halves(cosines)
    eye = np.eye(WIDE)
    cols_hi, cols_lo = (np.kron(eye, np.asarray(h, np.float32).T).astype(jnp.bfloat16) for h in (high, low))
    rows3 = np.concatenate([high, high, low], axis=1)
    back_rows3 = np.concatenate([high.T, high.T, low.T], axis=1)
    back_hi, back_lo = cols_hi.T, cols_lo.T
    back_rows = np.kron(np.eye(4), np.asarray(high, np.float32).T).astype(jnp.bfloat16)
    width = weight.shape[1]
    narrow = width // TILE * BAND
    rows = weight.shape[0]
    tokens = activations.shape[0]

    core = lax.axis_index("fsdp") % 2
    y = lax.axis_index("fsdp") // 8
    z = lax.axis_index("fsdp") // 2 % 4
    first = jnp.where(core == 0, y, z).astype(jnp.int32)
    second = jnp.where(core == 0, z, y).astype(jnp.int32)

    shape = jax.ShapeDtypeStruct
    exact, rounded = call(
        bands_kernel,
        (shape((BAND, narrow), F32), shape((BAND, narrow), BF16)),
        (momentum, gradient, cols_hi, cols_lo, rows3),
    )

    ahead, behind, across = (fetch(weight, along(0, s)) for s in (1, -1, 2))
    line = jnp.concatenate([weight, ahead, across, behind], axis=0)

    total = rounded.astype(F32)
    for part in [fetch(rounded, along_x(s)) for s in (1, -1, 2)]:
        total = total + part.astype(F32)
    sent = total.astype(BF16)
    total = sent.astype(F32) + fetch(sent, far_z).astype(F32)

    new_momentum = call(
        residual_kernel,
        shape(momentum.shape, F32),
        (momentum, gradient, exact, back_rows3, back_hi, back_lo),
    )
    other = fetch(activations, sibling)

    sent = total.astype(BF16)
    ahead, behind, across = (fetch(sent, along(0, s)) for s in (1, -1, 2))
    band_line = jnp.concatenate([sent, ahead, across, behind], axis=0)
    bands = [band_line] + [fetch(band_line, along(1, s)) for s in (1, 2, -1)]

    next_line = fetch(line, along(1, 1))
    last_line = fetch(line, along(1, -1))
    half = line.shape[0] // 2
    far_a = fetch(next_line[:half], along(1, 1))
    far_b = fetch(last_line[half:], along(1, -1))
    lines = [[line], [next_line], [far_a, far_b], [last_line]]

    direction = call(
        direction_kernel,
        shape((rows, width), F32),
        (total, back_rows3, back_hi, back_lo),
    )

    def forward(order):
        parts = [len(lines[g]) for g in order]
        inputs = [first[None], activations, other, back_rows, back_hi]
        inputs += [bands[g] for g in order]
        for g in order:
            inputs += lines[g]
        block = shape((tokens, 4 * rows), BF16)
        return call(
            lambda *refs: forward_kernel(parts, *refs),
            tuple([block] * (2 * len(order))),
            inputs,
            (
                pltpu.VMEM((width // (WIDE * TILE), 4 * rows, WIDE * BAND), BF16),
                pltpu.VMEM((2, 4 * rows, WIDE * TILE), BF16),
                pltpu.VMEM((2 * tokens, 4 * rows), F32),
            ),
            limit=40,
            flops=len(order) * 2 * 2 * tokens * 4 * rows * width,
            smem=1,
        )

    mine, theirs = [None] * 4, [None] * 4
    for order in ([0], [1, 3, 2]):
        result = forward(order)
        for n, g in enumerate(order):
            mine[g] = result[2 * n]
            theirs[g] = fetch(result[2 * n + 1], sibling)
    where = jnp.stack([core.astype(jnp.int32), second, first])
    projected = call(
        weave_kernel,
        shape((tokens, 32 * rows), BF16),
        (where, *mine, *theirs),
        (pltpu.VMEM((2, 4, tokens, 4 * rows), BF16),),
        smem=1,
    )
    return (new_momentum, direction, projected)


def solution(mesh):
    return jax.shard_map(
        on_device,
        mesh=mesh,
        in_specs=(
            P("rep", "fsdp", None),
            P("rep", "fsdp", None),
            P("fsdp", None),
            P(("rep", "fsdp"), None),
        ),
        out_specs=(P("rep", "fsdp", None), P("fsdp", None), P(("rep", "fsdp"), None)),
        check_vma=False,
    )
```

```python
import math

import jax
import jax.numpy as jnp
import numpy as np
from jax import lax
from jax.experimental import pallas as pl
from jax.experimental.pallas import tpu as pltpu
from jax.sharding import PartitionSpec as P

TILE = 64
BAND = 16
WIDE = 8
AXES = ("rep", "fsdp")

momentum_decay = 0.9
step_rate = 0.02
soft_width = 0.25

F32 = jnp.float32
BF16 = jnp.bfloat16
NT = (((1,), (1,)), ((), ()))


def cosine_rows():
    freq = np.arange(BAND, dtype=np.float64)[:, None]
    place = np.arange(TILE, dtype=np.float64)[None, :]
    factor = np.where(freq == 0.0, math.sqrt(1.0 / TILE), math.sqrt(2.0 / TILE))
    return factor * np.cos(math.pi * (2.0 * place + 1.0) * freq / (2.0 * TILE))


def halves(array):
    high = np.asarray(array, np.float32).astype(jnp.bfloat16)
    low = (np.asarray(array, np.float64) - high.astype(np.float64)).astype(jnp.bfloat16)
    return high, low


def split(value):
    high = value.astype(BF16)
    return high, (value - high.astype(F32)).astype(BF16)


def dot(a, b):
    return jnp.dot(a, b, preferred_element_type=F32)


def spot(index):
    rep, rest = divmod(index, 32)
    high, x = divmod(rep, 4)
    y, rest = divmod(rest, 8)
    low, core = divmod(rest, 2)
    return x, y, high * 4 + low, core


def place(x, y, z, core):
    x, y, z = x % 4, y % 4, z % 8
    return ((z // 4) * 4 + x) * 32 + y * 8 + (z % 4) * 2 + core


def fetch(value, source):
    return lax.ppermute(value, AXES, [(place(*source(*spot(i))), i) for i in range(256)])


def along(axis, step):
    def source(x, y, z, core):
        if (core + axis) % 2 == 0:
            return x, y + step, z, core
        if step == 2 and z % 2:
            return x, y, z - 2, core
        return x, y, z + step, core

    return source


def along_x(step):
    return lambda x, y, z, core: (x + step, y, z, core)


def far_z(x, y, z, core):
    return x, y, z + 4, core


def sibling(x, y, z, core):
    return x, y, z, 1 - core


def call(kernel, out_shape, inputs, scratch=(), limit=16, flops=0, smem=0, kept=()):
    specs = [pl.BlockSpec(memory_space=pltpu.SMEM)] * smem
    specs += [pl.BlockSpec(memory_space=pltpu.VMEM)] * (len(inputs) - smem)
    specs += [pl.BlockSpec(memory_space=pl.ANY)] * len(kept)
    inputs = (*inputs, *kept)
    moved = sum(math.prod(v.shape) * v.dtype.itemsize for v in inputs)
    return pl.pallas_call(
        kernel,
        out_shape=out_shape,
        in_specs=specs,
        out_specs=jax.tree.map(lambda _: pl.BlockSpec(memory_space=pltpu.VMEM), out_shape),
        scratch_shapes=list(scratch),
        compiler_params=pltpu.CompilerParams(vmem_limit_bytes=limit << 20),
        cost_estimate=pl.CostEstimate(flops=flops, bytes_accessed=moved, transcendentals=0),
    )(*inputs)


def stacked(value, wide):
    return jnp.concatenate(
        [value[:, k * wide : (k + 1) * wide] for k in range(value.shape[1] // wide)], axis=0
    )


def mixed_of(momentum, gradient):
    return momentum_decay * momentum[0] + gradient[0].astype(F32)


def bands_kernel(momentum, gradient, cols_hi, cols_lo, rows3, exact, rounded):
    high, low = split(mixed_of(momentum, gradient))
    high = stacked(high, WIDE * TILE)
    low = stacked(low, WIDE * TILE)
    narrow = dot(high, cols_hi[...]) + dot(low, cols_hi[...]) + dot(high, cols_lo[...])
    narrow = jnp.concatenate(
        [narrow[k * TILE : (k + 1) * TILE] for k in range(narrow.shape[0] // TILE)], axis=1
    )
    high, low = split(narrow)
    bands = dot(rows3[...], jnp.concatenate([high, low, high], axis=0))
    exact[...] = bands
    rounded[...] = bands.astype(BF16)


def restored(bands, back_rows3, back_hi, back_lo):
    high, low = split(bands)
    tall = dot(back_rows3[...], jnp.concatenate([high, low, high], axis=0))
    high, low = split(stacked(tall, WIDE * BAND))
    return dot(high, back_hi[...]) + dot(low, back_hi[...]) + dot(high, back_lo[...])


def residual_kernel(momentum, gradient, bands, back_rows3, back_hi, back_lo, out):
    mixed = mixed_of(momentum, gradient)
    low = restored(bands[...], back_rows3, back_hi, back_lo)
    wide = WIDE * TILE
    for k in range(mixed.shape[1] // wide):
        cut = slice(k * wide, (k + 1) * wide)
        out[0, :, cut] = mixed[:, cut] - low[k * TILE : (k + 1) * TILE]


def soft_sign(update):
    return update * lax.rsqrt(update * update + soft_width)


def direction_kernel(total, back_rows3, back_hi, back_lo, out):
    sign = soft_sign(restored(total[...], back_rows3, back_hi, back_lo))
    wide = WIDE * TILE
    for k in range(out.shape[1] // wide):
        out[:, k * wide : (k + 1) * wide] = sign[k * TILE : (k + 1) * TILE]


def forward_kernel(parts, first, back_rows, back_cols, *refs):
    groups = len(parts)
    refs = list(refs)
    bands = [refs.pop(0) for _ in range(groups)]
    tokens = [refs.pop(0) for _ in range(2)]
    weights = [[refs.pop(0) for _ in range(n)] for n in parts]
    outs = [refs.pop(0) for _ in range(2 * groups)]
    kept, raw, *fresh, token_sem, raw_sem = refs
    wide = WIDE * TILE
    rows, width = kept.shape[1:]
    start = first[0]

    pieces = []
    for g in range(groups):
        found = []
        for ref in weights[g]:
            found += [(ref, r) for r in range(0, ref.shape[0], TILE)]
        pieces.append(found)
    raw_copy = {}
    for g in range(groups):
        for f, (ref, r) in enumerate(pieces[g]):
            raw_copy[g, f] = pltpu.make_async_copy(ref.at[r : r + TILE], raw.at[g, f], raw_sem.at[g, f])
    per = tokens[0].shape[0] // rows
    token_copy = [
        pltpu.make_async_copy(tokens[t // per].at[pl.ds(t % per * rows, rows)], kept.at[t], token_sem.at[t])
        for t in range(4)
    ]
    for f in range(4):
        raw_copy[0, f].start()
    for copy in token_copy:
        copy.start()
    for g in range(1, groups):
        for f in range(4):
            raw_copy[g, f].start()

    def renew(g, f):
        raw_copy[g, f].wait()
        tall = dot(back_rows[...], bands[g][f * BAND : (f + 1) * BAND]).astype(BF16)
        sign = soft_sign(dot(stacked(tall, WIDE * BAND), back_cols[...]))
        at = pl.ds(pl.multiple_of(lax.rem(start + f, 4) * TILE, TILE), TILE)
        for k in range(width // wide):
            cut = slice(k * wide, (k + 1) * wide)
            new = raw[g, f, :, cut].astype(F32) - step_rate * sign[k * TILE : (k + 1) * TILE]
            fresh[g % 2][at, cut] = new.astype(BF16)

    for f in range(4):
        renew(0, f)
    for g in range(groups):
        for t in range(4):
            if g == 0:
                token_copy[t].wait()
            product = lax.dot_general(kept[t], fresh[g % 2][...], NT, preferred_element_type=F32)
            outs[2 * g + t // per][t % per * rows : (t % per + 1) * rows] = product.astype(BF16)
            if g + 1 < groups:
                renew(g + 1, t)


def weave_kernel(where, *refs):
    mine, theirs, out, held = refs[:4], refs[4:8], refs[8], refs[9]
    core, my_start, their_start = where[0], where[1], where[2]
    for g in range(4):
        held[1 - core, lax.rem(my_start + g, 4)] = mine[g][...]
        held[core, lax.rem(their_start + g, 4)] = theirs[g][...]
    for y in range(4):
        for z in range(4):
            left = held[0, y, :, z * TILE : (z + 1) * TILE]
            right = held[1, z, :, y * TILE : (y + 1) * TILE]
            j = (y * 4 + z) * 2 * TILE
            out[:, j : j + 2 * TILE] = jnp.concatenate([left, right], axis=1)


def on_device(momentum, gradient, weight, activations):
    cosines = cosine_rows()
    high, low = halves(cosines)
    eye = np.eye(WIDE)
    cols_hi, cols_lo = (np.kron(eye, np.asarray(h, np.float32).T).astype(jnp.bfloat16) for h in (high, low))
    rows3 = np.concatenate([high, high, low], axis=1)
    back_rows3 = np.concatenate([high.T, high.T, low.T], axis=1)
    back_hi, back_lo = cols_hi.T, cols_lo.T
    back_rows = high.T
    width = weight.shape[1]
    narrow = width // TILE * BAND
    rows = weight.shape[0]
    tokens = activations.shape[0]

    core = lax.axis_index("fsdp") % 2
    y = lax.axis_index("fsdp") // 8
    z = lax.axis_index("fsdp") // 2 % 4
    first = jnp.where(core == 0, y, z).astype(jnp.int32)
    second = jnp.where(core == 0, z, y).astype(jnp.int32)

    shape = jax.ShapeDtypeStruct
    exact, rounded = call(
        bands_kernel,
        (shape((BAND, narrow), F32), shape((BAND, narrow), BF16)),
        (momentum, gradient, cols_hi, cols_lo, rows3),
    )

    def after(value, *others):
        return lax.optimization_barrier((value, *others))[0]

    swapped = fetch(weight, sibling)
    swapped = after(swapped, rounded)
    ahead, behind, across = (fetch(swapped, along(0, s)) for s in (1, -1, 2))

    total = rounded.astype(F32) + fetch(rounded, along_x(1)).astype(F32)
    total = total + fetch(total.astype(BF16), along_x(2)).astype(F32)
    sent = total.astype(BF16)
    other = fetch(after(activations, sent), sibling)
    line = jnp.concatenate([swapped, ahead, across, behind], axis=0)
    line = after(line, sent)
    total = sent.astype(F32) + fetch(sent, far_z).astype(F32)

    new_momentum = call(
        residual_kernel,
        shape(momentum.shape, F32),
        (momentum, gradient, exact, back_rows3, back_hi, back_lo),
    )

    def gather(value):
        pair = jnp.concatenate([value, fetch(value, along(0, 1))], axis=0)
        return pair, fetch(pair, along(0, 2))

    band_line = jnp.concatenate(gather(total.astype(BF16)), axis=0)
    near, far = gather(fetch(band_line, sibling))
    blocks = jnp.concatenate([near, far], axis=0).reshape(4, 4, BAND, narrow)
    bands = [blocks[:, g].reshape(4 * BAND, narrow) for g in range(4)]

    next_line = fetch(line, along(1, 1))
    last_line = fetch(line, along(1, -1))
    half = line.shape[0] // 2
    far_a = fetch(next_line[:half], along(1, 1))
    far_b = fetch(last_line[half:], along(1, -1))
    lines = [[line], [next_line], [far_a, far_b], [last_line]]

    direction = call(
        direction_kernel,
        shape((rows, width), F32),
        (total, back_rows3, back_hi, back_lo),
    )

    def forward(order):
        parts = [len(lines[g]) for g in order]
        inputs = [first[None], back_rows, back_hi] + [bands[g] for g in order]
        kept = [activations, other] + [line for g in order for line in lines[g]]
        block = shape((tokens, 4 * rows), BF16)
        return call(
            lambda *refs: forward_kernel(parts, *refs),
            tuple([block] * (2 * len(order))),
            inputs,
            (
                pltpu.VMEM((4, tokens // 2, width), BF16),
                pltpu.VMEM((len(order), 4, rows, width), BF16),
                pltpu.VMEM((4 * rows, width), BF16),
                pltpu.VMEM((4 * rows, width), BF16),
                pltpu.SemaphoreType.DMA((4,)),
                pltpu.SemaphoreType.DMA((len(order), 4)),
            ),
            limit=48,
            flops=len(order) * 2 * 2 * tokens * 4 * rows * width,
            smem=1,
            kept=kept,
        )

    mine, theirs = [None] * 4, [None] * 4
    for order in ([0], [1, 3], [2]):
        result = forward(order)
        for n, g in enumerate(order):
            mine[g] = result[2 * n]
            theirs[g] = fetch(result[2 * n + 1], sibling)
    where = jnp.stack([core.astype(jnp.int32), second, first])
    projected = call(
        weave_kernel,
        shape((tokens, 32 * rows), BF16),
        (where, *mine, *theirs),
        (pltpu.VMEM((2, 4, tokens, 4 * rows), BF16),),
        smem=1,
    )
    return (new_momentum, direction, projected)


def solution(mesh):
    return jax.shard_map(
        on_device,
        mesh=mesh,
        in_specs=(
            P("rep", "fsdp", None),
            P("rep", "fsdp", None),
            P("fsdp", None),
            P(("rep", "fsdp"), None),
        ),
        out_specs=(P("rep", "fsdp", None), P("fsdp", None), P(("rep", "fsdp"), None)),
        check_vma=False,
    )
```

```python
import math

import jax
import jax.numpy as jnp
import numpy as np
from jax import lax
from jax.experimental import pallas as pl
from jax.experimental.pallas import tpu as pltpu
from jax.sharding import PartitionSpec as P

TILE = 64
BAND = 16
WIDE = 8
AXES = ("rep", "fsdp")

momentum_decay = 0.9
step_rate = 0.02
soft_width = 0.25

F32 = jnp.float32
BF16 = jnp.bfloat16
NT = (((1,), (1,)), ((), ()))


def cosine_rows():
    freq = np.arange(BAND, dtype=np.float64)[:, None]
    place = np.arange(TILE, dtype=np.float64)[None, :]
    factor = np.where(freq == 0.0, math.sqrt(1.0 / TILE), math.sqrt(2.0 / TILE))
    return factor * np.cos(math.pi * (2.0 * place + 1.0) * freq / (2.0 * TILE))


def halves(array):
    high = np.asarray(array, np.float32).astype(jnp.bfloat16)
    low = (np.asarray(array, np.float64) - high.astype(np.float64)).astype(jnp.bfloat16)
    return high, low


def split(value):
    high = value.astype(BF16)
    return high, (value - high.astype(F32)).astype(BF16)


def dot(a, b):
    return jnp.dot(a, b, preferred_element_type=F32)


def spot(index):
    rep, rest = divmod(index, 32)
    high, x = divmod(rep, 4)
    y, rest = divmod(rest, 8)
    low, core = divmod(rest, 2)
    return x, y, high * 4 + low, core


def place(x, y, z, core):
    x, y, z = x % 4, y % 4, z % 8
    return ((z // 4) * 4 + x) * 32 + y * 8 + (z % 4) * 2 + core


def fetch(value, source):
    return lax.ppermute(value, AXES, [(place(*source(*spot(i))), i) for i in range(256)])


def along(axis, step):
    def source(x, y, z, core):
        if (core + axis) % 2 == 0:
            return x, y + step, z, core
        if step == 2 and z % 2:
            return x, y, z - 2, core
        return x, y, z + step, core

    return source


def along_x(step):
    return lambda x, y, z, core: (x + step, y, z, core)


def pair_x(x, y, z, core):
    return x ^ 1, y, z, core


def far_z(x, y, z, core):
    return x, y, z + 4, core


def sibling(x, y, z, core):
    return x, y, z, 1 - core


def call(kernel, out_shape, inputs, scratch=(), limit=16, flops=0, smem=0, kept=(), resident=()):
    specs = [pl.BlockSpec(memory_space=pltpu.SMEM)] * smem
    specs += [pl.BlockSpec(memory_space=pltpu.VMEM)] * (len(inputs) - smem + len(resident))
    specs += [pl.BlockSpec(memory_space=pltpu.HBM)] * len(kept)
    resident = [pltpu.with_memory_space_constraint(v, pltpu.VMEM) for v in resident]
    kept = [pltpu.with_memory_space_constraint(v, pltpu.HBM) for v in kept]
    inputs = (*inputs, *resident, *kept)
    moved = sum(math.prod(v.shape) * v.dtype.itemsize for v in inputs)
    return pl.pallas_call(
        kernel,
        out_shape=out_shape,
        in_specs=specs,
        out_specs=jax.tree.map(
            lambda _: pl.BlockSpec(memory_space=pltpu.VMEM),
            out_shape,
            is_leaf=lambda v: not isinstance(v, tuple),
        ),
        scratch_shapes=list(scratch),
        compiler_params=pltpu.CompilerParams(vmem_limit_bytes=limit << 20),
        cost_estimate=pl.CostEstimate(flops=flops, bytes_accessed=moved, transcendentals=0),
    )(*inputs)


def stay_kernel(source, out, sem):
    copy = pltpu.make_async_copy(source, out, sem)
    copy.start()
    copy.wait()


def stay(value):
    return call(
        stay_kernel,
        pltpu.VMEM(value.shape, value.dtype),
        (),
        (pltpu.SemaphoreType.DMA,),
        kept=(value,),
    )


def stacked(value, wide):
    return jnp.concatenate(
        [value[:, k * wide : (k + 1) * wide] for k in range(value.shape[1] // wide)], axis=0
    )


def mixed_of(momentum, gradient):
    return momentum_decay * momentum[0] + gradient[0].astype(F32)


def bands_kernel(momentum, gradient, cols, rows3, exact, rounded, m, g, c, r, sems):
    wide = WIDE * TILE
    steps = momentum.shape[2] // wide
    copies = [pltpu.make_async_copy(cols, c, sems.at[2 * steps])]
    copies += [pltpu.make_async_copy(rows3, r, sems.at[2 * steps + 1])]
    for k in range(steps):
        cut = pl.ds(k * wide, wide)
        copies += [
            pltpu.make_async_copy(momentum.at[0, :, cut], m.at[k], sems.at[2 * k]),
            pltpu.make_async_copy(gradient.at[0, :, cut], g.at[k], sems.at[2 * k + 1]),
        ]
    for copy in copies:
        copy.start()
    copies[0].wait()
    narrow = []
    for k in range(steps):
        copies[2 * k + 2].wait()
        copies[2 * k + 3].wait()
        high, low = split(momentum_decay * m[k] + g[k].astype(F32))
        narrow.append(dot(high, c[:wide]) + dot(low, c[:wide]) + dot(high, c[wide:]))
    copies[1].wait()
    high, low = split(jnp.concatenate(narrow, axis=1))
    bands = dot(r[...], jnp.concatenate([high, low, high], axis=0))
    exact[...] = bands
    rounded[...] = bands.astype(BF16)


def restored(bands, back_rows3, back_hi, back_lo):
    high, low = split(bands)
    tall = dot(back_rows3[...], jnp.concatenate([high, low, high], axis=0))
    high, low = split(stacked(tall, WIDE * BAND))
    return dot(high, back_hi[...]) + dot(low, back_hi[...]) + dot(high, back_lo[...])


def residual_kernel(momentum, gradient, bands, back_rows3, back_hi, back_lo, out):
    mixed = mixed_of(momentum, gradient)
    low = restored(bands[...], back_rows3, back_hi, back_lo)
    wide = WIDE * TILE
    for k in range(mixed.shape[1] // wide):
        cut = slice(k * wide, (k + 1) * wide)
        out[0, :, cut] = mixed[:, cut] - low[k * TILE : (k + 1) * TILE]


def soft_sign(update):
    return update * lax.rsqrt(update * update + soft_width)


def direction_kernel(total, back_rows3, back_hi, back_lo, out):
    sign = soft_sign(restored(total[...], back_rows3, back_hi, back_lo))
    wide = WIDE * TILE
    for k in range(out.shape[1] // wide):
        out[:, k * wide : (k + 1) * wide] = sign[k * TILE : (k + 1) * TILE]


def forward_kernel(parts, first, back_rows, back_cols, *refs):
    groups = len(parts)
    refs = list(refs)
    bands = [refs.pop(0) for _ in range(groups)]
    tokens = [refs.pop(0) for _ in range(2)]
    weights = [[refs.pop(0) for _ in range(n)] for n in parts]
    outs = [refs.pop(0) for _ in range(2 * groups)]
    raw, *fresh, raw_sem = refs
    wide = WIDE * TILE
    rows, width = fresh[0].shape
    per = tokens[0].shape[0] // rows
    start = first[0]

    pieces = []
    for g in range(groups):
        found = []
        for ref in weights[g]:
            found += [(ref, r) for r in range(0, ref.shape[0], TILE)]
        pieces.append(found)
    raw_copy = {}
    for g in range(groups):
        for f, (ref, r) in enumerate(pieces[g]):
            raw_copy[g, f] = pltpu.make_async_copy(ref.at[r : r + TILE], raw.at[g, f], raw_sem.at[g, f])
    for g in range(groups):
        for f in range(4):
            raw_copy[g, f].start()

    def renew(g, f):
        tall = dot(back_rows[...], bands[g][f * BAND : (f + 1) * BAND]).astype(BF16)
        sign = soft_sign(dot(stacked(tall, WIDE * BAND), back_cols[...]))
        at = pl.ds(pl.multiple_of(lax.rem(start + f, 4) * TILE, TILE), TILE)
        for k in range(width // wide):
            cut = slice(k * wide, (k + 1) * wide)
            new = raw[g, f, :, cut].astype(F32) - step_rate * sign[k * TILE : (k + 1) * TILE]
            fresh[g % 2][at, cut] = new.astype(BF16)

    for f in range(4):
        raw_copy[0, f].wait()
        renew(0, f)
    for g in range(groups):
        if g + 1 < groups:
            for f in range(4):
                raw_copy[g + 1, f].wait()
        for t in range(4):
            cut = slice(t % per * rows, (t % per + 1) * rows)
            product = lax.dot_general(tokens[t // per][cut], fresh[g % 2][...], NT, preferred_element_type=F32)
            outs[2 * g + t // per][cut] = product.astype(BF16)
            if g + 1 < groups:
                renew(g + 1, t)


def weave_kernel(where, *refs):
    mine, theirs, out, held = refs[:4], refs[4:8], refs[8], refs[9]
    core, my_start, their_start = where[0], where[1], where[2]
    for g in range(4):
        held[1 - core, lax.rem(my_start + g, 4)] = mine[g][...]
        held[core, lax.rem(their_start + g, 4)] = theirs[g][...]
    for y in range(4):
        for z in range(4):
            left = held[0, y, :, z * TILE : (z + 1) * TILE]
            right = held[1, z, :, y * TILE : (y + 1) * TILE]
            j = (y * 4 + z) * 2 * TILE
            out[:, j : j + 2 * TILE] = jnp.concatenate([left, right], axis=1)


def on_device(momentum, gradient, weight, activations):
    cosines = cosine_rows()
    high, low = halves(cosines)
    eye = np.eye(WIDE)
    cols_hi, cols_lo = (np.kron(eye, np.asarray(h, np.float32).T).astype(jnp.bfloat16) for h in (high, low))
    rows3 = np.concatenate([high, high, low], axis=1)
    back_rows3 = np.concatenate([high.T, high.T, low.T], axis=1)
    back_hi, back_lo = cols_hi.T, cols_lo.T
    back_rows = high.T
    width = weight.shape[1]
    narrow = width // TILE * BAND
    rows = weight.shape[0]
    tokens = activations.shape[0]

    core = lax.axis_index("fsdp") % 2
    y = lax.axis_index("fsdp") // 8
    z = lax.axis_index("fsdp") // 2 % 4
    first = jnp.where(core == 0, y, z).astype(jnp.int32)
    second = jnp.where(core == 0, z, y).astype(jnp.int32)

    shape = jax.ShapeDtypeStruct
    steps = width // (WIDE * TILE)
    exact, rounded = call(
        bands_kernel,
        (shape((BAND, narrow), F32), shape((BAND, narrow), BF16)),
        (),
        (
            pltpu.VMEM((steps, rows, WIDE * TILE), F32),
            pltpu.VMEM((steps, rows, WIDE * TILE), BF16),
            pltpu.VMEM((2 * WIDE * TILE, WIDE * BAND), BF16),
            pltpu.VMEM(rows3.shape, BF16),
            pltpu.SemaphoreType.DMA((2 * steps + 2,)),
        ),
        kept=(momentum, gradient, np.concatenate([cols_hi, cols_lo], axis=0), rows3),
    )

    def after(value, *others):
        return lax.optimization_barrier((value, *others))[0]

    swapped = fetch(weight, sibling)
    other = fetch(after(activations, swapped), sibling)
    swapped = after(swapped, rounded)
    ahead, behind, across = (fetch(swapped, along(0, s)) for s in (1, -1, 2))

    def join(value, source):
        return value.astype(F32) + fetch(value, source).astype(F32)

    sent = join(rounded, far_z).astype(BF16)
    total = join(join(sent, pair_x).astype(BF16), along_x(2))
    own = stay(after(activations, sent))
    other = stay(other)

    new_momentum = call(
        residual_kernel,
        shape(momentum.shape, F32),
        (momentum, gradient, exact, back_rows3, back_hi, back_lo),
    )

    def gather(value):
        pair = jnp.concatenate([value, fetch(value, along(0, 1))], axis=0)
        return pair, fetch(pair, along(0, 2))

    band_line = jnp.concatenate(gather(total.astype(BF16)), axis=0)
    near, far = gather(fetch(band_line, sibling))
    blocks = jnp.concatenate([near, far], axis=0).reshape(4, 4, BAND, narrow)
    bands = [blocks[:, g].reshape(4 * BAND, narrow) for g in range(4)]

    early = after(jnp.concatenate([swapped, ahead], axis=0), sent)
    late = after(jnp.concatenate([across, behind], axis=0), new_momentum)
    next_early, last_early = fetch(early, along(1, 1)), fetch(early, along(1, -1))
    next_late, last_late = fetch(late, along(1, 1)), fetch(late, along(1, -1))
    far_early, far_late = fetch(next_early, along(1, 1)), fetch(last_late, along(1, -1))
    lines = [[early, late], [next_early, next_late], [far_early, far_late], [last_early, last_late]]

    direction = call(
        direction_kernel,
        shape((rows, width), F32),
        (total, back_rows3, back_hi, back_lo),
    )

    def forward(order):
        parts = [len(lines[g]) for g in order]
        inputs = [first[None], back_rows, back_hi] + [bands[g] for g in order]
        kept = [line for g in order for line in lines[g]]
        block = shape((tokens, 4 * rows), BF16)
        return call(
            lambda *refs: forward_kernel(parts, *refs),
            tuple([block] * (2 * len(order))),
            inputs,
            (
                pltpu.VMEM((len(order), 4, rows, width), BF16),
                pltpu.VMEM((4 * rows, width), BF16),
                pltpu.VMEM((4 * rows, width), BF16),
                pltpu.SemaphoreType.DMA((len(order), 4)),
            ),
            limit=24,
            flops=len(order) * 2 * 2 * tokens * 4 * rows * width,
            smem=1,
            kept=kept,
            resident=(own, other),
        )

    mine, theirs = [None] * 4, [None] * 4
    for order in ([0], [1, 3], [2]):
        result = forward(order)
        for n, g in enumerate(order):
            mine[g] = result[2 * n]
            theirs[g] = fetch(result[2 * n + 1], sibling)
    where = jnp.stack([core.astype(jnp.int32), second, first])
    projected = call(
        weave_kernel,
        shape((tokens, 32 * rows), BF16),
        (where, *mine, *theirs),
        (pltpu.VMEM((2, 4, tokens, 4 * rows), BF16),),
        smem=1,
    )
    return (new_momentum, direction, projected)


def solution(mesh):
    return jax.shard_map(
        on_device,
        mesh=mesh,
        in_specs=(
            P("rep", "fsdp", None),
            P("rep", "fsdp", None),
            P("fsdp", None),
            P(("rep", "fsdp"), None),
        ),
        out_specs=(P("rep", "fsdp", None), P("fsdp", None), P(("rep", "fsdp"), None)),
        check_vma=False,
    )
```

```python
import math

import jax
import jax.numpy as jnp
import numpy as np
from jax import lax
from jax.experimental import pallas as pl
from jax.experimental.pallas import tpu as pltpu
from jax.sharding import PartitionSpec as P

TILE = 64
BAND = 16
WIDE = 8
AXES = ("rep", "fsdp")

momentum_decay = 0.9
step_rate = 0.02
soft_width = 0.25

F32 = jnp.float32
BF16 = jnp.bfloat16
NT = (((1,), (1,)), ((), ()))


def cosine_rows():
    freq = np.arange(BAND, dtype=np.float64)[:, None]
    place = np.arange(TILE, dtype=np.float64)[None, :]
    factor = np.where(freq == 0.0, math.sqrt(1.0 / TILE), math.sqrt(2.0 / TILE))
    return factor * np.cos(math.pi * (2.0 * place + 1.0) * freq / (2.0 * TILE))


def halves(array):
    high = np.asarray(array, np.float32).astype(jnp.bfloat16)
    low = (np.asarray(array, np.float64) - high.astype(np.float64)).astype(jnp.bfloat16)
    return high, low


def split(value):
    high = value.astype(BF16)
    return high, (value - high.astype(F32)).astype(BF16)


def dot(a, b):
    return jnp.dot(a, b, preferred_element_type=F32)


def spot(index):
    rep, rest = divmod(index, 32)
    high, x = divmod(rep, 4)
    y, rest = divmod(rest, 8)
    low, core = divmod(rest, 2)
    return x, y, high * 4 + low, core


def place(x, y, z, core):
    x, y, z = x % 4, y % 4, z % 8
    return ((z // 4) * 4 + x) * 32 + y * 8 + (z % 4) * 2 + core


def fetch(value, source):
    return lax.ppermute(value, AXES, [(place(*source(*spot(i))), i) for i in range(256)])


def along(axis, step):
    def source(x, y, z, core):
        if (core + axis) % 2 == 0:
            return x, y + step, z, core
        if step == 2 and z % 2:
            return x, y, z - 2, core
        return x, y, z + step, core

    return source


def along_x(step):
    return lambda x, y, z, core: (x + step, y, z, core)


def pair_x(x, y, z, core):
    return x ^ 1, y, z, core


def far_z(x, y, z, core):
    return x, y, z + 4, core


def sibling(x, y, z, core):
    return x, y, z, 1 - core


def call(kernel, out_shape, inputs, scratch=(), limit=16, flops=0, smem=0, kept=(), resident=()):
    specs = [pl.BlockSpec(memory_space=pltpu.SMEM)] * smem
    specs += [pl.BlockSpec(memory_space=pltpu.VMEM)] * (len(inputs) - smem + len(resident))
    specs += [pl.BlockSpec(memory_space=pltpu.HBM)] * len(kept)
    resident = [pltpu.with_memory_space_constraint(v, pltpu.VMEM) for v in resident]
    kept = [pltpu.with_memory_space_constraint(v, pltpu.HBM) for v in kept]
    inputs = (*inputs, *resident, *kept)
    moved = sum(math.prod(v.shape) * v.dtype.itemsize for v in inputs)
    return pl.pallas_call(
        kernel,
        out_shape=out_shape,
        in_specs=specs,
        out_specs=jax.tree.map(
            lambda _: pl.BlockSpec(memory_space=pltpu.VMEM),
            out_shape,
            is_leaf=lambda v: not isinstance(v, tuple),
        ),
        scratch_shapes=list(scratch),
        compiler_params=pltpu.CompilerParams(vmem_limit_bytes=limit << 20),
        cost_estimate=pl.CostEstimate(flops=flops, bytes_accessed=moved, transcendentals=0),
    )(*inputs)


def stay_kernel(source, out, sem):
    copy = pltpu.make_async_copy(source, out, sem)
    copy.start()
    copy.wait()


def stay(value):
    return call(
        stay_kernel,
        pltpu.VMEM(value.shape, value.dtype),
        (),
        (pltpu.SemaphoreType.DMA,),
        kept=(value,),
    )


def stacked(value, wide):
    return jnp.concatenate(
        [value[:, k * wide : (k + 1) * wide] for k in range(value.shape[1] // wide)], axis=0
    )


def mixed_of(momentum, gradient):
    return momentum_decay * momentum[0] + gradient[0].astype(F32)


def bands_kernel(momentum, gradient, cols, rows3, exact, rounded, m, g, c, r, sems):
    wide = WIDE * TILE
    steps = momentum.shape[2] // wide
    copies = [pltpu.make_async_copy(cols, c, sems.at[2 * steps])]
    copies += [pltpu.make_async_copy(rows3, r, sems.at[2 * steps + 1])]
    for k in range(steps):
        cut = pl.ds(k * wide, wide)
        copies += [
            pltpu.make_async_copy(momentum.at[0, :, cut], m.at[k], sems.at[2 * k]),
            pltpu.make_async_copy(gradient.at[0, :, cut], g.at[k], sems.at[2 * k + 1]),
        ]
    for copy in copies:
        copy.start()
    copies[0].wait()
    narrow = []
    for k in range(steps):
        copies[2 * k + 2].wait()
        copies[2 * k + 3].wait()
        high, low = split(momentum_decay * m[k] + g[k].astype(F32))
        narrow.append(dot(high, c[:wide]) + dot(low, c[:wide]) + dot(high, c[wide:]))
    copies[1].wait()
    high, low = split(jnp.concatenate(narrow, axis=1))
    bands = dot(r[...], jnp.concatenate([high, low, high], axis=0))
    exact[...] = bands
    rounded[...] = bands.astype(BF16)


def restored(bands, back_rows3, back_hi, back_lo):
    high, low = split(bands)
    tall = dot(back_rows3[...], jnp.concatenate([high, low, high], axis=0))
    high, low = split(stacked(tall, WIDE * BAND))
    return dot(high, back_hi[...]) + dot(low, back_hi[...]) + dot(high, back_lo[...])


def residual_kernel(momentum, gradient, bands, back_rows3, back_hi, back_lo, out):
    mixed = mixed_of(momentum, gradient)
    low = restored(bands[...], back_rows3, back_hi, back_lo)
    wide = WIDE * TILE
    for k in range(mixed.shape[1] // wide):
        cut = slice(k * wide, (k + 1) * wide)
        out[0, :, cut] = mixed[:, cut] - low[k * TILE : (k + 1) * TILE]


def soft_sign(update):
    return update * lax.rsqrt(update * update + soft_width)


def direction_kernel(total, back_rows3, back_hi, back_lo, out):
    sign = soft_sign(restored(total[...], back_rows3, back_hi, back_lo))
    wide = WIDE * TILE
    for k in range(out.shape[1] // wide):
        out[:, k * wide : (k + 1) * wide] = sign[k * TILE : (k + 1) * TILE]


def row_copies(weights, raw, sems):
    copies = []
    for g, refs in enumerate(weights):
        pieces = [(ref, r) for ref in refs for r in range(0, ref.shape[0], TILE)]
        copies.append(
            [
                pltpu.make_async_copy(ref.at[r : r + TILE], raw.at[g, f], sems.at[g, f])
                for f, (ref, r) in enumerate(pieces)
            ]
        )
        for copy in copies[g]:
            copy.start()
    return copies


def rows_at(start, f):
    return pl.ds(pl.multiple_of(lax.rem(start + f, 4) * TILE, TILE), TILE)


def products(tokens, fresh, outs, t):
    rows = fresh.shape[0]
    per = tokens[0].shape[0] // rows
    cut = slice(t % per * rows, (t % per + 1) * rows)
    product = lax.dot_general(tokens[t // per][cut], fresh[...], NT, preferred_element_type=F32)
    outs[t // per][cut] = product.astype(BF16)


def forward_kernel(parts, first, back_rows, back_cols, *refs):
    groups = len(parts)
    refs = list(refs)
    bands = [refs.pop(0) for _ in range(groups + 1)]
    tokens = [refs.pop(0) for _ in range(2)]
    weights = [[refs.pop(0) for _ in range(n)] for n in parts]
    outs = [refs.pop(0) for _ in range(2 * groups)]
    step, raw, *fresh, sems = refs
    wide = WIDE * TILE
    width = step.shape[1]
    start = first[0]
    copies = row_copies(weights, raw, sems)

    def renew(g, f):
        tall = dot(back_rows[...], bands[g][f * BAND : (f + 1) * BAND]).astype(BF16)
        sign = step_rate * soft_sign(dot(stacked(tall, WIDE * BAND), back_cols[...]))
        at = rows_at(start, f)
        for k in range(width // wide):
            cut = slice(k * wide, (k + 1) * wide)
            part = sign[k * TILE : (k + 1) * TILE]
            if g == groups:
                step[at, cut] = part.astype(BF16)
            else:
                fresh[g % 2][at, cut] = (raw[g, f, :, cut].astype(F32) - part).astype(BF16)

    for f in range(4):
        copies[0][f].wait()
        renew(0, f)
    for g in range(groups):
        if g + 1 < groups:
            for f in range(4):
                copies[g + 1][f].wait()
        for t in range(4):
            products(tokens, fresh[g % 2], outs[2 * g : 2 * g + 2], t)
            renew(g + 1, t)


def last_kernel(parts, first, own, other, step, *refs):
    refs = list(refs)
    weights = [refs.pop(0) for _ in range(parts)]
    out_own, out_other, raw, fresh, sems = refs
    copies = row_copies([weights], raw, sems)[0]
    for f in range(4):
        copies[f].wait()
        at = rows_at(first[0], f)
        fresh[at] = (raw[0, f].astype(F32) - step[at].astype(F32)).astype(BF16)
    for t in range(4):
        products((own, other), fresh, (out_own, out_other), t)


def weave_kernel(where, *refs):
    mine, theirs, out, held = refs[:4], refs[4:8], refs[8], refs[9]
    core, my_start, their_start = where[0], where[1], where[2]
    for g in range(4):
        held[1 - core, lax.rem(my_start + g, 4)] = mine[g][...]
        held[core, lax.rem(their_start + g, 4)] = theirs[g][...]
    for y in range(4):
        for z in range(4):
            left = held[0, y, :, z * TILE : (z + 1) * TILE]
            right = held[1, z, :, y * TILE : (y + 1) * TILE]
            j = (y * 4 + z) * 2 * TILE
            out[:, j : j + 2 * TILE] = jnp.concatenate([left, right], axis=1)


def on_device(momentum, gradient, weight, activations):
    cosines = cosine_rows()
    high, low = halves(cosines)
    eye = np.eye(WIDE)
    cols_hi, cols_lo = (np.kron(eye, np.asarray(h, np.float32).T).astype(jnp.bfloat16) for h in (high, low))
    rows3 = np.concatenate([high, high, low], axis=1)
    back_rows3 = np.concatenate([high.T, high.T, low.T], axis=1)
    back_hi, back_lo = cols_hi.T, cols_lo.T
    back_rows = high.T
    width = weight.shape[1]
    narrow = width // TILE * BAND
    rows = weight.shape[0]
    tokens = activations.shape[0]

    core = lax.axis_index("fsdp") % 2
    y = lax.axis_index("fsdp") // 8
    z = lax.axis_index("fsdp") // 2 % 4
    first = jnp.where(core == 0, y, z).astype(jnp.int32)
    second = jnp.where(core == 0, z, y).astype(jnp.int32)

    shape = jax.ShapeDtypeStruct
    steps = width // (WIDE * TILE)
    exact, rounded = call(
        bands_kernel,
        (shape((BAND, narrow), F32), shape((BAND, narrow), BF16)),
        (),
        (
            pltpu.VMEM((steps, rows, WIDE * TILE), F32),
            pltpu.VMEM((steps, rows, WIDE * TILE), BF16),
            pltpu.VMEM((2 * WIDE * TILE, WIDE * BAND), BF16),
            pltpu.VMEM(rows3.shape, BF16),
            pltpu.SemaphoreType.DMA((2 * steps + 2,)),
        ),
        kept=(momentum, gradient, np.concatenate([cols_hi, cols_lo], axis=0), rows3),
    )

    def after(value, *others):
        return lax.optimization_barrier((value, *others))[0]

    swapped = fetch(weight, sibling)
    swapped = after(swapped, rounded)
    ahead, behind, across = (fetch(swapped, along(0, s)) for s in (1, -1, 2))

    def join(value, source):
        return value.astype(F32) + fetch(value, source).astype(F32)

    sent = join(after(rounded, swapped), far_z).astype(BF16)
    other = fetch(after(activations, sent), sibling)
    second_sum = join(after(sent, ahead, behind), pair_x).astype(BF16)
    total = join(after(second_sum, across), along_x(2))
    own, other = stay(after(activations, sent)), stay(other)

    new_momentum = call(
        residual_kernel,
        shape(momentum.shape, F32),
        (momentum, gradient, exact, back_rows3, back_hi, back_lo),
    )
    direction = call(
        direction_kernel,
        shape((rows, width), F32),
        (total, back_rows3, back_hi, back_lo),
    )

    early = after(jnp.concatenate([swapped, ahead], axis=0), sent)
    late = jnp.concatenate([across, behind], axis=0)
    next_early, last_early = fetch(early, along(1, 1)), fetch(early, along(1, -1))
    next_late, last_late = fetch(late, along(1, 1)), fetch(late, along(1, -1))
    far_early, far_late = fetch(next_early, along(1, 1)), fetch(last_late, along(1, -1))
    lines = [[early, late], [next_early, next_late], [far_early, far_late], [last_early, last_late]]

    def gather(value, *others):
        pair = jnp.concatenate([value, fetch(value, along(0, 1))], axis=0)
        return jnp.concatenate([pair, fetch(after(pair, *others), along(0, 2))], axis=0)

    band_line = gather(after(total.astype(BF16), late, new_momentum, own, other))
    band_line = fetch(after(band_line, next_early, last_early, direction), sibling)
    blocks = gather(band_line, next_late, last_late).reshape(4, 4, BAND, narrow)
    bands = [blocks[:, g].reshape(4 * BAND, narrow) for g in range(4)]

    block = shape((tokens, 4 * rows), BF16)
    step = pltpu.VMEM((4 * rows, width), BF16)
    order = [0, 3, 1]
    parts = [len(lines[g]) for g in order]
    *results, step = call(
        lambda *refs: forward_kernel(parts, *refs),
        (*[block] * 6, step),
        [first[None], back_rows, back_hi] + [bands[g] for g in order + [2]],
        (
            pltpu.VMEM((3, 4, rows, width), BF16),
            pltpu.VMEM((4 * rows, width), BF16),
            pltpu.VMEM((4 * rows, width), BF16),
            pltpu.SemaphoreType.DMA((3, 4)),
        ),
        limit=24,
        flops=3 * 2 * 2 * tokens * 4 * rows * width,
        smem=1,
        kept=[line for g in order for line in lines[g]],
        resident=(own, other),
    )
    results += call(
        lambda *refs: last_kernel(len(lines[2]), *refs),
        (block, block),
        [first[None]],
        (
            pltpu.VMEM((1, 4, rows, width), BF16),
            pltpu.VMEM((4 * rows, width), BF16),
            pltpu.SemaphoreType.DMA((1, 4)),
        ),
        limit=24,
        flops=2 * 2 * tokens * 4 * rows * width,
        smem=1,
        kept=lines[2],
        resident=(own, other, step),
    )
    mine, theirs = [None] * 4, [None] * 4
    for n, g in enumerate(order + [2]):
        mine[g] = results[2 * n]
        theirs[g] = fetch(results[2 * n + 1], sibling)
    where = jnp.stack([core.astype(jnp.int32), second, first])
    projected = call(
        weave_kernel,
        shape((tokens, 32 * rows), BF16),
        (where, *mine, *theirs),
        (pltpu.VMEM((2, 4, tokens, 4 * rows), BF16),),
        smem=1,
    )
    return (new_momentum, direction, projected)


def solution(mesh):
    return jax.shard_map(
        on_device,
        mesh=mesh,
        in_specs=(
            P("rep", "fsdp", None),
            P("rep", "fsdp", None),
            P("fsdp", None),
            P(("rep", "fsdp"), None),
        ),
        out_specs=(P("rep", "fsdp", None), P("fsdp", None), P(("rep", "fsdp"), None)),
        check_vma=False,
    )
```

```python
import math

import jax
import jax.numpy as jnp
import numpy as np
from jax import lax
from jax.experimental import pallas as pl
from jax.experimental.pallas import tpu as pltpu
from jax.sharding import PartitionSpec as P

TILE = 64
BAND = 16
WIDE = 8
AXES = ("rep", "fsdp")

momentum_decay = 0.9
step_rate = 0.02
soft_width = 0.25

F32 = jnp.float32
BF16 = jnp.bfloat16
NT = (((1,), (1,)), ((), ()))


def cosine_rows():
    freq = np.arange(BAND, dtype=np.float64)[:, None]
    place = np.arange(TILE, dtype=np.float64)[None, :]
    factor = np.where(freq == 0.0, math.sqrt(1.0 / TILE), math.sqrt(2.0 / TILE))
    return factor * np.cos(math.pi * (2.0 * place + 1.0) * freq / (2.0 * TILE))


def halves(array):
    high = np.asarray(array, np.float32).astype(jnp.bfloat16)
    low = (np.asarray(array, np.float64) - high.astype(np.float64)).astype(jnp.bfloat16)
    return high, low


def split(value):
    high = value.astype(BF16)
    return high, (value - high.astype(F32)).astype(BF16)


def dot(a, b):
    return jnp.dot(a, b, preferred_element_type=F32)


def spot(index):
    rep, rest = divmod(index, 32)
    high, x = divmod(rep, 4)
    y, rest = divmod(rest, 8)
    low, core = divmod(rest, 2)
    return x, y, high * 4 + low, core


def place(x, y, z, core):
    x, y, z = x % 4, y % 4, z % 8
    return ((z // 4) * 4 + x) * 32 + y * 8 + (z % 4) * 2 + core


def fetch(value, source):
    return lax.ppermute(value, AXES, [(place(*source(*spot(i))), i) for i in range(256)])


def along(axis, step):
    def source(x, y, z, core):
        if (core + axis) % 2 == 0:
            return x, y + step, z, core
        if step == 2 and z % 2:
            return x, y, z - 2, core
        return x, y, z + step, core

    return source


def along_x(step):
    return lambda x, y, z, core: (x + step, y, z, core)


def pair_x(x, y, z, core):
    return x ^ 1, y, z, core


def far_z(x, y, z, core):
    return x, y, z + 4, core


def sibling(x, y, z, core):
    return x, y, z, 1 - core


def call(kernel, out_shape, inputs, scratch=(), limit=16, flops=0, smem=0, kept=(), resident=()):
    specs = [pl.BlockSpec(memory_space=pltpu.SMEM)] * smem
    specs += [pl.BlockSpec(memory_space=pltpu.VMEM)] * (len(inputs) - smem + len(resident))
    specs += [pl.BlockSpec(memory_space=pltpu.HBM)] * len(kept)
    resident = [pltpu.with_memory_space_constraint(v, pltpu.VMEM) for v in resident]
    kept = [pltpu.with_memory_space_constraint(v, pltpu.HBM) for v in kept]
    inputs = (*inputs, *resident, *kept)
    moved = sum(math.prod(v.shape) * v.dtype.itemsize for v in inputs)
    return pl.pallas_call(
        kernel,
        out_shape=out_shape,
        in_specs=specs,
        out_specs=jax.tree.map(
            lambda _: pl.BlockSpec(memory_space=pltpu.VMEM),
            out_shape,
            is_leaf=lambda v: not isinstance(v, tuple),
        ),
        scratch_shapes=list(scratch),
        compiler_params=pltpu.CompilerParams(vmem_limit_bytes=limit << 20),
        cost_estimate=pl.CostEstimate(flops=flops, bytes_accessed=moved, transcendentals=0),
    )(*inputs)


def stacked(value, wide):
    return jnp.concatenate(
        [value[:, k * wide : (k + 1) * wide] for k in range(value.shape[1] // wide)], axis=0
    )


def mixed_of(momentum, gradient):
    return momentum_decay * momentum[0] + gradient[0].astype(F32)


def bands_kernel(momentum, gradient, cols, rows3, exact, rounded, m, g, c, r, sems):
    wide = WIDE * TILE
    steps = momentum.shape[2] // wide
    copies = [pltpu.make_async_copy(cols, c, sems.at[2 * steps])]
    copies += [pltpu.make_async_copy(rows3, r, sems.at[2 * steps + 1])]
    for k in range(steps):
        cut = pl.ds(k * wide, wide)
        copies += [
            pltpu.make_async_copy(momentum.at[0, :, cut], m.at[k], sems.at[2 * k]),
            pltpu.make_async_copy(gradient.at[0, :, cut], g.at[k], sems.at[2 * k + 1]),
        ]
    for copy in copies:
        copy.start()
    copies[0].wait()
    narrow = []
    for k in range(steps):
        copies[2 * k + 2].wait()
        copies[2 * k + 3].wait()
        high, low = split(momentum_decay * m[k] + g[k].astype(F32))
        narrow.append(dot(high, c[:wide]) + dot(low, c[:wide]) + dot(high, c[wide:]))
    copies[1].wait()
    high, low = split(jnp.concatenate(narrow, axis=1))
    bands = dot(r[...], jnp.concatenate([high, low, high], axis=0))
    exact[...] = bands
    rounded[...] = bands.astype(BF16)


def restored(bands, back_rows3, back_hi, back_lo):
    high, low = split(bands)
    tall = dot(back_rows3[...], jnp.concatenate([high, low, high], axis=0))
    high, low = split(stacked(tall, WIDE * BAND))
    return dot(high, back_hi[...]) + dot(low, back_hi[...]) + dot(high, back_lo[...])


def residual_kernel(momentum, gradient, bands, back_rows3, back_hi, back_lo, out):
    mixed = mixed_of(momentum, gradient)
    low = restored(bands[...], back_rows3, back_hi, back_lo)
    wide = WIDE * TILE
    for k in range(mixed.shape[1] // wide):
        cut = slice(k * wide, (k + 1) * wide)
        out[0, :, cut] = mixed[:, cut] - low[k * TILE : (k + 1) * TILE]


def soft_sign(update):
    return update * lax.rsqrt(update * update + soft_width)


def direction_kernel(total, back_rows3, back_hi, back_lo, out):
    sign = soft_sign(restored(total[...], back_rows3, back_hi, back_lo))
    wide = WIDE * TILE
    for k in range(out.shape[1] // wide):
        out[:, k * wide : (k + 1) * wide] = sign[k * TILE : (k + 1) * TILE]


def row_copies(weights, raw, sems, base):
    copies = []
    for g, refs in enumerate(weights):
        pieces = [(ref, r) for ref in refs for r in range(0, ref.shape[0], TILE)]
        copies.append(
            [
                pltpu.make_async_copy(ref.at[r : r + TILE], raw.at[base + g, f], sems.at[base + g, f])
                for f, (ref, r) in enumerate(pieces)
            ]
        )
        for copy in copies[g]:
            copy.start()
    return copies


def rows_at(start, f):
    return pl.ds(pl.multiple_of(lax.rem(start + f, 4) * TILE, TILE), TILE)


def products(tokens, fresh, outs, t):
    rows = fresh.shape[0]
    per = tokens[0].shape[0] // rows
    cut = slice(t % per * rows, (t % per + 1) * rows)
    product = lax.dot_general(tokens[t // per][cut], fresh[...], NT, preferred_element_type=F32)
    outs[t // per][cut] = product.astype(BF16)


def move_of(update):
    update = update.astype(BF16)
    return update * lax.rsqrt(update * update * BF16(1 / step_rate**2) + BF16(soft_width / step_rate**2))


def forward_kernel(parts, first, back_rows, back_cols, *refs):
    groups = len(parts)
    refs = list(refs)
    bands = [refs.pop(0) for _ in range(groups + 1)]
    sources = [refs.pop(0) for _ in range(2)]
    weights = [[refs.pop(0) for _ in range(n)] for n in parts]
    outs = [refs.pop(0) for _ in range(2 * groups)]
    step, own, other, raw, *fresh, sems, token_sems = refs
    tokens = (own, other)
    wide = WIDE * TILE
    rows, width = step.shape
    per = own.shape[0] // rows
    start = first[0]
    copies = row_copies(weights[:1], raw, sems, 0)
    token_copies = []
    for t in range(2 * per):
        cut = pl.ds(t % per * rows, rows)
        token_copies.append(
            pltpu.make_async_copy(sources[t // per].at[cut], tokens[t // per].at[cut], token_sems.at[t])
        )
        token_copies[t].start()
    copies += row_copies(weights[1:], raw, sems, 1)

    def renew(g, f):
        tall = dot(back_rows[...], bands[g][f * BAND : (f + 1) * BAND]).astype(BF16)
        move = move_of(dot(stacked(tall, WIDE * BAND), back_cols[...]))
        at = rows_at(start, f)
        for k in range(width // wide):
            cut = slice(k * wide, (k + 1) * wide)
            part = move[k * TILE : (k + 1) * TILE]
            if g == groups:
                step[at, cut] = part
            else:
                fresh[g % 2][at, cut] = raw[g, f, :, cut] - part

    for f in range(4):
        copies[0][f].wait()
        renew(0, f)
    for g in range(groups):
        if g + 1 < groups:
            for f in range(4):
                copies[g + 1][f].wait()
        for t in range(4):
            if g == 0:
                token_copies[t].wait()
            products(tokens, fresh[g % 2], outs[2 * g : 2 * g + 2], t)
            renew(g + 1, t)


def last_kernel(parts, first, own, other, step, *refs):
    refs = list(refs)
    weights = [refs.pop(0) for _ in range(parts)]
    out_own, out_other, raw, fresh, sems = refs
    copies = row_copies([weights], raw, sems, 0)[0]
    for f in range(4):
        copies[f].wait()
        at = rows_at(first[0], f)
        fresh[at] = raw[0, f] - step[at]
    for t in range(4):
        products((own, other), fresh, (out_own, out_other), t)


def weave_kernel(where, *refs):
    mine, theirs, out, held = refs[:4], refs[4:8], refs[8], refs[9]
    core, my_start, their_start = where[0], where[1], where[2]
    for g in range(4):
        held[1 - core, lax.rem(my_start + g, 4)] = mine[g][...]
        held[core, lax.rem(their_start + g, 4)] = theirs[g][...]
    for y in range(4):
        for z in range(4):
            left = held[0, y, :, z * TILE : (z + 1) * TILE]
            right = held[1, z, :, y * TILE : (y + 1) * TILE]
            j = (y * 4 + z) * 2 * TILE
            out[:, j : j + 2 * TILE] = jnp.concatenate([left, right], axis=1)


def on_device(momentum, gradient, weight, activations):
    cosines = cosine_rows()
    high, low = halves(cosines)
    eye = np.eye(WIDE)
    cols_hi, cols_lo = (np.kron(eye, np.asarray(h, np.float32).T).astype(jnp.bfloat16) for h in (high, low))
    rows3 = np.concatenate([high, high, low], axis=1)
    back_rows3 = np.concatenate([high.T, high.T, low.T], axis=1)
    back_hi, back_lo = cols_hi.T, cols_lo.T
    back_rows = high.T
    width = weight.shape[1]
    narrow = width // TILE * BAND
    rows = weight.shape[0]
    tokens = activations.shape[0]

    core = lax.axis_index("fsdp") % 2
    y = lax.axis_index("fsdp") // 8
    z = lax.axis_index("fsdp") // 2 % 4
    first = jnp.where(core == 0, y, z).astype(jnp.int32)
    second = jnp.where(core == 0, z, y).astype(jnp.int32)

    shape = jax.ShapeDtypeStruct
    steps = width // (WIDE * TILE)
    exact, rounded = call(
        bands_kernel,
        (shape((BAND, narrow), F32), shape((BAND, narrow), BF16)),
        (),
        (
            pltpu.VMEM((steps, rows, WIDE * TILE), F32),
            pltpu.VMEM((steps, rows, WIDE * TILE), BF16),
            pltpu.VMEM((2 * WIDE * TILE, WIDE * BAND), BF16),
            pltpu.VMEM(rows3.shape, BF16),
            pltpu.SemaphoreType.DMA((2 * steps + 2,)),
        ),
        kept=(momentum, gradient, np.concatenate([cols_hi, cols_lo], axis=0), rows3),
    )

    def after(value, *others):
        return lax.optimization_barrier((value, *others))[0]

    swapped = fetch(weight, sibling)
    other = fetch(after(activations, swapped), sibling)
    swapped = after(swapped, rounded)
    ahead, behind, across = (fetch(swapped, along(0, s)) for s in (1, -1, 2))

    def join(value, source):
        return value.astype(F32) + fetch(value, source).astype(F32)

    sent = join(after(rounded, swapped), far_z).astype(BF16)
    second_sum = join(after(sent, ahead, behind, other), pair_x).astype(BF16)
    total = join(after(second_sum, across), along_x(2))

    new_momentum = call(
        residual_kernel,
        shape(momentum.shape, F32),
        (momentum, gradient, exact, back_rows3, back_hi, back_lo),
    )
    direction = call(
        direction_kernel,
        shape((rows, width), F32),
        (total, back_rows3, back_hi, back_lo),
    )

    early = after(jnp.concatenate([swapped, ahead], axis=0), sent)
    late = jnp.concatenate([across, behind], axis=0)
    next_early, last_early = fetch(early, along(1, 1)), fetch(early, along(1, -1))
    next_late, last_late = fetch(late, along(1, 1)), fetch(late, along(1, -1))
    far_early, far_late = fetch(next_early, along(1, 1)), fetch(last_late, along(1, -1))
    lines = [[early, late], [next_early, next_late], [far_early, far_late], [last_early, last_late]]

    def gather(value, *others):
        pair = jnp.concatenate([value, fetch(value, along(0, 1))], axis=0)
        return jnp.concatenate([pair, fetch(after(pair, *others), along(0, 2))], axis=0)

    band_line = gather(after(total.astype(BF16), late, new_momentum))
    band_line = fetch(after(band_line, next_early, last_early, direction), sibling)
    blocks = gather(band_line, next_late, last_late).reshape(4, 4, BAND, narrow)
    bands = [blocks[:, g].reshape(4 * BAND, narrow) for g in range(4)]

    block = shape((tokens, 4 * rows), BF16)
    step = pltpu.VMEM((4 * rows, width), BF16)
    order = [0, 3, 1]
    parts = [len(lines[g]) for g in order]
    *results, step, own, other = call(
        lambda *refs: forward_kernel(parts, *refs),
        (*[block] * 6, step, *[pltpu.VMEM(activations.shape, BF16)] * 2),
        [first[None], back_rows, back_hi] + [bands[g] for g in order + [2]],
        (
            pltpu.VMEM((3, 4, rows, width), BF16),
            pltpu.VMEM((4 * rows, width), BF16),
            pltpu.VMEM((4 * rows, width), BF16),
            pltpu.SemaphoreType.DMA((3, 4)),
            pltpu.SemaphoreType.DMA((4,)),
        ),
        limit=40,
        flops=3 * 2 * 2 * tokens * 4 * rows * width,
        smem=1,
        kept=[activations, other] + [line for g in order for line in lines[g]],
    )
    results += call(
        lambda *refs: last_kernel(len(lines[2]), *refs),
        (block, block),
        [first[None]],
        (
            pltpu.VMEM((1, 4, rows, width), BF16),
            pltpu.VMEM((4 * rows, width), BF16),
            pltpu.SemaphoreType.DMA((1, 4)),
        ),
        limit=24,
        flops=2 * 2 * tokens * 4 * rows * width,
        smem=1,
        kept=lines[2],
        resident=(own, other, step),
    )
    mine, theirs = [None] * 4, [None] * 4
    for n, g in enumerate(order + [2]):
        mine[g] = results[2 * n]
        theirs[g] = fetch(results[2 * n + 1], sibling)
    where = jnp.stack([core.astype(jnp.int32), second, first])
    projected = call(
        weave_kernel,
        shape((tokens, 32 * rows), BF16),
        (where, *mine, *theirs),
        (pltpu.VMEM((2, 4, tokens, 4 * rows), BF16),),
        smem=1,
    )
    return (new_momentum, direction, projected)


def solution(mesh):
    return jax.shard_map(
        on_device,
        mesh=mesh,
        in_specs=(
            P("rep", "fsdp", None),
            P("rep", "fsdp", None),
            P("fsdp", None),
            P(("rep", "fsdp"), None),
        ),
        out_specs=(P("rep", "fsdp", None), P("fsdp", None), P(("rep", "fsdp"), None)),
        check_vma=False,
    )
```

```python
import math

import jax
import jax.numpy as jnp
import numpy as np
from jax import lax
from jax.experimental import pallas as pl
from jax.experimental.pallas import tpu as pltpu
from jax.sharding import PartitionSpec as P

TILE = 64
BAND = 16
WIDE = 8
AXES = ("rep", "fsdp")

momentum_decay = 0.9
step_rate = 0.02
soft_width = 0.25

F32 = jnp.float32
BF16 = jnp.bfloat16
NT = (((1,), (1,)), ((), ()))


def cosine_rows():
    freq = np.arange(BAND, dtype=np.float64)[:, None]
    place = np.arange(TILE, dtype=np.float64)[None, :]
    factor = np.where(freq == 0.0, math.sqrt(1.0 / TILE), math.sqrt(2.0 / TILE))
    return factor * np.cos(math.pi * (2.0 * place + 1.0) * freq / (2.0 * TILE))


def halves(array):
    high = np.asarray(array, np.float32).astype(jnp.bfloat16)
    low = (np.asarray(array, np.float64) - high.astype(np.float64)).astype(jnp.bfloat16)
    return high, low


def split(value):
    high = value.astype(BF16)
    return high, (value - high.astype(F32)).astype(BF16)


def dot(a, b):
    return jnp.dot(a, b, preferred_element_type=F32)


def spot(index):
    rep, rest = divmod(index, 32)
    high, x = divmod(rep, 4)
    y, rest = divmod(rest, 8)
    low, core = divmod(rest, 2)
    return x, y, high * 4 + low, core


def place(x, y, z, core):
    x, y, z = x % 4, y % 4, z % 8
    return ((z // 4) * 4 + x) * 32 + y * 8 + (z % 4) * 2 + core


def fetch(value, source):
    return lax.ppermute(value, AXES, [(place(*source(*spot(i))), i) for i in range(256)])


def along(axis, step):
    def source(x, y, z, core):
        if (core + axis) % 2 == 0:
            return x, y + step, z, core
        if step == 2 and z % 2:
            return x, y, z - 2, core
        return x, y, z + step, core

    return source


def along_x(step):
    return lambda x, y, z, core: (x + step, y, z, core)


def pair_x(x, y, z, core):
    return x ^ 1, y, z, core


def far_z(x, y, z, core):
    return x, y, z + 4, core


def sibling(x, y, z, core):
    return x, y, z, 1 - core


def call(kernel, out_shape, inputs, scratch=(), limit=16, flops=0, smem=0, kept=(), resident=()):
    specs = [pl.BlockSpec(memory_space=pltpu.SMEM)] * smem
    specs += [pl.BlockSpec(memory_space=pltpu.VMEM)] * (len(inputs) - smem + len(resident))
    specs += [pl.BlockSpec(memory_space=pltpu.HBM)] * len(kept)
    resident = [pltpu.with_memory_space_constraint(v, pltpu.VMEM) for v in resident]
    kept = [pltpu.with_memory_space_constraint(v, pltpu.HBM) for v in kept]
    inputs = (*inputs, *resident, *kept)
    moved = sum(math.prod(v.shape) * v.dtype.itemsize for v in inputs)
    return pl.pallas_call(
        kernel,
        out_shape=out_shape,
        in_specs=specs,
        out_specs=jax.tree.map(
            lambda _: pl.BlockSpec(memory_space=pltpu.VMEM),
            out_shape,
            is_leaf=lambda v: not isinstance(v, tuple),
        ),
        scratch_shapes=list(scratch),
        compiler_params=pltpu.CompilerParams(vmem_limit_bytes=limit << 20),
        cost_estimate=pl.CostEstimate(flops=flops, bytes_accessed=moved, transcendentals=0),
    )(*inputs)


def stacked(value, wide):
    return jnp.concatenate(
        [value[:, k * wide : (k + 1) * wide] for k in range(value.shape[1] // wide)], axis=0
    )


def mixed_of(momentum, gradient):
    return momentum_decay * momentum[0] + gradient[0].astype(F32)


def bands_kernel(momentum, gradient, cols, rows3, exact, rounded, m, g, c, r, sems):
    wide = WIDE * TILE
    steps = momentum.shape[2] // wide
    copies = [pltpu.make_async_copy(cols, c, sems.at[2 * steps])]
    copies += [pltpu.make_async_copy(rows3, r, sems.at[2 * steps + 1])]
    for k in range(steps):
        cut = pl.ds(k * wide, wide)
        copies += [
            pltpu.make_async_copy(momentum.at[0, :, cut], m.at[k], sems.at[2 * k]),
            pltpu.make_async_copy(gradient.at[0, :, cut], g.at[k], sems.at[2 * k + 1]),
        ]
    for copy in copies:
        copy.start()
    copies[0].wait()
    narrow = []
    for k in range(steps):
        copies[2 * k + 2].wait()
        copies[2 * k + 3].wait()
        high, low = split(momentum_decay * m[k] + g[k].astype(F32))
        narrow.append(dot(high, c[:wide]) + dot(low, c[:wide]) + dot(high, c[wide:]))
    copies[1].wait()
    high, low = split(jnp.concatenate(narrow, axis=1))
    bands = dot(r[...], jnp.concatenate([high, low, high], axis=0))
    exact[...] = bands
    rounded[...] = bands.astype(BF16)


def restored(bands, back_rows3, back_hi, back_lo):
    high, low = split(bands)
    tall = dot(back_rows3[...], jnp.concatenate([high, low, high], axis=0))
    high, low = split(stacked(tall, WIDE * BAND))
    return dot(high, back_hi[...]) + dot(low, back_hi[...]) + dot(high, back_lo[...])


def residual_kernel(momentum, gradient, bands, back_rows3, back_hi, back_lo, out):
    mixed = mixed_of(momentum, gradient)
    low = restored(bands[...], back_rows3, back_hi, back_lo)
    wide = WIDE * TILE
    for k in range(mixed.shape[1] // wide):
        cut = slice(k * wide, (k + 1) * wide)
        out[0, :, cut] = mixed[:, cut] - low[k * TILE : (k + 1) * TILE]


def soft_sign(update):
    return update * lax.rsqrt(update * update + soft_width)


def direction_kernel(total, back_rows3, back_hi, back_lo, out):
    sign = soft_sign(restored(total[...], back_rows3, back_hi, back_lo))
    wide = WIDE * TILE
    for k in range(out.shape[1] // wide):
        out[:, k * wide : (k + 1) * wide] = sign[k * TILE : (k + 1) * TILE]


def row_copies(weights, raw, sems, base):
    copies = []
    for g, refs in enumerate(weights):
        pieces = [(ref, r) for ref in refs for r in range(0, ref.shape[0], TILE)]
        copies.append(
            [
                pltpu.make_async_copy(ref.at[r : r + TILE], raw.at[base + g, f], sems.at[base + g, f])
                for f, (ref, r) in enumerate(pieces)
            ]
        )
        for copy in copies[g]:
            copy.start()
    return copies


def rows_at(start, f):
    return pl.ds(pl.multiple_of(lax.rem(start + f, 4) * TILE, TILE), TILE)


def products(tokens, fresh, outs, t):
    rows = fresh.shape[0]
    per = tokens[0].shape[0] // rows
    cut = slice(t % per * rows, (t % per + 1) * rows)
    product = lax.dot_general(tokens[t // per][cut], fresh[...], NT, preferred_element_type=F32)
    outs[t // per][cut] = product.astype(BF16)


def move_of(update):
    update = update.astype(BF16)
    return update * lax.rsqrt(update * update * BF16(1 / step_rate**2) + BF16(soft_width / step_rate**2))


def forward_kernel(parts, load, extra, first, back_rows, back_cols, *refs):
    groups = len(parts)
    refs = list(refs)
    bands = [refs.pop(0) for _ in range(groups + extra)]
    sources = [refs.pop(0) for _ in range(2)]
    weights = [[refs.pop(0) for _ in range(n)] for n in parts]
    outs = [refs.pop(0) for _ in range(2 * groups)]
    tokens = [refs.pop(0) for _ in range(2)] if load else sources
    step = refs.pop(0) if extra else None
    token_sems = refs.pop() if load else None
    raw, *fresh, sems = refs
    wide = WIDE * TILE
    rows, width = fresh[0].shape
    per = tokens[0].shape[0] // rows
    start = first[0]
    copies = row_copies(weights[:1], raw, sems, 0)
    token_copies = []
    if load:
        for t in range(2 * per):
            cut = pl.ds(t % per * rows, rows)
            token_copies.append(
                pltpu.make_async_copy(sources[t // per].at[cut], tokens[t // per].at[cut], token_sems.at[t])
            )
            token_copies[t].start()
    copies += row_copies(weights[1:], raw, sems, 1)

    def renew(g, f):
        tall = dot(back_rows[...], bands[g][f * BAND : (f + 1) * BAND]).astype(BF16)
        move = move_of(dot(stacked(tall, WIDE * BAND), back_cols[...]))
        at = rows_at(start, f)
        for k in range(width // wide):
            cut = slice(k * wide, (k + 1) * wide)
            part = move[k * TILE : (k + 1) * TILE]
            if g == groups:
                step[at, cut] = part
            else:
                fresh[g % 2][at, cut] = raw[g, f, :, cut] - part

    for f in range(4):
        copies[0][f].wait()
        renew(0, f)
    for g in range(groups):
        if g + 1 < groups:
            for f in range(4):
                copies[g + 1][f].wait()
        for t in range(4):
            if g == 0 and load:
                token_copies[t].wait()
            products(tokens, fresh[g % 2], outs[2 * g : 2 * g + 2], t)
            if g + 1 < groups + extra:
                renew(g + 1, t)


def last_kernel(parts, first, own, other, step, *refs):
    refs = list(refs)
    weights = [refs.pop(0) for _ in range(parts)]
    out_own, out_other, raw, fresh, sems = refs
    copies = row_copies([weights], raw, sems, 0)[0]
    for f in range(4):
        copies[f].wait()
        at = rows_at(first[0], f)
        fresh[at] = raw[0, f] - step[at]
    for t in range(4):
        products((own, other), fresh, (out_own, out_other), t)


def weave_kernel(where, *refs):
    mine, theirs, out, held = refs[:4], refs[4:8], refs[8], refs[9]
    core, my_start, their_start = where[0], where[1], where[2]
    for g in range(4):
        held[1 - core, lax.rem(my_start + g, 4)] = mine[g][...]
        held[core, lax.rem(their_start + g, 4)] = theirs[g][...]
    for y in range(4):
        for z in range(4):
            left = held[0, y, :, z * TILE : (z + 1) * TILE]
            right = held[1, z, :, y * TILE : (y + 1) * TILE]
            j = (y * 4 + z) * 2 * TILE
            out[:, j : j + 2 * TILE] = jnp.concatenate([left, right], axis=1)


def on_device(momentum, gradient, weight, activations):
    cosines = cosine_rows()
    high, low = halves(cosines)
    eye = np.eye(WIDE)
    cols_hi, cols_lo = (np.kron(eye, np.asarray(h, np.float32).T).astype(jnp.bfloat16) for h in (high, low))
    rows3 = np.concatenate([high, high, low], axis=1)
    back_rows3 = np.concatenate([high.T, high.T, low.T], axis=1)
    back_hi, back_lo = cols_hi.T, cols_lo.T
    back_rows = high.T
    width = weight.shape[1]
    narrow = width // TILE * BAND
    rows = weight.shape[0]
    tokens = activations.shape[0]

    core = lax.axis_index("fsdp") % 2
    y = lax.axis_index("fsdp") // 8
    z = lax.axis_index("fsdp") // 2 % 4
    first = jnp.where(core == 0, y, z).astype(jnp.int32)
    second = jnp.where(core == 0, z, y).astype(jnp.int32)

    shape = jax.ShapeDtypeStruct
    steps = width // (WIDE * TILE)
    exact, rounded = call(
        bands_kernel,
        (shape((BAND, narrow), F32), shape((BAND, narrow), BF16)),
        (),
        (
            pltpu.VMEM((steps, rows, WIDE * TILE), F32),
            pltpu.VMEM((steps, rows, WIDE * TILE), BF16),
            pltpu.VMEM((2 * WIDE * TILE, WIDE * BAND), BF16),
            pltpu.VMEM(rows3.shape, BF16),
            pltpu.SemaphoreType.DMA((2 * steps + 2,)),
        ),
        kept=(momentum, gradient, np.concatenate([cols_hi, cols_lo], axis=0), rows3),
    )

    def after(value, *others):
        return lax.optimization_barrier((value, *others))[0]

    swapped = fetch(weight, sibling)
    swapped = after(swapped, rounded)
    other = fetch(after(activations, swapped), sibling)
    ahead, behind, across = (fetch(swapped, along(0, s)) for s in (1, -1, 2))

    def join(value, source):
        return value.astype(F32) + fetch(value, source).astype(F32)

    sent = join(after(rounded, swapped), far_z).astype(BF16)
    second_sum = join(after(sent, ahead, behind, other), pair_x).astype(BF16)
    total = join(second_sum, along_x(2))

    early = after(jnp.concatenate([swapped, ahead], axis=0), sent)
    late = jnp.concatenate([across, behind], axis=0)
    next_early, last_early = fetch(early, along(1, 1)), fetch(early, along(1, -1))
    def gather(value):
        return jnp.concatenate([value] + [fetch(value, along(0, s)) for s in (1, 2, -1)], axis=0)

    band_line = gather(after(total.astype(BF16), late))
    late = after(late, band_line)
    next_late, last_late = fetch(late, along(1, 1)), fetch(late, along(1, -1))
    band_line = fetch(after(band_line, next_early, last_early), sibling)
    blocks = gather(band_line).reshape(4, 4, BAND, narrow)
    far_early = fetch(after(next_early, blocks), along(1, 1))
    lines = [[early, late], [next_early, next_late], [far_early], [last_early, last_late]]
    bands = [blocks[:, g].reshape(4 * BAND, narrow) for g in range(4)]

    block = shape((tokens, 4 * rows), BF16)
    held = pltpu.VMEM(activations.shape, BF16)
    rows_like = pltpu.VMEM((4 * rows, width), BF16)

    def forward(order, more=()):
        parts, load = [len(lines[g]) for g in order], not more
        count = len(order)
        return call(
            lambda *refs: forward_kernel(parts, load, len(more), *refs),
            (*[block] * (2 * count), *([held] * 2 if load else []), *[rows_like] * len(more)),
            [first[None], back_rows, back_hi] + [bands[g] for g in (*order, *more)],
            (
                pltpu.VMEM((count, 4, rows, width), BF16),
                rows_like,
                rows_like,
                pltpu.SemaphoreType.DMA((count, 4)),
                *([pltpu.SemaphoreType.DMA((4,))] if load else []),
            ),
            limit=32,
            flops=count * 2 * 2 * tokens * 4 * rows * width,
            smem=1,
            resident=() if load else (own, other),
            kept=([activations, other] if load else []) + [line for g in order for line in lines[g]],
        )

    *results, own, other = forward([0])
    first_out = results[0]
    lines[2].append(fetch(after(last_late, first_out), along(1, -1)))
    new_momentum = call(
        residual_kernel,
        shape(momentum.shape, F32),
        (momentum, gradient, after(exact, first_out), back_rows3, back_hi, back_lo),
    )
    direction = call(
        direction_kernel,
        shape((rows, width), F32),
        (after(total, first_out), back_rows3, back_hi, back_lo),
    )
    *more, step = forward([3, 1], [2])
    results += more
    lines[2][0] = after(lines[2][0], direction, new_momentum)
    results += call(
        lambda *refs: last_kernel(len(lines[2]), *refs),
        (block, block),
        [first[None]],
        (
            pltpu.VMEM((1, 4, rows, width), BF16),
            rows_like,
            pltpu.SemaphoreType.DMA((1, 4)),
        ),
        limit=24,
        flops=2 * 2 * tokens * 4 * rows * width,
        smem=1,
        kept=lines[2],
        resident=(own, other, step),
    )
    mine, theirs = [None] * 4, [None] * 4
    for n, g in enumerate((0, 3, 1, 2)):
        mine[g] = results[2 * n]
        theirs[g] = fetch(results[2 * n + 1], sibling)
    where = jnp.stack([core.astype(jnp.int32), second, first])
    projected = call(
        weave_kernel,
        shape((tokens, 32 * rows), BF16),
        (where, *mine, *theirs),
        (pltpu.VMEM((2, 4, tokens, 4 * rows), BF16),),
        smem=1,
    )
    return (new_momentum, direction, projected)


def solution(mesh):
    return jax.shard_map(
        on_device,
        mesh=mesh,
        in_specs=(
            P("rep", "fsdp", None),
            P("rep", "fsdp", None),
            P("fsdp", None),
            P(("rep", "fsdp"), None),
        ),
        out_specs=(P("rep", "fsdp", None), P("fsdp", None), P(("rep", "fsdp"), None)),
        check_vma=False,
    )
```

```python
import math

import jax
import jax.numpy as jnp
import numpy as np
from jax import lax
from jax.experimental import pallas as pl
from jax.experimental.pallas import tpu as pltpu
from jax.sharding import PartitionSpec as P

TILE = 64
BAND = 16
WIDE = 8
AXES = ("rep", "fsdp")

momentum_decay = 0.9
step_rate = 0.02
soft_width = 0.25

F32 = jnp.float32
BF16 = jnp.bfloat16
NT = (((1,), (1,)), ((), ()))


def cosine_rows():
    freq = np.arange(BAND, dtype=np.float64)[:, None]
    place = np.arange(TILE, dtype=np.float64)[None, :]
    factor = np.where(freq == 0.0, math.sqrt(1.0 / TILE), math.sqrt(2.0 / TILE))
    return factor * np.cos(math.pi * (2.0 * place + 1.0) * freq / (2.0 * TILE))


def halves(array):
    high = np.asarray(array, np.float32).astype(jnp.bfloat16)
    low = (np.asarray(array, np.float64) - high.astype(np.float64)).astype(jnp.bfloat16)
    return high, low


def split(value):
    high = value.astype(BF16)
    return high, (value - high.astype(F32)).astype(BF16)


def dot(a, b):
    return jnp.dot(a, b, preferred_element_type=F32)


def spot(index):
    rep, rest = divmod(index, 32)
    high, x = divmod(rep, 4)
    y, rest = divmod(rest, 8)
    low, core = divmod(rest, 2)
    return x, y, high * 4 + low, core


def place(x, y, z, core):
    x, y, z = x % 4, y % 4, z % 8
    return ((z // 4) * 4 + x) * 32 + y * 8 + (z % 4) * 2 + core


def fetch(value, source):
    return lax.ppermute(value, AXES, [(place(*source(*spot(i))), i) for i in range(256)])


def along(axis, step):
    def source(x, y, z, core):
        if (core + axis) % 2 == 0:
            return x, y + step, z, core
        if step == 2 and z % 2:
            return x, y, z - 2, core
        return x, y, z + step, core

    return source


def along_x(step):
    return lambda x, y, z, core: (x + step, y, z, core)


def pair_x(x, y, z, core):
    return x ^ 1, y, z, core


def far_z(x, y, z, core):
    return x, y, z + 4, core


def sibling(x, y, z, core):
    return x, y, z, 1 - core


def call(kernel, out_shape, inputs, scratch=(), limit=16, flops=0, smem=0, kept=(), resident=()):
    specs = [pl.BlockSpec(memory_space=pltpu.SMEM)] * smem
    specs += [pl.BlockSpec(memory_space=pltpu.VMEM)] * (len(inputs) - smem + len(resident))
    specs += [pl.BlockSpec(memory_space=pltpu.HBM)] * len(kept)
    resident = [pltpu.with_memory_space_constraint(v, pltpu.VMEM) for v in resident]
    kept = [pltpu.with_memory_space_constraint(v, pltpu.HBM) for v in kept]
    inputs = (*inputs, *resident, *kept)
    moved = sum(math.prod(v.shape) * v.dtype.itemsize for v in inputs)
    return pl.pallas_call(
        kernel,
        out_shape=out_shape,
        in_specs=specs,
        out_specs=jax.tree.map(
            lambda _: pl.BlockSpec(memory_space=pltpu.VMEM),
            out_shape,
            is_leaf=lambda v: not isinstance(v, tuple),
        ),
        scratch_shapes=list(scratch),
        compiler_params=pltpu.CompilerParams(vmem_limit_bytes=limit << 20),
        cost_estimate=pl.CostEstimate(flops=flops, bytes_accessed=moved, transcendentals=0),
    )(*inputs)


def stacked(value, wide):
    return jnp.concatenate(
        [value[:, k * wide : (k + 1) * wide] for k in range(value.shape[1] // wide)], axis=0
    )


def mixed_of(momentum, gradient):
    return momentum_decay * momentum[0] + gradient[0].astype(F32)


def bands_kernel(momentum, gradient, cols, rows3, exact, rounded, m, g, c, r, sems):
    wide = WIDE * TILE
    steps = momentum.shape[2] // wide
    copies = [pltpu.make_async_copy(cols, c, sems.at[2 * steps])]
    copies += [pltpu.make_async_copy(rows3, r, sems.at[2 * steps + 1])]
    for k in range(steps):
        cut = pl.ds(k * wide, wide)
        copies += [
            pltpu.make_async_copy(momentum.at[0, :, cut], m.at[k], sems.at[2 * k]),
            pltpu.make_async_copy(gradient.at[0, :, cut], g.at[k], sems.at[2 * k + 1]),
        ]
    for copy in copies:
        copy.start()
    copies[0].wait()
    narrow = []
    for k in range(steps):
        copies[2 * k + 2].wait()
        copies[2 * k + 3].wait()
        high, low = split(momentum_decay * m[k] + g[k].astype(F32))
        narrow.append(dot(high, c[:wide]) + dot(low, c[:wide]) + dot(high, c[wide:]))
    copies[1].wait()
    high, low = split(jnp.concatenate(narrow, axis=1))
    bands = dot(r[...], jnp.concatenate([high, low, high], axis=0))
    exact[...] = bands
    rounded[...] = bands.astype(BF16)


def restored(bands, back_rows3, back_hi, back_lo):
    high, low = split(bands)
    tall = dot(back_rows3[...], jnp.concatenate([high, low, high], axis=0))
    high, low = split(stacked(tall, WIDE * BAND))
    return dot(high, back_hi[...]) + dot(low, back_hi[...]) + dot(high, back_lo[...])


def residual_kernel(momentum, gradient, bands, back_rows3, back_hi, back_lo, out):
    mixed = mixed_of(momentum, gradient)
    low = restored(bands[...], back_rows3, back_hi, back_lo)
    wide = WIDE * TILE
    for k in range(mixed.shape[1] // wide):
        cut = slice(k * wide, (k + 1) * wide)
        out[0, :, cut] = mixed[:, cut] - low[k * TILE : (k + 1) * TILE]


def soft_sign(update):
    return update * lax.rsqrt(update * update + soft_width)


def direction_kernel(total, back_rows3, back_hi, back_lo, out):
    sign = soft_sign(restored(total[...], back_rows3, back_hi, back_lo))
    wide = WIDE * TILE
    for k in range(out.shape[1] // wide):
        out[:, k * wide : (k + 1) * wide] = sign[k * TILE : (k + 1) * TILE]


def row_copies(weights, raw, sems, base):
    copies = []
    for g, refs in enumerate(weights):
        pieces = [(ref, r) for ref in refs for r in range(0, ref.shape[0], TILE)]
        copies.append(
            [
                pltpu.make_async_copy(ref.at[r : r + TILE], raw.at[base + g, f], sems.at[base + g, f])
                for f, (ref, r) in enumerate(pieces)
            ]
        )
        for copy in copies[g]:
            copy.start()
    return copies


def rows_at(start, f):
    return pl.ds(pl.multiple_of(lax.rem(start + f, 4) * TILE, TILE), TILE)


def products(tokens, fresh, outs, t):
    rows = fresh.shape[0]
    per = tokens[0].shape[0] // rows
    cut = slice(t % per * rows, (t % per + 1) * rows)
    product = lax.dot_general(tokens[t // per][cut], fresh[...], NT, preferred_element_type=F32)
    outs[t // per][cut] = product.astype(BF16)


def move_of(update):
    update = update.astype(BF16)
    return update * lax.rsqrt(update * update * BF16(1 / step_rate**2) + BF16(soft_width / step_rate**2))


def forward_kernel(parts, load, extra, first, back_rows, back_cols, *refs):
    groups = len(parts)
    refs = list(refs)
    bands = [refs.pop(0) for _ in range(groups + extra)]
    sources = [refs.pop(0) for _ in range(2)]
    weights = [[refs.pop(0) for _ in range(n)] for n in parts]
    outs = [refs.pop(0) for _ in range(2 * groups)]
    tokens = [refs.pop(0) for _ in range(2)] if load else sources
    step = refs.pop(0) if extra else None
    token_sems = refs.pop() if load else None
    raw, *fresh, sems = refs
    wide = WIDE * TILE
    rows, width = fresh[0].shape
    per = tokens[0].shape[0] // rows
    start = first[0]
    copies = row_copies(weights[:1], raw, sems, 0)
    token_copies = []
    if load:
        for t in range(2 * per):
            cut = pl.ds(t % per * rows, rows)
            token_copies.append(
                pltpu.make_async_copy(sources[t // per].at[cut], tokens[t // per].at[cut], token_sems.at[t])
            )
            token_copies[t].start()
    copies += row_copies(weights[1:], raw, sems, 1)

    def renew(g, f):
        tall = dot(back_rows[...], bands[g][f * BAND : (f + 1) * BAND]).astype(BF16)
        move = move_of(dot(stacked(tall, WIDE * BAND), back_cols[...]))
        at = rows_at(start, f)
        for k in range(width // wide):
            cut = slice(k * wide, (k + 1) * wide)
            part = move[k * TILE : (k + 1) * TILE]
            if g == groups:
                step[at, cut] = part
            else:
                fresh[g % 2][at, cut] = raw[g, f, :, cut] - part

    for f in range(4):
        copies[0][f].wait()
        renew(0, f)
    for g in range(groups):
        if g + 1 < groups:
            for f in range(4):
                copies[g + 1][f].wait()
        for t in range(4):
            if g == 0 and load:
                token_copies[t].wait()
            products(tokens, fresh[g % 2], outs[2 * g : 2 * g + 2], t)
            if g + 1 < groups + extra:
                renew(g + 1, t)


def last_kernel(parts, first, own, other, step, *refs):
    refs = list(refs)
    weights = [refs.pop(0) for _ in range(parts)]
    out_own, out_other, raw, fresh, sems = refs
    copies = row_copies([weights], raw, sems, 0)[0]
    for f in range(4):
        copies[f].wait()
        at = rows_at(first[0], f)
        fresh[at] = raw[0, f] - step[at]
    for t in range(4):
        products((own, other), fresh, (out_own, out_other), t)


def weave_kernel(where, *refs):
    mine, theirs, out, held = refs[:4], refs[4:8], refs[8], refs[9]
    core, my_start, their_start = where[0], where[1], where[2]
    for g in range(4):
        held[1 - core, lax.rem(my_start + g, 4)] = mine[g][...]
        held[core, lax.rem(their_start + g, 4)] = theirs[g][...]
    for y in range(4):
        for z in range(4):
            left = held[0, y, :, z * TILE : (z + 1) * TILE]
            right = held[1, z, :, y * TILE : (y + 1) * TILE]
            j = (y * 4 + z) * 2 * TILE
            out[:, j : j + 2 * TILE] = jnp.concatenate([left, right], axis=1)


def on_device(momentum, gradient, weight, activations):
    cosines = cosine_rows()
    high, low = halves(cosines)
    eye = np.eye(WIDE)
    cols_hi, cols_lo = (np.kron(eye, np.asarray(h, np.float32).T).astype(jnp.bfloat16) for h in (high, low))
    rows3 = np.concatenate([high, high, low], axis=1)
    back_rows3 = np.concatenate([high.T, high.T, low.T], axis=1)
    back_hi, back_lo = cols_hi.T, cols_lo.T
    back_rows = high.T
    width = weight.shape[1]
    narrow = width // TILE * BAND
    rows = weight.shape[0]
    tokens = activations.shape[0]

    core = lax.axis_index("fsdp") % 2
    y = lax.axis_index("fsdp") // 8
    z = lax.axis_index("fsdp") // 2 % 4
    first = jnp.where(core == 0, y, z).astype(jnp.int32)
    second = jnp.where(core == 0, z, y).astype(jnp.int32)

    shape = jax.ShapeDtypeStruct
    steps = width // (WIDE * TILE)
    exact, rounded = call(
        bands_kernel,
        (shape((BAND, narrow), F32), shape((BAND, narrow), BF16)),
        (),
        (
            pltpu.VMEM((steps, rows, WIDE * TILE), F32),
            pltpu.VMEM((steps, rows, WIDE * TILE), BF16),
            pltpu.VMEM((2 * WIDE * TILE, WIDE * BAND), BF16),
            pltpu.VMEM(rows3.shape, BF16),
            pltpu.SemaphoreType.DMA((2 * steps + 2,)),
        ),
        kept=(momentum, gradient, np.concatenate([cols_hi, cols_lo], axis=0), rows3),
    )

    def after(value, *others):
        return lax.optimization_barrier((value, *others))[0]

    swapped = fetch(weight, sibling)
    swapped = after(swapped, rounded)
    other = fetch(after(activations, swapped), sibling)
    ahead, behind, across = (fetch(swapped, along(0, s)) for s in (1, -1, 2))

    def join(value, source):
        return value.astype(F32) + fetch(value, source).astype(F32)

    sent = join(after(rounded, swapped), far_z).astype(BF16)
    second_sum = join(after(sent, ahead, behind, other), pair_x).astype(BF16)
    total = join(second_sum, along_x(2))

    early = after(jnp.concatenate([swapped, ahead], axis=0), second_sum)
    late = jnp.concatenate([across, behind], axis=0)
    next_early, last_early = fetch(early, along(1, 1)), fetch(early, along(1, -1))
    def gather(value):
        return jnp.concatenate([value] + [fetch(value, along(0, s)) for s in (1, 2, -1)], axis=0)

    band_line = gather(after(total.astype(BF16), late))
    late = after(late, band_line)
    next_late, last_late = fetch(late, along(1, 1)), fetch(late, along(1, -1))
    band_line = fetch(band_line, sibling)
    blocks = gather(after(band_line, next_early, last_early)).reshape(4, 4, BAND, narrow)
    far_early = fetch(after(next_early, blocks), along(1, 1))
    lines = [[early, late], [next_early, next_late], [far_early], [last_early, last_late]]
    bands = [blocks[:, g].reshape(4 * BAND, narrow) for g in range(4)]

    block = shape((tokens, 4 * rows), BF16)
    held = pltpu.VMEM(activations.shape, BF16)
    rows_like = pltpu.VMEM((4 * rows, width), BF16)

    def forward(order, more=()):
        parts, load = [len(lines[g]) for g in order], not more
        count = len(order)
        return call(
            lambda *refs: forward_kernel(parts, load, len(more), *refs),
            (*[block] * (2 * count), *([held] * 2 if load else []), *[rows_like] * len(more)),
            [first[None], back_rows, back_hi] + [bands[g] for g in (*order, *more)],
            (
                pltpu.VMEM((count, 4, rows, width), BF16),
                rows_like,
                rows_like,
                pltpu.SemaphoreType.DMA((count, 4)),
                *([pltpu.SemaphoreType.DMA((4,))] if load else []),
            ),
            limit=32,
            flops=count * 2 * 2 * tokens * 4 * rows * width,
            smem=1,
            resident=() if load else (own, other),
            kept=([activations, other] if load else []) + [line for g in order for line in lines[g]],
        )

    *results, own, other = forward([0])
    first_out = results[0]
    lines[2].append(fetch(after(last_late, first_out), along(1, -1)))
    *more, step = forward([3, 1], [2])
    results += more
    second_out = more[0]
    new_momentum = call(
        residual_kernel,
        shape(momentum.shape, F32),
        (momentum, gradient, after(exact, second_out), back_rows3, back_hi, back_lo),
    )
    direction = call(
        direction_kernel,
        shape((rows, width), F32),
        (after(total, second_out), back_rows3, back_hi, back_lo),
    )
    lines[2][0] = after(lines[2][0], direction, new_momentum)
    results += call(
        lambda *refs: last_kernel(len(lines[2]), *refs),
        (block, block),
        [first[None]],
        (
            pltpu.VMEM((1, 4, rows, width), BF16),
            rows_like,
            pltpu.SemaphoreType.DMA((1, 4)),
        ),
        limit=24,
        flops=2 * 2 * tokens * 4 * rows * width,
        smem=1,
        kept=lines[2],
        resident=(own, other, step),
    )
    mine, theirs = [None] * 4, [None] * 4
    for n, g in enumerate((0, 3, 1, 2)):
        mine[g] = results[2 * n]
        theirs[g] = fetch(results[2 * n + 1], sibling)
    where = jnp.stack([core.astype(jnp.int32), second, first])
    projected = call(
        weave_kernel,
        shape((tokens, 32 * rows), BF16),
        (where, *mine, *theirs),
        (pltpu.VMEM((2, 4, tokens, 4 * rows), BF16),),
        smem=1,
    )
    return (new_momentum, direction, projected)


def solution(mesh):
    return jax.shard_map(
        on_device,
        mesh=mesh,
        in_specs=(
            P("rep", "fsdp", None),
            P("rep", "fsdp", None),
            P("fsdp", None),
            P(("rep", "fsdp"), None),
        ),
        out_specs=(P("rep", "fsdp", None), P("fsdp", None), P(("rep", "fsdp"), None)),
        check_vma=False,
    )
```

```python
import math

import jax
import jax.numpy as jnp
import numpy as np
from jax import lax
from jax.experimental import pallas as pl
from jax.experimental.pallas import tpu as pltpu
from jax.sharding import PartitionSpec as P

TILE = 64
BAND = 16
WIDE = 8
AXES = ("rep", "fsdp")

momentum_decay = 0.9
step_rate = 0.02
soft_width = 0.25

F32 = jnp.float32
BF16 = jnp.bfloat16
NT = (((1,), (1,)), ((), ()))


def cosine_rows():
    freq = np.arange(BAND, dtype=np.float64)[:, None]
    place = np.arange(TILE, dtype=np.float64)[None, :]
    factor = np.where(freq == 0.0, math.sqrt(1.0 / TILE), math.sqrt(2.0 / TILE))
    return factor * np.cos(math.pi * (2.0 * place + 1.0) * freq / (2.0 * TILE))


def halves(array):
    high = np.asarray(array, np.float32).astype(jnp.bfloat16)
    low = (np.asarray(array, np.float64) - high.astype(np.float64)).astype(jnp.bfloat16)
    return high, low


def split(value):
    high = value.astype(BF16)
    return high, (value - high.astype(F32)).astype(BF16)


def dot(a, b):
    return jnp.dot(a, b, preferred_element_type=F32)


def spot(index):
    rep, rest = divmod(index, 32)
    high, x = divmod(rep, 4)
    y, rest = divmod(rest, 8)
    low, core = divmod(rest, 2)
    return x, y, high * 4 + low, core


def place(x, y, z, core):
    x, y, z = x % 4, y % 4, z % 8
    return ((z // 4) * 4 + x) * 32 + y * 8 + (z % 4) * 2 + core


def fetch(value, source):
    return lax.ppermute(value, AXES, [(place(*source(*spot(i))), i) for i in range(256)])


def along(axis, step):
    def source(x, y, z, core):
        if (core + axis) % 2 == 0:
            return x, y + step, z, core
        if step == 2 and z % 2:
            return x, y, z - 2, core
        return x, y, z + step, core

    return source


def along_x(step):
    return lambda x, y, z, core: (x + step, y, z, core)


def pair_x(x, y, z, core):
    return x ^ 1, y, z, core


def far_z(x, y, z, core):
    return x, y, z + 4, core


def sibling(x, y, z, core):
    return x, y, z, 1 - core


def call(kernel, out_shape, inputs, scratch=(), limit=16, flops=0, smem=0, kept=(), resident=()):
    specs = [pl.BlockSpec(memory_space=pltpu.SMEM)] * smem
    specs += [pl.BlockSpec(memory_space=pltpu.VMEM)] * (len(inputs) - smem + len(resident))
    specs += [pl.BlockSpec(memory_space=pltpu.HBM)] * len(kept)
    resident = [pltpu.with_memory_space_constraint(v, pltpu.VMEM) for v in resident]
    kept = [pltpu.with_memory_space_constraint(v, pltpu.HBM) for v in kept]
    inputs = (*inputs, *resident, *kept)
    moved = sum(math.prod(v.shape) * v.dtype.itemsize for v in inputs)
    return pl.pallas_call(
        kernel,
        out_shape=out_shape,
        in_specs=specs,
        out_specs=jax.tree.map(
            lambda _: pl.BlockSpec(memory_space=pltpu.VMEM),
            out_shape,
            is_leaf=lambda v: not isinstance(v, tuple),
        ),
        scratch_shapes=list(scratch),
        compiler_params=pltpu.CompilerParams(vmem_limit_bytes=limit << 20),
        cost_estimate=pl.CostEstimate(flops=flops, bytes_accessed=moved, transcendentals=0),
    )(*inputs)


def stacked(value, wide):
    return jnp.concatenate(
        [value[:, k * wide : (k + 1) * wide] for k in range(value.shape[1] // wide)], axis=0
    )


def mixed_of(momentum, gradient):
    return momentum_decay * momentum[0] + gradient[0].astype(F32)


def bands_kernel(momentum, gradient, cols, rows3, exact, rounded, m, g, c, r, sems):
    wide = WIDE * TILE
    steps = momentum.shape[2] // wide
    copies = [pltpu.make_async_copy(cols, c, sems.at[2 * steps])]
    copies += [pltpu.make_async_copy(rows3, r, sems.at[2 * steps + 1])]
    for k in range(steps):
        cut = pl.ds(k * wide, wide)
        copies += [
            pltpu.make_async_copy(momentum.at[0, :, cut], m.at[k], sems.at[2 * k]),
            pltpu.make_async_copy(gradient.at[0, :, cut], g.at[k], sems.at[2 * k + 1]),
        ]
    for copy in copies:
        copy.start()
    copies[0].wait()
    narrow = []
    for k in range(steps):
        copies[2 * k + 2].wait()
        copies[2 * k + 3].wait()
        high, low = split(momentum_decay * m[k] + g[k].astype(F32))
        narrow.append(dot(high, c[:wide]) + dot(low, c[:wide]) + dot(high, c[wide:]))
    copies[1].wait()
    high, low = split(jnp.concatenate(narrow, axis=1))
    bands = dot(r[...], jnp.concatenate([high, low, high], axis=0))
    exact[...] = bands
    rounded[...] = bands.astype(BF16)


def restored(bands, back_rows3, back_hi, back_lo):
    high, low = split(bands)
    tall = dot(back_rows3[...], jnp.concatenate([high, low, high], axis=0))
    high, low = split(stacked(tall, WIDE * BAND))
    return dot(high, back_hi[...]) + dot(low, back_hi[...]) + dot(high, back_lo[...])


def residual_kernel(momentum, gradient, bands, back_rows3, back_hi, back_lo, out):
    mixed = mixed_of(momentum, gradient)
    low = restored(bands[...], back_rows3, back_hi, back_lo)
    wide = WIDE * TILE
    for k in range(mixed.shape[1] // wide):
        cut = slice(k * wide, (k + 1) * wide)
        out[0, :, cut] = mixed[:, cut] - low[k * TILE : (k + 1) * TILE]


def soft_sign(update):
    return update * lax.rsqrt(update * update + soft_width)


def direction_kernel(total, back_rows3, back_hi, back_lo, out):
    sign = soft_sign(restored(total[...], back_rows3, back_hi, back_lo))
    wide = WIDE * TILE
    for k in range(out.shape[1] // wide):
        out[:, k * wide : (k + 1) * wide] = sign[k * TILE : (k + 1) * TILE]


def row_copies(weights, raw, sems, base):
    copies = []
    for g, refs in enumerate(weights):
        pieces = [(ref, r) for ref in refs for r in range(0, ref.shape[0], TILE)]
        copies.append(
            [
                pltpu.make_async_copy(ref.at[r : r + TILE], raw.at[base + g, f], sems.at[base + g, f])
                for f, (ref, r) in enumerate(pieces)
            ]
        )
        for copy in copies[g]:
            copy.start()
    return copies


def rows_at(start, f):
    return pl.ds(pl.multiple_of(lax.rem(start + f, 4) * TILE, TILE), TILE)


def products(tokens, fresh, outs, t):
    rows = fresh.shape[0]
    per = tokens[0].shape[0] // rows
    cut = slice(t % per * rows, (t % per + 1) * rows)
    product = lax.dot_general(tokens[t // per][cut], fresh[...], NT, preferred_element_type=F32)
    outs[t // per][cut] = product.astype(BF16)


def move_of(update):
    update = update.astype(BF16)
    return update * lax.rsqrt(update * update * BF16(1 / step_rate**2) + BF16(soft_width / step_rate**2))


def forward_kernel(parts, load, extra, first, back_rows, back_cols, *refs):
    groups = len(parts)
    refs = list(refs)
    bands = [refs.pop(0) for _ in range(groups + extra)]
    sources = [refs.pop(0) for _ in range(2)]
    weights = [[refs.pop(0) for _ in range(n)] for n in parts]
    outs = [refs.pop(0) for _ in range(2 * groups)]
    tokens = [refs.pop(0) for _ in range(2)] if load else sources
    step = refs.pop(0) if extra else None
    token_sems = refs.pop() if load else None
    raw, *fresh, sems = refs
    wide = WIDE * TILE
    rows, width = fresh[0].shape
    per = tokens[0].shape[0] // rows
    start = first[0]
    copies = row_copies(weights[:1], raw, sems, 0)
    token_copies = []
    if load:
        for t in range(2 * per):
            cut = pl.ds(t % per * rows, rows)
            token_copies.append(
                pltpu.make_async_copy(sources[t // per].at[cut], tokens[t // per].at[cut], token_sems.at[t])
            )
            token_copies[t].start()
    copies += row_copies(weights[1:], raw, sems, 1)

    def renew(g, f):
        tall = dot(back_rows[...], bands[g][f * BAND : (f + 1) * BAND]).astype(BF16)
        move = move_of(dot(stacked(tall, WIDE * BAND), back_cols[...]))
        at = rows_at(start, f)
        for k in range(width // wide):
            cut = slice(k * wide, (k + 1) * wide)
            part = move[k * TILE : (k + 1) * TILE]
            if g == groups:
                step[at, cut] = part
            else:
                fresh[g % 2][at, cut] = raw[g, f, :, cut] - part

    for f in range(4):
        copies[0][f].wait()
        renew(0, f)
    for g in range(groups):
        if g + 1 < groups:
            for f in range(4):
                copies[g + 1][f].wait()
        for t in range(4):
            if g == 0 and load:
                token_copies[t].wait()
            products(tokens, fresh[g % 2], outs[2 * g : 2 * g + 2], t)
            if g + 1 < groups + extra:
                renew(g + 1, t)


def last_kernel(parts, first, own, other, step, *refs):
    refs = list(refs)
    weights = [refs.pop(0) for _ in range(parts)]
    out_own, out_other, raw, fresh, sems = refs
    copies = row_copies([weights], raw, sems, 0)[0]
    for f in range(4):
        copies[f].wait()
        at = rows_at(first[0], f)
        fresh[at] = raw[0, f] - step[at]
    for t in range(4):
        products((own, other), fresh, (out_own, out_other), t)


def weave_kernel(where, *refs):
    mine, theirs, out, held = refs[:4], refs[4:8], refs[8], refs[9]
    core, my_start, their_start = where[0], where[1], where[2]
    for g in range(4):
        held[1 - core, lax.rem(my_start + g, 4)] = mine[g][...]
        held[core, lax.rem(their_start + g, 4)] = theirs[g][...]
    for y in range(4):
        for z in range(4):
            left = held[0, y, :, z * TILE : (z + 1) * TILE]
            right = held[1, z, :, y * TILE : (y + 1) * TILE]
            j = (y * 4 + z) * 2 * TILE
            out[:, j : j + 2 * TILE] = jnp.concatenate([left, right], axis=1)


def on_device(momentum, gradient, weight, activations):
    cosines = cosine_rows()
    high, low = halves(cosines)
    eye = np.eye(WIDE)
    cols_hi, cols_lo = (np.kron(eye, np.asarray(h, np.float32).T).astype(jnp.bfloat16) for h in (high, low))
    rows3 = np.concatenate([high, high, low], axis=1)
    back_rows3 = np.concatenate([high.T, high.T, low.T], axis=1)
    back_hi, back_lo = cols_hi.T, cols_lo.T
    back_rows = high.T
    width = weight.shape[1]
    narrow = width // TILE * BAND
    rows = weight.shape[0]
    tokens = activations.shape[0]

    core = lax.axis_index("fsdp") % 2
    y = lax.axis_index("fsdp") // 8
    z = lax.axis_index("fsdp") // 2 % 4
    first = jnp.where(core == 0, y, z).astype(jnp.int32)
    second = jnp.where(core == 0, z, y).astype(jnp.int32)

    shape = jax.ShapeDtypeStruct
    steps = width // (WIDE * TILE)
    exact, rounded = call(
        bands_kernel,
        (shape((BAND, narrow), F32), shape((BAND, narrow), BF16)),
        (),
        (
            pltpu.VMEM((steps, rows, WIDE * TILE), F32),
            pltpu.VMEM((steps, rows, WIDE * TILE), BF16),
            pltpu.VMEM((2 * WIDE * TILE, WIDE * BAND), BF16),
            pltpu.VMEM(rows3.shape, BF16),
            pltpu.SemaphoreType.DMA((2 * steps + 2,)),
        ),
        kept=(momentum, gradient, np.concatenate([cols_hi, cols_lo], axis=0), rows3),
    )

    def after(value, *others):
        return lax.optimization_barrier((value, *others))[0]

    swapped = fetch(weight, sibling)
    other = fetch(after(activations, swapped, rounded), sibling)
    ahead, behind = (fetch(swapped, along(0, s)) for s in (1, -1))
    across = [fetch(ahead[: rows // 2], along(0, 1)), fetch(behind[rows // 2 :], along(0, -1))]

    new_momentum = call(
        residual_kernel,
        shape(momentum.shape, F32),
        (momentum, gradient, exact, back_rows3, back_hi, back_lo),
    )

    def join(value, source):
        return value.astype(F32) + fetch(value, source).astype(F32)

    sent = join(after(rounded, swapped), far_z).astype(BF16)
    second_sum = join(after(sent, ahead, behind, other, new_momentum), pair_x).astype(BF16)
    total = join(second_sum, along_x(2))

    early = after(jnp.concatenate([swapped, ahead], axis=0), second_sum)
    late = jnp.concatenate([*across, behind], axis=0)
    next_early, last_early = fetch(early, along(1, 1)), fetch(early, along(1, -1))
    def gather(value):
        return jnp.concatenate([value] + [fetch(value, along(0, s)) for s in (1, 2, -1)], axis=0)

    band_line = gather(after(total.astype(BF16), late))
    late = after(late, band_line)
    next_late, last_late = fetch(late, along(1, 1)), fetch(late, along(1, -1))
    band_line = fetch(band_line, sibling)
    direction = call(
        direction_kernel,
        shape((rows, width), F32),
        (total, back_rows3, back_hi, back_lo),
    )
    blocks = gather(after(band_line, next_early, last_early, direction)).reshape(4, 4, BAND, narrow)
    far_early = fetch(after(next_early, blocks), along(1, 1))
    lines = [[early, late], [next_early, next_late], [far_early, fetch(last_late, along(1, -1))], [last_early, last_late]]
    bands = [blocks[:, g].reshape(4 * BAND, narrow) for g in range(4)]

    block = shape((tokens, 4 * rows), BF16)
    held = pltpu.VMEM(activations.shape, BF16)
    rows_like = pltpu.VMEM((4 * rows, width), BF16)

    def forward(order, more=()):
        parts, load = [len(lines[g]) for g in order], not more
        count = len(order)
        return call(
            lambda *refs: forward_kernel(parts, load, len(more), *refs),
            (*[block] * (2 * count), *([held] * 2 if load else []), *[rows_like] * len(more)),
            [first[None], back_rows, back_hi] + [bands[g] for g in (*order, *more)],
            (
                pltpu.VMEM((count, 4, rows, width), BF16),
                rows_like,
                rows_like,
                pltpu.SemaphoreType.DMA((count, 4)),
                *([pltpu.SemaphoreType.DMA((4,))] if load else []),
            ),
            limit=32,
            flops=count * 2 * 2 * tokens * 4 * rows * width,
            smem=1,
            resident=() if load else (own, other),
            kept=([activations, other] if load else []) + [line for g in order for line in lines[g]],
        )

    *results, own, other = forward([0])
    *more, step = forward([3, 1], [2])
    results += more
    results += call(
        lambda *refs: last_kernel(len(lines[2]), *refs),
        (block, block),
        [first[None]],
        (
            pltpu.VMEM((1, 4, rows, width), BF16),
            rows_like,
            pltpu.SemaphoreType.DMA((1, 4)),
        ),
        limit=24,
        flops=2 * 2 * tokens * 4 * rows * width,
        smem=1,
        kept=lines[2],
        resident=(own, other, step),
    )
    mine, theirs = [None] * 4, [None] * 4
    for n, g in enumerate((0, 3, 1, 2)):
        mine[g] = results[2 * n]
        theirs[g] = fetch(results[2 * n + 1], sibling)
    where = jnp.stack([core.astype(jnp.int32), second, first])
    projected = call(
        weave_kernel,
        shape((tokens, 32 * rows), BF16),
        (where, *mine, *theirs),
        (pltpu.VMEM((2, 4, tokens, 4 * rows), BF16),),
        smem=1,
    )
    return (new_momentum, direction, projected)


def solution(mesh):
    return jax.shard_map(
        on_device,
        mesh=mesh,
        in_specs=(
            P("rep", "fsdp", None),
            P("rep", "fsdp", None),
            P("fsdp", None),
            P(("rep", "fsdp"), None),
        ),
        out_specs=(P("rep", "fsdp", None), P("fsdp", None), P(("rep", "fsdp"), None)),
        check_vma=False,
    )
```

```python
import math

import jax
import jax.numpy as jnp
import numpy as np
from jax import lax
from jax.experimental import pallas as pl
from jax.experimental.pallas import tpu as pltpu
from jax.sharding import PartitionSpec as P

TILE = 64
BAND = 16
WIDE = 8
AXES = ("rep", "fsdp")

momentum_decay = 0.9
step_rate = 0.02
soft_width = 0.25

F32 = jnp.float32
BF16 = jnp.bfloat16
NT = (((1,), (1,)), ((), ()))


def cosine_rows():
    freq = np.arange(BAND, dtype=np.float64)[:, None]
    place = np.arange(TILE, dtype=np.float64)[None, :]
    factor = np.where(freq == 0.0, math.sqrt(1.0 / TILE), math.sqrt(2.0 / TILE))
    return factor * np.cos(math.pi * (2.0 * place + 1.0) * freq / (2.0 * TILE))


def halves(array):
    high = np.asarray(array, np.float32).astype(jnp.bfloat16)
    low = (np.asarray(array, np.float64) - high.astype(np.float64)).astype(jnp.bfloat16)
    return high, low


def split(value):
    high = value.astype(BF16)
    return high, (value - high.astype(F32)).astype(BF16)


def dot(a, b):
    return jnp.dot(a, b, preferred_element_type=F32)


def spot(index):
    rep, rest = divmod(index, 32)
    high, x = divmod(rep, 4)
    y, rest = divmod(rest, 8)
    low, core = divmod(rest, 2)
    return x, y, high * 4 + low, core


def place(x, y, z, core):
    x, y, z = x % 4, y % 4, z % 8
    return ((z // 4) * 4 + x) * 32 + y * 8 + (z % 4) * 2 + core


def fetch(value, source):
    return lax.ppermute(value, AXES, [(place(*source(*spot(i))), i) for i in range(256)])


def along(axis, step):
    def source(x, y, z, core):
        if (core + axis) % 2 == 0:
            return x, y + step, z, core
        if step == 2 and z % 2:
            return x, y, z - 2, core
        return x, y, z + step, core

    return source


def along_x(step):
    return lambda x, y, z, core: (x + step, y, z, core)


def pair_x(x, y, z, core):
    return x ^ 1, y, z, core


def far_z(x, y, z, core):
    return x, y, z + 4, core


def sibling(x, y, z, core):
    return x, y, z, 1 - core


def call(kernel, out_shape, inputs, scratch=(), limit=16, flops=0, smem=0, kept=(), resident=()):
    specs = [pl.BlockSpec(memory_space=pltpu.SMEM)] * smem
    specs += [pl.BlockSpec(memory_space=pltpu.VMEM)] * (len(inputs) - smem + len(resident))
    specs += [pl.BlockSpec(memory_space=pltpu.HBM)] * len(kept)
    resident = [pltpu.with_memory_space_constraint(v, pltpu.VMEM) for v in resident]
    kept = [pltpu.with_memory_space_constraint(v, pltpu.HBM) for v in kept]
    inputs = (*inputs, *resident, *kept)
    moved = sum(math.prod(v.shape) * v.dtype.itemsize for v in inputs)
    return pl.pallas_call(
        kernel,
        out_shape=out_shape,
        in_specs=specs,
        out_specs=jax.tree.map(
            lambda _: pl.BlockSpec(memory_space=pltpu.VMEM),
            out_shape,
            is_leaf=lambda v: not isinstance(v, tuple),
        ),
        scratch_shapes=list(scratch),
        compiler_params=pltpu.CompilerParams(vmem_limit_bytes=limit << 20),
        cost_estimate=pl.CostEstimate(flops=flops, bytes_accessed=moved, transcendentals=0),
    )(*inputs)


def stacked(value, wide):
    return jnp.concatenate(
        [value[:, k * wide : (k + 1) * wide] for k in range(value.shape[1] // wide)], axis=0
    )


def mixed_of(momentum, gradient):
    return momentum_decay * momentum[0] + gradient[0].astype(F32)


def bands_kernel(momentum, gradient, cols, rows3, exact, rounded, m, g, c, r, sems):
    wide = WIDE * TILE
    steps = momentum.shape[2] // wide
    copies = [pltpu.make_async_copy(cols, c, sems.at[2 * steps])]
    copies += [pltpu.make_async_copy(rows3, r, sems.at[2 * steps + 1])]
    for k in range(steps):
        cut = pl.ds(k * wide, wide)
        copies += [
            pltpu.make_async_copy(momentum.at[0, :, cut], m.at[k], sems.at[2 * k]),
            pltpu.make_async_copy(gradient.at[0, :, cut], g.at[k], sems.at[2 * k + 1]),
        ]
    for copy in copies:
        copy.start()
    copies[0].wait()
    narrow = []
    for k in range(steps):
        copies[2 * k + 2].wait()
        copies[2 * k + 3].wait()
        high, low = split(momentum_decay * m[k] + g[k].astype(F32))
        narrow.append(dot(high, c[:wide]) + dot(low, c[:wide]) + dot(high, c[wide:]))
    copies[1].wait()
    high, low = split(jnp.concatenate(narrow, axis=1))
    bands = dot(r[...], jnp.concatenate([high, low, high], axis=0))
    exact[...] = bands
    rounded[...] = bands.astype(BF16)


def restored(bands, back_rows3, back_hi, back_lo):
    high, low = split(bands)
    tall = dot(back_rows3[...], jnp.concatenate([high, low, high], axis=0))
    high, low = split(stacked(tall, WIDE * BAND))
    return dot(high, back_hi[...]) + dot(low, back_hi[...]) + dot(high, back_lo[...])


def residual_kernel(momentum, gradient, bands, back_rows3, back_hi, back_lo, out):
    mixed = mixed_of(momentum, gradient)
    low = restored(bands[...], back_rows3, back_hi, back_lo)
    wide = WIDE * TILE
    for k in range(mixed.shape[1] // wide):
        cut = slice(k * wide, (k + 1) * wide)
        out[0, :, cut] = mixed[:, cut] - low[k * TILE : (k + 1) * TILE]


def soft_sign(update):
    return update * lax.rsqrt(update * update + soft_width)


def update_kernel(total, weight, back_rows3, back_hi, back_lo, direction, new_weight):
    sign = soft_sign(restored(total[...], back_rows3, back_hi, back_lo))
    wide = WIDE * TILE
    for k in range(direction.shape[1] // wide):
        cut = slice(k * wide, (k + 1) * wide)
        part = sign[k * TILE : (k + 1) * TILE]
        direction[:, cut] = part
        new_weight[:, cut] = (weight[:, cut].astype(F32) - step_rate * part).astype(BF16)


def forward_kernel(pieces, load, first, *refs):
    groups = len(pieces)
    refs = list(refs)
    sources = [refs.pop(0) for _ in range(2)]
    weights = [refs.pop(0) for _ in range(1 + max(n for group in pieces for n, _ in group))]
    outs = [refs.pop(0) for _ in range(2 * groups)]
    tokens = [refs.pop(0) for _ in range(2)] if load else sources
    fresh = [refs.pop(0) for _ in range(groups)]
    sems, token_sems = refs
    rows = fresh[0].shape[0]
    per = tokens[0].shape[0] // rows
    copies = []
    for g, group in enumerate(pieces):
        for f, (n, row) in enumerate(group):
            at = pl.ds(pl.multiple_of(lax.rem(first[0] + f, 4) * TILE, TILE), TILE)
            copies.append(
                pltpu.make_async_copy(weights[n].at[pl.ds(row, TILE)], fresh[g].at[at], sems.at[g, f])
            )
    token_copies = []
    if load:
        for t in range(2 * per):
            cut = pl.ds(t % per * rows, rows)
            token_copies.append(
                pltpu.make_async_copy(sources[t // per].at[cut], tokens[t // per].at[cut], token_sems.at[t])
            )
    for copy in copies[:4] + token_copies + copies[4:]:
        copy.start()
    for g in range(groups):
        for f in range(4):
            copies[4 * g + f].wait()
        for t in range(2 * per):
            if g == 0 and load:
                token_copies[t].wait()
            cut = slice(t % per * rows, (t % per + 1) * rows)
            product = lax.dot_general(tokens[t // per][cut], fresh[g][...], NT, preferred_element_type=F32)
            outs[2 * g + t // per][cut] = product.astype(BF16)


def weave_kernel(where, *refs):
    mine, theirs, out, held = refs[:4], refs[4:8], refs[8], refs[9]
    core, my_start, their_start = where[0], where[1], where[2]
    for g in range(4):
        held[core, lax.rem(my_start + g, 4)] = mine[g][...]
        held[1 - core, lax.rem(their_start + g, 4)] = theirs[g][...]
    for y in range(4):
        for z in range(4):
            left = held[0, z, :, y * TILE : (y + 1) * TILE]
            right = held[1, y, :, z * TILE : (z + 1) * TILE]
            j = (y * 4 + z) * 2 * TILE
            out[:, j : j + 2 * TILE] = jnp.concatenate([left, right], axis=1)


def on_device(momentum, gradient, weight, activations):
    cosines = cosine_rows()
    high, low = halves(cosines)
    eye = np.eye(WIDE)
    cols_hi, cols_lo = (np.kron(eye, np.asarray(h, np.float32).T).astype(jnp.bfloat16) for h in (high, low))
    rows3 = np.concatenate([high, high, low], axis=1)
    back_rows3 = np.concatenate([high.T, high.T, low.T], axis=1)
    back_hi, back_lo = cols_hi.T, cols_lo.T
    back_rows = high.T
    width = weight.shape[1]
    narrow = width // TILE * BAND
    rows = weight.shape[0]
    tokens = activations.shape[0]

    core = lax.axis_index("fsdp") % 2
    y = lax.axis_index("fsdp") // 8
    z = lax.axis_index("fsdp") // 2 % 4
    first = jnp.where(core == 0, y, z).astype(jnp.int32)
    second = jnp.where(core == 0, z, y).astype(jnp.int32)

    shape = jax.ShapeDtypeStruct
    steps = width // (WIDE * TILE)
    exact, rounded = call(
        bands_kernel,
        (shape((BAND, narrow), F32), shape((BAND, narrow), BF16)),
        (),
        (
            pltpu.VMEM((steps, rows, WIDE * TILE), F32),
            pltpu.VMEM((steps, rows, WIDE * TILE), BF16),
            pltpu.VMEM((2 * WIDE * TILE, WIDE * BAND), BF16),
            pltpu.VMEM(rows3.shape, BF16),
            pltpu.SemaphoreType.DMA((2 * steps + 2,)),
        ),
        kept=(momentum, gradient, np.concatenate([cols_hi, cols_lo], axis=0), rows3),
    )

    def after(value, *others):
        return lax.optimization_barrier((value, *others))[0]

    other = fetch(after(activations, rounded), sibling)

    parts = [rounded.astype(F32)] + [fetch(rounded, along_x(n)).astype(F32) for n in (1, 2, -1)]
    sent = ((parts[0] + parts[2]) + (parts[1] + parts[3])).astype(BF16)
    new_momentum = call(
        residual_kernel,
        shape(momentum.shape, F32),
        (momentum, gradient, exact, back_rows3, back_hi, back_lo),
    )
    total = sent.astype(F32) + fetch(sent, far_z).astype(F32)
    direction, own = call(
        update_kernel,
        (shape((rows, width), F32), shape((rows, width), BF16)),
        (after(total, new_momentum, other), weight, back_rows3, back_hi, back_lo),
    )

    ahead, behind = (fetch(own, along(0, n)) for n in (1, -1))
    next_own, last_own = (fetch(own, along(1, n)) for n in (1, -1))
    across = fetch(ahead, along(0, 1))
    pair = jnp.concatenate([ahead, behind], axis=0)
    next_pair, last_pair = (fetch(pair, along(1, n)) for n in (1, -1))
    next_across, last_across = (fetch(across, along(1, n)) for n in (1, -1))
    far_pair = fetch(next_pair, along(1, 1))
    far_rest = fetch(jnp.concatenate([last_own, last_across], axis=0), along(1, -1))
    lines = [
        [(own, 0), (ahead, 0), (across, 0), (behind, 0)],
        [(next_own, 0), (next_pair, 0), (next_across, 0), (next_pair, TILE)],
        [(far_rest, 0), (far_pair, 0), (far_rest, TILE), (far_pair, TILE)],
        [(last_own, 0), (last_pair, 0), (last_across, 0), (last_pair, TILE)],
    ]

    block = shape((tokens, 4 * rows), BF16)

    def forward(order, load):
        used, pieces = [], []
        for g in order:
            pieces.append([])
            for value, row in lines[g]:
                found = [n for n, v in enumerate(used) if v is value]
                if not found:
                    used.append(value)
                pieces[-1].append((found[0] if found else len(used) - 1, row))
        count = len(order)
        held = pltpu.VMEM(activations.shape, BF16)
        return call(
            lambda *refs: forward_kernel(pieces, load, *refs),
            (*[block] * (2 * count), *([held] * 2 if load else [])),
            [first[None]],
            (
                *[pltpu.VMEM((4 * rows, width), BF16)] * count,
                pltpu.SemaphoreType.DMA((count, 4)),
                pltpu.SemaphoreType.DMA((4,)),
            ),
            limit=24,
            flops=count * 2 * 2 * tokens * 4 * rows * width,
            smem=1,
            resident=() if load else (activations_in, other_in),
            kept=([activations, other] if load else []) + used,
        )

    *results, activations_in, other_in = forward([0], True)
    results += forward([3, 1], False)
    results += forward([2], False)
    mine, theirs = [None] * 4, [None] * 4
    for n, g in enumerate((0, 3, 1, 2)):
        mine[g] = results[2 * n]
        theirs[g] = fetch(results[2 * n + 1], sibling)
    where = jnp.stack([core.astype(jnp.int32), second, first])
    projected = call(
        weave_kernel,
        shape((tokens, 32 * rows), BF16),
        (where, *mine, *theirs),
        (pltpu.VMEM((2, 4, tokens, 4 * rows), BF16),),
        smem=1,
    )
    return (new_momentum, direction, projected)


def solution(mesh):
    return jax.shard_map(
        on_device,
        mesh=mesh,
        in_specs=(
            P("rep", "fsdp", None),
            P("rep", "fsdp", None),
            P("fsdp", None),
            P(("rep", "fsdp"), None),
        ),
        out_specs=(P("rep", "fsdp", None), P("fsdp", None), P(("rep", "fsdp"), None)),
        check_vma=False,
    )
```

```python
import math

import jax
import jax.numpy as jnp
import numpy as np
from jax import lax
from jax.experimental import pallas as pl
from jax.experimental.pallas import tpu as pltpu
from jax.sharding import PartitionSpec as P

TILE = 64
BAND = 16
WIDE = 8
AXES = ("rep", "fsdp")

momentum_decay = 0.9
step_rate = 0.02
soft_width = 0.25

F32 = jnp.float32
BF16 = jnp.bfloat16
NT = (((1,), (1,)), ((), ()))


def cosine_rows():
    freq = np.arange(BAND, dtype=np.float64)[:, None]
    place = np.arange(TILE, dtype=np.float64)[None, :]
    factor = np.where(freq == 0.0, math.sqrt(1.0 / TILE), math.sqrt(2.0 / TILE))
    return factor * np.cos(math.pi * (2.0 * place + 1.0) * freq / (2.0 * TILE))


def halves(array):
    high = np.asarray(array, np.float32).astype(jnp.bfloat16)
    low = (np.asarray(array, np.float64) - high.astype(np.float64)).astype(jnp.bfloat16)
    return high, low


def split(value):
    high = value.astype(BF16)
    return high, (value - high.astype(F32)).astype(BF16)


def dot(a, b):
    return jnp.dot(a, b, preferred_element_type=F32)


def spot(index):
    rep, rest = divmod(index, 32)
    high, x = divmod(rep, 4)
    y, rest = divmod(rest, 8)
    low, core = divmod(rest, 2)
    return x, y, high * 4 + low, core


def place(x, y, z, core):
    x, y, z = x % 4, y % 4, z % 8
    return ((z // 4) * 4 + x) * 32 + y * 8 + (z % 4) * 2 + core


def fetch(value, source):
    return lax.ppermute(value, AXES, [(place(*source(*spot(i))), i) for i in range(256)])


def along(axis, step):
    def source(x, y, z, core):
        if (core + axis) % 2 == 0:
            return x, y + step, z, core
        if step == 2 and z % 2:
            return x, y, z - 2, core
        return x, y, z + step, core

    return source


def along_x(step):
    return lambda x, y, z, core: (x + step, y, z, core)


def pair_x(x, y, z, core):
    return x ^ 1, y, z, core


def far_z(x, y, z, core):
    return x, y, z + 4, core


def sibling(x, y, z, core):
    return x, y, z, 1 - core


def call(kernel, out_shape, inputs, scratch=(), limit=16, flops=0, smem=0, kept=(), resident=(), anywhere=()):
    specs = [pl.BlockSpec(memory_space=pltpu.SMEM)] * smem
    specs += [pl.BlockSpec(memory_space=pltpu.VMEM)] * (len(inputs) - smem + len(resident))
    specs += [pl.BlockSpec(memory_space=pltpu.HBM)] * len(kept)
    specs += [pl.BlockSpec(memory_space=pl.ANY)] * len(anywhere)
    resident = [pltpu.with_memory_space_constraint(v, pltpu.VMEM) for v in resident]
    kept = [pltpu.with_memory_space_constraint(v, pltpu.HBM) for v in kept]
    inputs = (*inputs, *resident, *kept, *anywhere)
    moved = sum(math.prod(v.shape) * v.dtype.itemsize for v in inputs)
    return pl.pallas_call(
        kernel,
        out_shape=out_shape,
        in_specs=specs,
        out_specs=jax.tree.map(
            lambda _: pl.BlockSpec(memory_space=pltpu.VMEM),
            out_shape,
            is_leaf=lambda v: not isinstance(v, tuple),
        ),
        scratch_shapes=list(scratch),
        compiler_params=pltpu.CompilerParams(vmem_limit_bytes=limit << 20),
        cost_estimate=pl.CostEstimate(flops=flops, bytes_accessed=moved, transcendentals=0),
    )(*inputs)


def stacked(value, wide):
    return jnp.concatenate(
        [value[:, k * wide : (k + 1) * wide] for k in range(value.shape[1] // wide)], axis=0
    )


def mixed_of(momentum, gradient):
    return momentum_decay * momentum[0] + gradient[0].astype(F32)


def bands_kernel(
    momentum, gradient, cols_in, rows3, back_rows3, weight_in, exact, rounded, mixed, cols, back, weight, g, r, sems
):
    wide = WIDE * TILE
    steps = momentum.shape[2] // wide
    copies = [
        pltpu.make_async_copy(cols_in, cols, sems.at[2 * steps]),
        pltpu.make_async_copy(rows3, r, sems.at[2 * steps + 1]),
    ]
    for k in range(steps):
        cut = pl.ds(k * wide, wide)
        copies += [
            pltpu.make_async_copy(momentum.at[0, :, cut], mixed.at[k], sems.at[2 * k]),
            pltpu.make_async_copy(gradient.at[0, :, cut], g.at[k], sems.at[2 * k + 1]),
        ]
    copies += [
        pltpu.make_async_copy(back_rows3, back, sems.at[2 * steps + 2]),
        pltpu.make_async_copy(weight_in, weight, sems.at[2 * steps + 3]),
    ]
    for copy in copies:
        copy.start()
    copies[0].wait()
    narrow = []
    for k in range(steps):
        copies[2 * k + 2].wait()
        copies[2 * k + 3].wait()
        value = momentum_decay * mixed[k] + g[k].astype(F32)
        mixed[k] = value
        high, low = split(value)
        narrow.append(dot(high, cols[:wide]) + dot(low, cols[:wide]) + dot(high, cols[wide:]))
    copies[1].wait()
    high, low = split(jnp.concatenate(narrow, axis=1))
    bands = dot(r[...], jnp.concatenate([high, low, high], axis=0))
    exact[...] = bands
    rounded[...] = bands.astype(BF16)
    for copy in copies[-2:]:
        copy.wait()


def restored(bands, back, cols):
    wide = WIDE * TILE
    high, low = split(bands)
    tall = dot(back[...], jnp.concatenate([high, low, high], axis=0))
    high, low = split(stacked(tall, WIDE * BAND))

    def spread(a, b):
        return lax.dot_general(a, b, NT, preferred_element_type=F32)

    return spread(high, cols[:wide]) + spread(low, cols[:wide]) + spread(high, cols[wide:])


def residual_kernel(bands, mixed, cols, back, out):
    low = restored(bands[...], back, cols)
    wide = WIDE * TILE
    for k in range(mixed.shape[0]):
        out[0, :, k * wide : (k + 1) * wide] = mixed[k] - low[k * TILE : (k + 1) * TILE]


def soft_sign(update):
    return update * lax.rsqrt(update * update + soft_width)


def update_kernel(total, cols, back, weight, direction, new_weight):
    sign = soft_sign(restored(total[...], back, cols))
    wide = WIDE * TILE
    for k in range(direction.shape[1] // wide):
        cut = slice(k * wide, (k + 1) * wide)
        part = sign[k * TILE : (k + 1) * TILE]
        direction[:, cut] = part
        new_weight[:, cut] = (weight[:, cut].astype(F32) - step_rate * part).astype(BF16)


def forward_kernel(pieces, load, first, *refs):
    groups = len(pieces)
    refs = list(refs)
    sources = [refs.pop(0) for _ in range(2)]
    weights = [refs.pop(0) for _ in range(1 + max(n for group in pieces for n, _ in group))]
    outs = [refs.pop(0) for _ in range(2 * groups)]
    tokens = [refs.pop(0) for _ in range(2)] if load else sources
    fresh = [refs.pop(0) for _ in range(groups)]
    sems, token_sems = refs
    rows = fresh[0].shape[0]
    per = tokens[0].shape[0] // rows
    copies = []
    for g, group in enumerate(pieces):
        for f, (n, row) in enumerate(group):
            at = pl.ds(pl.multiple_of(lax.rem(first[0] + f, 4) * TILE, TILE), TILE)
            copies.append(
                pltpu.make_async_copy(weights[n].at[pl.ds(row, TILE)], fresh[g].at[at], sems.at[g, f])
            )
    token_copies = []
    if load:
        for t in range(2 * per):
            cut = pl.ds(t % per * rows, rows)
            token_copies.append(
                pltpu.make_async_copy(sources[t // per].at[cut], tokens[t // per].at[cut], token_sems.at[t])
            )
    for copy in copies[:4] + token_copies + copies[4:]:
        copy.start()
    for g in range(groups):
        for f in range(4):
            copies[4 * g + f].wait()
        for t in range(2 * per):
            if g == 0 and load:
                token_copies[t].wait()
            cut = slice(t % per * rows, (t % per + 1) * rows)
            product = lax.dot_general(tokens[t // per][cut], fresh[g][...], NT, preferred_element_type=F32)
            outs[2 * g + t // per][cut] = product.astype(BF16)


def weave_kernel(where, *refs):
    mine, theirs, out, held = refs[:4], refs[4:8], refs[8], refs[9]
    core, my_start, their_start = where[0], where[1], where[2]
    for g in range(4):
        held[core, lax.rem(my_start + g, 4)] = mine[g][...]
        held[1 - core, lax.rem(their_start + g, 4)] = theirs[g][...]
    for y in range(4):
        for z in range(4):
            left = held[0, z, :, y * TILE : (y + 1) * TILE]
            right = held[1, y, :, z * TILE : (z + 1) * TILE]
            j = (y * 4 + z) * 2 * TILE
            out[:, j : j + 2 * TILE] = jnp.concatenate([left, right], axis=1)


def on_device(momentum, gradient, weight, activations):
    cosines = cosine_rows()
    high, low = halves(cosines)
    eye = np.eye(WIDE)
    cols_hi, cols_lo = (np.kron(eye, np.asarray(h, np.float32).T).astype(jnp.bfloat16) for h in (high, low))
    rows3 = np.concatenate([high, high, low], axis=1)
    back_rows3 = np.concatenate([high.T, high.T, low.T], axis=1)
    width = weight.shape[1]
    narrow = width // TILE * BAND
    rows = weight.shape[0]
    tokens = activations.shape[0]

    core = lax.axis_index("fsdp") % 2
    y = lax.axis_index("fsdp") // 8
    z = lax.axis_index("fsdp") // 2 % 4
    first = jnp.where(core == 0, y, z).astype(jnp.int32)
    second = jnp.where(core == 0, z, y).astype(jnp.int32)

    shape = jax.ShapeDtypeStruct
    steps = width // (WIDE * TILE)
    cols_in = np.concatenate([cols_hi, cols_lo], axis=0)
    exact, rounded, mixed, cols, back, held_weight = call(
        bands_kernel,
        (
            shape((BAND, narrow), F32),
            shape((BAND, narrow), BF16),
            pltpu.VMEM((steps, rows, WIDE * TILE), F32),
            pltpu.VMEM(cols_in.shape, BF16),
            pltpu.VMEM(back_rows3.shape, BF16),
            pltpu.VMEM(weight.shape, BF16),
        ),
        (),
        (
            pltpu.VMEM((steps, rows, WIDE * TILE), BF16),
            pltpu.VMEM(rows3.shape, BF16),
            pltpu.SemaphoreType.DMA((2 * steps + 4,)),
        ),
        kept=(momentum, gradient, cols_in, rows3, back_rows3, weight),
    )

    def after(value, *others):
        return lax.optimization_barrier((value, *others))[0]

    other = fetch(after(activations, rounded), sibling)

    parts = [rounded.astype(F32)] + [fetch(rounded, along_x(n)).astype(F32) for n in (1, 2, -1)]
    sent = ((parts[0] + parts[2]) + (parts[1] + parts[3])).astype(BF16)
    total = sent.astype(F32) + fetch(sent, far_z).astype(F32)
    direction, own = call(
        update_kernel,
        (shape((rows, width), F32), shape((rows, width), BF16)),
        (after(total, other),),
        resident=(cols, back, held_weight),
    )
    new_momentum = call(
        residual_kernel,
        shape(momentum.shape, F32),
        (after(exact, own),),
        resident=(mixed, cols, back),
    )

    ahead, behind = (fetch(own, along(0, n)) for n in (1, -1))
    next_own, last_own = (fetch(own, along(1, n)) for n in (1, -1))
    pair = after(jnp.concatenate([ahead, behind], axis=0), next_own, last_own, new_momentum)
    across = fetch(ahead, along(0, 1))
    next_pair, last_pair = (fetch(pair, along(1, n)) for n in (1, -1))
    far_own = fetch(last_own, along(1, -1))
    next_across, last_across = (fetch(across, along(1, n)) for n in (1, -1))
    far_pair = fetch(after(next_pair, across, far_own), along(1, 1))
    far_across = fetch(last_across, along(1, -1))
    lines = [
        [(own, 0), (ahead, 0), (across, 0), (behind, 0)],
        [(next_own, 0), (next_pair, 0), (next_across, 0), (next_pair, TILE)],
        [(far_own, 0), (far_pair, 0), (far_across, 0), (far_pair, TILE)],
        [(last_own, 0), (last_pair, 0), (last_across, 0), (last_pair, TILE)],
    ]

    block = shape((tokens, 4 * rows), BF16)

    def forward(order, load):
        used, pieces = [], []
        for g in order:
            pieces.append([])
            for value, row in lines[g]:
                found = [n for n, v in enumerate(used) if v is value]
                if not found:
                    used.append(value)
                pieces[-1].append((found[0] if found else len(used) - 1, row))
        count = len(order)
        held = pltpu.VMEM(activations.shape, BF16)
        return call(
            lambda *refs: forward_kernel(pieces, load, *refs),
            (*[block] * (2 * count), *([held] * 2 if load else [])),
            [first[None]],
            (
                *[pltpu.VMEM((4 * rows, width), BF16)] * count,
                pltpu.SemaphoreType.DMA((count, 4)),
                pltpu.SemaphoreType.DMA((4,)),
            ),
            limit=24,
            flops=count * 2 * 2 * tokens * 4 * rows * width,
            smem=1,
            resident=() if load else (activations_in, other_in),
            kept=[activations, other] if load else [],
            anywhere=used,
        )

    *results, activations_in, other_in = forward([0], True)
    results += forward([3, 1], False)
    results += forward([2], False)
    mine, theirs = [None] * 4, [None] * 4
    for n, g in enumerate((0, 3, 1, 2)):
        mine[g] = results[2 * n]
        theirs[g] = fetch(results[2 * n + 1], sibling)
    where = jnp.stack([core.astype(jnp.int32), second, first])
    projected = call(
        weave_kernel,
        shape((tokens, 32 * rows), BF16),
        (where, *mine, *theirs),
        (pltpu.VMEM((2, 4, tokens, 4 * rows), BF16),),
        smem=1,
    )
    return (new_momentum, direction, projected)


def solution(mesh):
    return jax.shard_map(
        on_device,
        mesh=mesh,
        in_specs=(
            P("rep", "fsdp", None),
            P("rep", "fsdp", None),
            P("fsdp", None),
            P(("rep", "fsdp"), None),
        ),
        out_specs=(P("rep", "fsdp", None), P("fsdp", None), P(("rep", "fsdp"), None)),
        check_vma=False,
    )
```

```python
import math

import jax
import jax.numpy as jnp
import numpy as np
from jax import lax
from jax.experimental import pallas as pl
from jax.experimental.pallas import tpu as pltpu
from jax.sharding import PartitionSpec as P

TILE = 64
BAND = 16
WIDE = 8
AXES = ("rep", "fsdp")

momentum_decay = 0.9
step_rate = 0.02
soft_width = 0.25

F32 = jnp.float32
BF16 = jnp.bfloat16
NT = (((1,), (1,)), ((), ()))


def cosine_rows():
    freq = np.arange(BAND, dtype=np.float64)[:, None]
    place = np.arange(TILE, dtype=np.float64)[None, :]
    factor = np.where(freq == 0.0, math.sqrt(1.0 / TILE), math.sqrt(2.0 / TILE))
    return factor * np.cos(math.pi * (2.0 * place + 1.0) * freq / (2.0 * TILE))


def halves(array):
    high = np.asarray(array, np.float32).astype(jnp.bfloat16)
    low = (np.asarray(array, np.float64) - high.astype(np.float64)).astype(jnp.bfloat16)
    return high, low


def split(value):
    high = value.astype(BF16)
    return high, (value - high.astype(F32)).astype(BF16)


def dot(a, b):
    return jnp.dot(a, b, preferred_element_type=F32)


def spot(index):
    rep, rest = divmod(index, 32)
    high, x = divmod(rep, 4)
    y, rest = divmod(rest, 8)
    low, core = divmod(rest, 2)
    return x, y, high * 4 + low, core


def place(x, y, z, core):
    x, y, z = x % 4, y % 4, z % 8
    return ((z // 4) * 4 + x) * 32 + y * 8 + (z % 4) * 2 + core


def fetch(value, source):
    return lax.ppermute(value, AXES, [(place(*source(*spot(i))), i) for i in range(256)])


def along(axis, step):
    def source(x, y, z, core):
        if (core + axis) % 2 == 0:
            return x, y + step, z, core
        if step == 2 and z % 2:
            return x, y, z - 2, core
        return x, y, z + step, core

    return source


def along_x(step):
    return lambda x, y, z, core: (x + step, y, z, core)


def pair_x(x, y, z, core):
    return x ^ 1, y, z, core


def far_z(x, y, z, core):
    return x, y, z + 4, core


def sibling(x, y, z, core):
    return x, y, z, 1 - core


def call(kernel, out_shape, inputs, scratch=(), limit=16, flops=0, smem=0, kept=(), resident=(), anywhere=()):
    specs = [pl.BlockSpec(memory_space=pltpu.SMEM)] * smem
    specs += [pl.BlockSpec(memory_space=pltpu.VMEM)] * (len(inputs) - smem + len(resident))
    specs += [pl.BlockSpec(memory_space=pltpu.HBM)] * len(kept)
    specs += [pl.BlockSpec(memory_space=pl.ANY)] * len(anywhere)
    resident = [pltpu.with_memory_space_constraint(v, pltpu.VMEM) for v in resident]
    kept = [pltpu.with_memory_space_constraint(v, pltpu.HBM) for v in kept]
    inputs = (*inputs, *resident, *kept, *anywhere)
    moved = sum(math.prod(v.shape) * v.dtype.itemsize for v in inputs)
    return pl.pallas_call(
        kernel,
        out_shape=out_shape,
        in_specs=specs,
        out_specs=jax.tree.map(
            lambda _: pl.BlockSpec(memory_space=pltpu.VMEM),
            out_shape,
            is_leaf=lambda v: not isinstance(v, tuple),
        ),
        scratch_shapes=list(scratch),
        compiler_params=pltpu.CompilerParams(vmem_limit_bytes=limit << 20),
        cost_estimate=pl.CostEstimate(flops=flops, bytes_accessed=moved, transcendentals=0),
    )(*inputs)


def stacked(value, wide):
    return jnp.concatenate(
        [value[:, k * wide : (k + 1) * wide] for k in range(value.shape[1] // wide)], axis=0
    )


def mixed_of(momentum, gradient):
    return momentum_decay * momentum[0] + gradient[0].astype(F32)


def bands_kernel(
    momentum, gradient, cols_in, rows3, back_rows3, weight_in, exact, rounded, mixed, cols, back, weight, g, r, sems
):
    wide = WIDE * TILE
    steps = momentum.shape[2] // wide
    copies = [
        pltpu.make_async_copy(cols_in, cols, sems.at[2 * steps]),
        pltpu.make_async_copy(rows3, r, sems.at[2 * steps + 1]),
    ]
    for k in range(steps):
        cut = pl.ds(k * wide, wide)
        copies += [
            pltpu.make_async_copy(momentum.at[0, :, cut], mixed.at[k], sems.at[2 * k]),
            pltpu.make_async_copy(gradient.at[0, :, cut], g.at[k], sems.at[2 * k + 1]),
        ]
    copies += [
        pltpu.make_async_copy(back_rows3, back, sems.at[2 * steps + 2]),
        pltpu.make_async_copy(weight_in, weight, sems.at[2 * steps + 3]),
    ]
    for copy in copies:
        copy.start()
    copies[0].wait()
    narrow = []
    for k in range(steps):
        copies[2 * k + 2].wait()
        copies[2 * k + 3].wait()
        value = momentum_decay * mixed[k] + g[k].astype(F32)
        mixed[k] = value
        high, low = split(value)
        narrow.append(dot(high, cols[:wide]) + dot(low, cols[:wide]) + dot(high, cols[wide:]))
    copies[1].wait()
    high, low = split(jnp.concatenate(narrow, axis=1))
    bands = dot(r[...], jnp.concatenate([high, low, high], axis=0))
    exact[...] = bands
    rounded[...] = bands.astype(BF16)
    for copy in copies[-2:]:
        copy.wait()


def restored(bands, back, cols):
    wide = WIDE * TILE
    high, low = split(bands)
    tall = dot(back[...], jnp.concatenate([high, low, high], axis=0))
    high, low = split(stacked(tall, WIDE * BAND))

    def spread(a, b):
        return lax.dot_general(a, b, NT, preferred_element_type=F32)

    return spread(high, cols[:wide]) + spread(low, cols[:wide]) + spread(high, cols[wide:])


def residual_kernel(bands, mixed, cols, back, out):
    low = restored(bands[...], back, cols)
    wide = WIDE * TILE
    for k in range(mixed.shape[0]):
        out[0, :, k * wide : (k + 1) * wide] = mixed[k] - low[k * TILE : (k + 1) * TILE]


def soft_sign(update):
    return update * lax.rsqrt(update * update + soft_width)


def direction_kernel(total, cols, back, direction):
    sign = soft_sign(restored(total[...], back, cols))
    wide = WIDE * TILE
    for k in range(direction.shape[1] // wide):
        direction[:, k * wide : (k + 1) * wide] = sign[k * TILE : (k + 1) * TILE]


def renew_kernel(bands, ahead, behind, ahead_half, behind_half, cols, back, weight, top, bottom):
    wide = WIDE * TILE
    half = TILE // 2
    for f in range(4):
        band = bands[f * BAND : (f + 1) * BAND]
        tall = dot(back[:, BAND:], jnp.concatenate([band, band], axis=0)).astype(BF16)
        move = step_rate * soft_sign(
            lax.dot_general(stacked(tall, WIDE * BAND), cols[:wide], NT, preferred_element_type=F32)
        )
        out, at = (top, bottom)[f // 2], f % 2 * TILE
        raws = ([(weight, 0, TILE)], [(ahead, 0, TILE)], [(ahead_half, 0, half), (behind_half, half, half)])
        for raw, row, count in (*raws, [(behind, 0, TILE)])[f]:
            for k in range(weight.shape[1] // wide):
                cut = slice(k * wide, (k + 1) * wide)
                part = move[k * TILE + row : k * TILE + row + count]
                out[at + row : at + row + count, cut] = (raw[:, cut].astype(F32) - part).astype(BF16)


def forward_kernel(pieces, load, first, *refs):
    groups = len(pieces)
    refs = list(refs)
    sources = [refs.pop(0) for _ in range(2)]
    weights = [refs.pop(0) for _ in range(1 + max(n for group in pieces for n, _ in group))]
    outs = [refs.pop(0) for _ in range(2 * groups)]
    tokens = [refs.pop(0) for _ in range(2)] if load else sources
    fresh = [refs.pop(0) for _ in range(groups)]
    sems, token_sems = refs
    rows = fresh[0].shape[0]
    per = tokens[0].shape[0] // rows
    copies = []
    for g, group in enumerate(pieces):
        for f, (n, row) in enumerate(group):
            at = pl.ds(pl.multiple_of(lax.rem(first[0] + f, 4) * TILE, TILE), TILE)
            copies.append(
                pltpu.make_async_copy(weights[n].at[pl.ds(row, TILE)], fresh[g].at[at], sems.at[g, f])
            )
    token_copies = []
    if load:
        for t in range(2 * per):
            cut = pl.ds(t % per * rows, rows)
            token_copies.append(
                pltpu.make_async_copy(sources[t // per].at[cut], tokens[t // per].at[cut], token_sems.at[t])
            )
    for copy in copies[:4] + token_copies + copies[4:]:
        copy.start()
    for g in range(groups):
        for f in range(4):
            copies[4 * g + f].wait()
        for t in range(2 * per):
            if g == 0 and load:
                token_copies[t].wait()
            cut = slice(t % per * rows, (t % per + 1) * rows)
            product = lax.dot_general(tokens[t // per][cut], fresh[g][...], NT, preferred_element_type=F32)
            outs[2 * g + t // per][cut] = product.astype(BF16)


def weave_kernel(where, *refs):
    mine, theirs, out, held = refs[:4], refs[4:8], refs[8], refs[9]
    core, my_start, their_start = where[0], where[1], where[2]
    for g in range(4):
        held[core, lax.rem(my_start + g, 4)] = mine[g][...]
        held[1 - core, lax.rem(their_start + g, 4)] = theirs[g][...]
    for y in range(4):
        for z in range(4):
            left = held[0, z, :, y * TILE : (y + 1) * TILE]
            right = held[1, y, :, z * TILE : (z + 1) * TILE]
            j = (y * 4 + z) * 2 * TILE
            out[:, j : j + 2 * TILE] = jnp.concatenate([left, right], axis=1)


def on_device(momentum, gradient, weight, activations):
    cosines = cosine_rows()
    high, low = halves(cosines)
    eye = np.eye(WIDE)
    cols_hi, cols_lo = (np.kron(eye, np.asarray(h, np.float32).T).astype(jnp.bfloat16) for h in (high, low))
    rows3 = np.concatenate([high, high, low], axis=1)
    back_rows3 = np.concatenate([high.T, high.T, low.T], axis=1)
    width = weight.shape[1]
    narrow = width // TILE * BAND
    rows = weight.shape[0]
    tokens = activations.shape[0]

    core = lax.axis_index("fsdp") % 2
    y = lax.axis_index("fsdp") // 8
    z = lax.axis_index("fsdp") // 2 % 4
    first = jnp.where(core == 0, y, z).astype(jnp.int32)
    second = jnp.where(core == 0, z, y).astype(jnp.int32)

    shape = jax.ShapeDtypeStruct
    steps = width // (WIDE * TILE)
    cols_in = np.concatenate([cols_hi, cols_lo], axis=0)
    exact, rounded, mixed, cols, back, held_weight = call(
        bands_kernel,
        (
            shape((BAND, narrow), F32),
            shape((BAND, narrow), BF16),
            pltpu.VMEM((steps, rows, WIDE * TILE), F32),
            pltpu.VMEM(cols_in.shape, BF16),
            pltpu.VMEM(back_rows3.shape, BF16),
            pltpu.VMEM(weight.shape, BF16),
        ),
        (),
        (
            pltpu.VMEM((steps, rows, WIDE * TILE), BF16),
            pltpu.VMEM(rows3.shape, BF16),
            pltpu.SemaphoreType.DMA((2 * steps + 4,)),
        ),
        kept=(momentum, gradient, cols_in, rows3, back_rows3, weight),
    )

    def after(value, *others):
        return lax.optimization_barrier((value, *others))[0]

    ahead, behind = (fetch(after(weight, rounded), along(0, n)) for n in (1, -1))

    parts = [rounded.astype(F32)] + [fetch(rounded, along_x(n)).astype(F32) for n in (1, 2, -1)]
    sent = ((parts[0] + parts[2]) + (parts[1] + parts[3])).astype(BF16)
    total = sent.astype(F32) + fetch(after(sent, ahead, behind), far_z).astype(F32)
    halves_across = [fetch(ahead[: rows // 2], along(0, 1)), fetch(behind[rows // 2 :], along(0, -1))]

    sent = total.astype(BF16)
    line = jnp.concatenate([sent] + [fetch(sent, along(0, n)) for n in (1, 2, -1)], axis=0)
    direction = call(
        direction_kernel,
        shape((rows, width), F32),
        (total,),
        resident=(cols, back),
    )
    half_rows = shape((2 * rows, width), BF16)
    top, bottom = call(
        renew_kernel,
        (half_rows, half_rows),
        (line, ahead, behind, *halves_across),
        resident=(cols, back, held_weight),
    )
    other = fetch(after(activations, top), sibling)
    new_momentum = call(
        residual_kernel,
        shape(momentum.shape, F32),
        (after(exact, top),),
        resident=(mixed, cols, back),
    )

    next_top, last_bottom = fetch(top, along(1, 1)), fetch(bottom, along(1, -1))
    next_bottom, last_top = fetch(bottom, along(1, 1)), fetch(top, along(1, -1))
    far_top, far_bottom = fetch(next_top, along(1, 1)), fetch(last_bottom, along(1, -1))
    lines = [
        [(a, row) for a in pair for row in (0, TILE)]
        for pair in (
            (after(top, new_momentum, direction), bottom),
            (next_top, next_bottom),
            (far_top, far_bottom),
            (last_top, last_bottom),
        )
    ]

    block = shape((tokens, 4 * rows), BF16)

    def forward(order, load):
        used, pieces = [], []
        for g in order:
            pieces.append([])
            for value, row in lines[g]:
                found = [n for n, v in enumerate(used) if v is value]
                if not found:
                    used.append(value)
                pieces[-1].append((found[0] if found else len(used) - 1, row))
        count = len(order)
        held = pltpu.VMEM(activations.shape, BF16)
        return call(
            lambda *refs: forward_kernel(pieces, load, *refs),
            (*[block] * (2 * count), *([held] * 2 if load else [])),
            [first[None]],
            (
                *[pltpu.VMEM((4 * rows, width), BF16)] * count,
                pltpu.SemaphoreType.DMA((count, 4)),
                pltpu.SemaphoreType.DMA((4,)),
            ),
            limit=24,
            flops=count * 2 * 2 * tokens * 4 * rows * width,
            smem=1,
            resident=() if load else (activations_in, other_in),
            kept=[activations] if load else [],
            anywhere=([other] if load else []) + used,
        )

    *results, activations_in, other_in = forward([0], True)
    results += forward([3, 1], False)
    results += forward([2], False)
    mine, theirs = [None] * 4, [None] * 4
    for n, g in enumerate((0, 3, 1, 2)):
        mine[g] = results[2 * n]
        theirs[g] = fetch(results[2 * n + 1], sibling)
    where = jnp.stack([core.astype(jnp.int32), second, first])
    projected = call(
        weave_kernel,
        shape((tokens, 32 * rows), BF16),
        (where, *mine, *theirs),
        (pltpu.VMEM((2, 4, tokens, 4 * rows), BF16),),
        smem=1,
    )
    return (new_momentum, direction, projected)


def solution(mesh):
    return jax.shard_map(
        on_device,
        mesh=mesh,
        in_specs=(
            P("rep", "fsdp", None),
            P("rep", "fsdp", None),
            P("fsdp", None),
            P(("rep", "fsdp"), None),
        ),
        out_specs=(P("rep", "fsdp", None), P("fsdp", None), P(("rep", "fsdp"), None)),
        check_vma=False,
    )
```

```python
import math

import jax
import jax.numpy as jnp
import numpy as np
from jax import lax
from jax.experimental import pallas as pl
from jax.experimental.pallas import tpu as pltpu
from jax.sharding import PartitionSpec as P

TILE = 64
BAND = 16
WIDE = 8
AXES = ("rep", "fsdp")

momentum_decay = 0.9
step_rate = 0.02
soft_width = 0.25

F32 = jnp.float32
BF16 = jnp.bfloat16
NT = (((1,), (1,)), ((), ()))


def cosine_rows():
    freq = np.arange(BAND, dtype=np.float64)[:, None]
    place = np.arange(TILE, dtype=np.float64)[None, :]
    factor = np.where(freq == 0.0, math.sqrt(1.0 / TILE), math.sqrt(2.0 / TILE))
    return factor * np.cos(math.pi * (2.0 * place + 1.0) * freq / (2.0 * TILE))


def halves(array):
    high = np.asarray(array, np.float32).astype(jnp.bfloat16)
    low = (np.asarray(array, np.float64) - high.astype(np.float64)).astype(jnp.bfloat16)
    return high, low


def split(value):
    high = value.astype(BF16)
    return high, (value - high.astype(F32)).astype(BF16)


def dot(a, b):
    return jnp.dot(a, b, preferred_element_type=F32)


def spot(index):
    rep, rest = divmod(index, 32)
    high, x = divmod(rep, 4)
    y, rest = divmod(rest, 8)
    low, core = divmod(rest, 2)
    return x, y, high * 4 + low, core


def place(x, y, z, core):
    x, y, z = x % 4, y % 4, z % 8
    return ((z // 4) * 4 + x) * 32 + y * 8 + (z % 4) * 2 + core


def fetch(value, source):
    return lax.ppermute(value, AXES, [(place(*source(*spot(i))), i) for i in range(256)])


def along(axis, step):
    def source(x, y, z, core):
        if (core + axis) % 2 == 0:
            return x, y + step, z, core
        if step == 2 and z % 2:
            return x, y, z - 2, core
        return x, y, z + step, core

    return source


def along_x(step):
    return lambda x, y, z, core: (x + step, y, z, core)


def pair_x(x, y, z, core):
    return x ^ 1, y, z, core


def far_z(x, y, z, core):
    return x, y, z + 4, core


def sibling(x, y, z, core):
    return x, y, z, 1 - core


def call(kernel, out_shape, inputs, scratch=(), limit=16, flops=0, smem=0, kept=(), resident=(), anywhere=(), out_space=pltpu.VMEM):
    specs = [pl.BlockSpec(memory_space=pltpu.SMEM)] * smem
    specs += [pl.BlockSpec(memory_space=pltpu.VMEM)] * (len(inputs) - smem + len(resident))
    specs += [pl.BlockSpec(memory_space=pltpu.HBM)] * len(kept)
    specs += [pl.BlockSpec(memory_space=pl.ANY)] * len(anywhere)
    resident = [pltpu.with_memory_space_constraint(v, pltpu.VMEM) for v in resident]
    kept = [pltpu.with_memory_space_constraint(v, pltpu.HBM) for v in kept]
    inputs = (*inputs, *resident, *kept, *anywhere)
    moved = sum(math.prod(v.shape) * v.dtype.itemsize for v in inputs)
    return pl.pallas_call(
        kernel,
        out_shape=out_shape,
        in_specs=specs,
        out_specs=jax.tree.map(
            lambda _: pl.BlockSpec(memory_space=out_space),
            out_shape,
            is_leaf=lambda v: not isinstance(v, tuple),
        ),
        scratch_shapes=list(scratch),
        compiler_params=pltpu.CompilerParams(vmem_limit_bytes=limit << 20),
        cost_estimate=pl.CostEstimate(flops=flops, bytes_accessed=moved, transcendentals=0),
    )(*inputs)


def stacked(value, wide):
    return jnp.concatenate(
        [value[:, k * wide : (k + 1) * wide] for k in range(value.shape[1] // wide)], axis=0
    )


def mixed_of(momentum, gradient):
    return momentum_decay * momentum[0] + gradient[0].astype(F32)


def bands_kernel(
    momentum, gradient, cols_in, rows3, back_rows3, weight_in, exact, rounded, mixed, cols, back, weight, g, r, sems
):
    wide = WIDE * TILE
    steps = momentum.shape[2] // wide
    copies = [
        pltpu.make_async_copy(cols_in, cols, sems.at[2 * steps]),
        pltpu.make_async_copy(rows3, r, sems.at[2 * steps + 1]),
    ]
    for k in range(steps):
        cut = pl.ds(k * wide, wide)
        copies += [
            pltpu.make_async_copy(momentum.at[0, :, cut], mixed.at[k], sems.at[2 * k]),
            pltpu.make_async_copy(gradient.at[0, :, cut], g.at[k], sems.at[2 * k + 1]),
        ]
    copies += [
        pltpu.make_async_copy(back_rows3, back, sems.at[2 * steps + 2]),
        pltpu.make_async_copy(weight_in, weight, sems.at[2 * steps + 3]),
    ]
    for copy in copies:
        copy.start()
    copies[0].wait()
    narrow = []
    for k in range(steps):
        copies[2 * k + 2].wait()
        copies[2 * k + 3].wait()
        value = momentum_decay * mixed[k] + g[k].astype(F32)
        mixed[k] = value
        high, low = split(value)
        narrow.append(dot(high, cols[:wide]) + dot(low, cols[:wide]) + dot(high, cols[wide:]))
    copies[1].wait()
    high, low = split(jnp.concatenate(narrow, axis=1))
    bands = dot(r[...], jnp.concatenate([high, low, high], axis=0))
    exact[...] = bands
    rounded[...] = bands.astype(BF16)
    for copy in copies[-2:]:
        copy.wait()


def restored(bands, back, cols):
    wide = WIDE * TILE
    high, low = split(bands)
    tall = dot(back[...], jnp.concatenate([high, low, high], axis=0))
    high, low = split(stacked(tall, WIDE * BAND))

    def spread(a, b):
        return lax.dot_general(a, b, NT, preferred_element_type=F32)

    return spread(high, cols[:wide]) + spread(low, cols[:wide]) + spread(high, cols[wide:])


def residual_kernel(bands, mixed, cols, back, out):
    low = restored(bands[...], back, cols)
    wide = WIDE * TILE
    for k in range(mixed.shape[0]):
        out[0, :, k * wide : (k + 1) * wide] = mixed[k] - low[k * TILE : (k + 1) * TILE]


def soft_sign(update):
    return update * lax.rsqrt(update * update + soft_width)


def direction_kernel(total, cols, back, direction):
    sign = soft_sign(restored(total[...], back, cols))
    wide = WIDE * TILE
    for k in range(direction.shape[1] // wide):
        direction[:, k * wide : (k + 1) * wide] = sign[k * TILE : (k + 1) * TILE]


def renew_kernel(bands, ahead, behind, ahead_half, behind_half, cols, back, weight, top, bottom):
    wide = WIDE * TILE
    half = TILE // 2
    for f in range(4):
        band = bands[f * BAND : (f + 1) * BAND]
        tall = dot(back[:, BAND:], jnp.concatenate([band, band], axis=0)).astype(BF16)
        move = step_rate * soft_sign(
            lax.dot_general(stacked(tall, WIDE * BAND), cols[:wide], NT, preferred_element_type=F32)
        )
        out, at = (top, bottom)[f // 2], f % 2 * TILE
        raws = ([(weight, 0, TILE)], [(ahead, 0, TILE)], [(ahead_half, 0, half), (behind_half, half, half)])
        for raw, row, count in (*raws, [(behind, 0, TILE)])[f]:
            for k in range(weight.shape[1] // wide):
                cut = slice(k * wide, (k + 1) * wide)
                part = move[k * TILE + row : k * TILE + row + count]
                out[at + row : at + row + count, cut] = (raw[:, cut].astype(F32) - part).astype(BF16)


def forward_kernel(pieces, load, first, *refs):
    groups = len(pieces)
    refs = list(refs)
    sources = [refs.pop(0) for _ in range(2)]
    weights = [refs.pop(0) for _ in range(1 + max(n for group in pieces for n, _ in group))]
    outs = [refs.pop(0) for _ in range(2 * groups)]
    tokens = [refs.pop(0) for _ in range(2)] if load else sources
    fresh = [refs.pop(0) for _ in range(groups)]
    sems, token_sems = refs
    rows = fresh[0].shape[0]
    per = tokens[0].shape[0] // rows
    copies = []
    for g, group in enumerate(pieces):
        for f, (n, row) in enumerate(group):
            at = pl.ds(pl.multiple_of(lax.rem(first[0] + f, 4) * TILE, TILE), TILE)
            copies.append(
                pltpu.make_async_copy(weights[n].at[pl.ds(row, TILE)], fresh[g].at[at], sems.at[g, f])
            )
    token_copies = []
    if load:
        for t in range(2 * per):
            cut = pl.ds(t % per * rows, rows)
            token_copies.append(
                pltpu.make_async_copy(sources[t // per].at[cut], tokens[t // per].at[cut], token_sems.at[t])
            )
    for copy in copies[:4] + token_copies + copies[4:]:
        copy.start()
    for g in range(groups):
        for f in range(4):
            copies[4 * g + f].wait()
        for t in range(2 * per):
            if g == 0 and load:
                token_copies[t].wait()
            cut = slice(t % per * rows, (t % per + 1) * rows)
            product = lax.dot_general(tokens[t // per][cut], fresh[g][...], NT, preferred_element_type=F32)
            outs[2 * g + t // per][cut] = product.astype(BF16)


def weave_kernel(where, *refs):
    mine, theirs = refs[:4], refs[4:8]
    out, held, ready, sems = refs[8:]
    copies = []
    core, my_start, their_start = where[0], where[1], where[2]
    for g in range(4):
        held[core, lax.rem(my_start + g, 4)] = mine[g][...]
        held[1 - core, lax.rem(their_start + g, 4)] = theirs[g][...]
    for y in range(4):
        for z in range(4):
            left = held[0, z, :, y * TILE : (y + 1) * TILE]
            right = held[1, y, :, z * TILE : (z + 1) * TILE]
            chip = y * 4 + z
            ready[chip] = jnp.concatenate([left, right], axis=1)
            cut = pl.ds(chip * 2 * TILE, 2 * TILE)
            copies.append(pltpu.make_async_copy(ready.at[chip], out.at[:, cut], sems.at[chip]))
            copies[-1].start()
    for copy in copies:
        copy.wait()


def on_device(momentum, gradient, weight, activations):
    cosines = cosine_rows()
    high, low = halves(cosines)
    eye = np.eye(WIDE)
    cols_hi, cols_lo = (np.kron(eye, np.asarray(h, np.float32).T).astype(jnp.bfloat16) for h in (high, low))
    rows3 = np.concatenate([high, high, low], axis=1)
    back_rows3 = np.concatenate([high.T, high.T, low.T], axis=1)
    width = weight.shape[1]
    narrow = width // TILE * BAND
    rows = weight.shape[0]
    tokens = activations.shape[0]

    core = lax.axis_index("fsdp") % 2
    y = lax.axis_index("fsdp") // 8
    z = lax.axis_index("fsdp") // 2 % 4
    first = jnp.where(core == 0, y, z).astype(jnp.int32)
    second = jnp.where(core == 0, z, y).astype(jnp.int32)

    shape = jax.ShapeDtypeStruct
    steps = width // (WIDE * TILE)
    cols_in = np.concatenate([cols_hi, cols_lo], axis=0)
    exact, rounded, mixed, cols, back, held_weight = call(
        bands_kernel,
        (
            shape((BAND, narrow), F32),
            shape((BAND, narrow), BF16),
            pltpu.VMEM((steps, rows, WIDE * TILE), F32),
            pltpu.VMEM(cols_in.shape, BF16),
            pltpu.VMEM(back_rows3.shape, BF16),
            pltpu.VMEM(weight.shape, BF16),
        ),
        (),
        (
            pltpu.VMEM((steps, rows, WIDE * TILE), BF16),
            pltpu.VMEM(rows3.shape, BF16),
            pltpu.SemaphoreType.DMA((2 * steps + 4,)),
        ),
        kept=(momentum, gradient, cols_in, rows3, back_rows3, weight),
    )

    def after(value, *others):
        return lax.optimization_barrier((value, *others))[0]

    ahead, behind = (fetch(after(weight, rounded), along(0, n)) for n in (1, -1))

    parts = [rounded.astype(F32)] + [fetch(rounded, along_x(n)).astype(F32) for n in (1, 2, -1)]
    sent = ((parts[0] + parts[2]) + (parts[1] + parts[3])).astype(BF16)
    other = fetch(after(activations, ahead, behind, sent), sibling)
    total = sent.astype(F32) + fetch(after(sent, ahead, behind), far_z).astype(F32)
    halves_across = [fetch(ahead[: rows // 2], along(0, 1)), fetch(behind[rows // 2 :], along(0, -1))]

    sent = after(total.astype(BF16), other)
    line = jnp.concatenate([sent] + [fetch(sent, along(0, n)) for n in (1, 2, -1)], axis=0)
    direction = call(
        direction_kernel,
        shape((rows, width), F32),
        (total,),
        resident=(cols, back),
    )
    half_rows = shape((2 * rows, width), BF16)
    top, bottom = call(
        renew_kernel,
        (half_rows, half_rows),
        (line, ahead, behind, *halves_across),
        resident=(cols, back, held_weight),
    )
    new_momentum = call(
        residual_kernel,
        shape(momentum.shape, F32),
        (after(exact, top),),
        resident=(mixed, cols, back),
    )

    next_top, last_bottom = fetch(top, along(1, 1)), fetch(bottom, along(1, -1))
    next_bottom, last_top = fetch(bottom, along(1, 1)), fetch(top, along(1, -1))
    far_top, far_bottom = fetch(next_top, along(1, 1)), fetch(last_bottom, along(1, -1))
    lines = [
        [(a, row) for a in pair for row in (0, TILE)]
        for pair in (
            (after(top, new_momentum, direction), bottom),
            (next_top, next_bottom),
            (far_top, far_bottom),
            (last_top, last_bottom),
        )
    ]

    block = shape((tokens, 4 * rows), BF16)

    def forward(order, load):
        used, pieces = [], []
        for g in order:
            pieces.append([])
            for value, row in lines[g]:
                found = [n for n, v in enumerate(used) if v is value]
                if not found:
                    used.append(value)
                pieces[-1].append((found[0] if found else len(used) - 1, row))
        count = len(order)
        held = pltpu.VMEM(activations.shape, BF16)
        return call(
            lambda *refs: forward_kernel(pieces, load, *refs),
            (*[block] * (2 * count), *([held] * 2 if load else [])),
            [first[None]],
            (
                *[pltpu.VMEM((4 * rows, width), BF16)] * count,
                pltpu.SemaphoreType.DMA((count, 4)),
                pltpu.SemaphoreType.DMA((4,)),
            ),
            limit=24,
            flops=count * 2 * 2 * tokens * 4 * rows * width,
            smem=1,
            resident=() if load else (activations_in, other_in),
            kept=[activations] if load else [],
            anywhere=([other] if load else []) + used,
        )

    *results, activations_in, other_in = forward([0], True)
    results += forward([3, 1], False)
    results += forward([2], False)
    mine, theirs = [None] * 4, [None] * 4
    for n, g in enumerate((0, 3, 1, 2)):
        mine[g] = results[2 * n]
        theirs[g] = fetch(results[2 * n + 1], sibling)
    where = jnp.stack([core.astype(jnp.int32), second, first])
    projected = call(
        weave_kernel,
        shape((tokens, 32 * rows), BF16),
        (where, *mine, *theirs),
        (
            pltpu.VMEM((2, 4, tokens, 4 * rows), BF16),
            pltpu.VMEM((16, tokens, 2 * rows), BF16),
            pltpu.SemaphoreType.DMA((16,)),
        ),
        smem=1,
        out_space=pl.ANY,
    )
    return (new_momentum, direction, projected)


def solution(mesh):
    return jax.shard_map(
        on_device,
        mesh=mesh,
        in_specs=(
            P("rep", "fsdp", None),
            P("rep", "fsdp", None),
            P("fsdp", None),
            P(("rep", "fsdp"), None),
        ),
        out_specs=(P("rep", "fsdp", None), P("fsdp", None), P(("rep", "fsdp"), None)),
        check_vma=False,
    )
```

```python
import math

import jax
import jax.numpy as jnp
import numpy as np
from jax import lax
from jax.experimental import pallas as pl
from jax.experimental.pallas import tpu as pltpu
from jax.sharding import PartitionSpec as P

TILE = 64
BAND = 16
WIDE = 8
AXES = ("rep", "fsdp")

momentum_decay = 0.9
step_rate = 0.02
soft_width = 0.25

F32 = jnp.float32
BF16 = jnp.bfloat16
NT = (((1,), (1,)), ((), ()))


def cosine_rows():
    freq = np.arange(BAND, dtype=np.float64)[:, None]
    place = np.arange(TILE, dtype=np.float64)[None, :]
    factor = np.where(freq == 0.0, math.sqrt(1.0 / TILE), math.sqrt(2.0 / TILE))
    return factor * np.cos(math.pi * (2.0 * place + 1.0) * freq / (2.0 * TILE))


def halves(array):
    high = np.asarray(array, np.float32).astype(jnp.bfloat16)
    low = (np.asarray(array, np.float64) - high.astype(np.float64)).astype(jnp.bfloat16)
    return high, low


def split(value):
    high = value.astype(BF16)
    return high, (value - high.astype(F32)).astype(BF16)


def dot(a, b):
    return jnp.dot(a, b, preferred_element_type=F32)


def spot(index):
    rep, rest = divmod(index, 32)
    high, x = divmod(rep, 4)
    y, rest = divmod(rest, 8)
    low, core = divmod(rest, 2)
    return x, y, high * 4 + low, core


def place(x, y, z, core):
    x, y, z = x % 4, y % 4, z % 8
    return ((z // 4) * 4 + x) * 32 + y * 8 + (z % 4) * 2 + core


def fetch(value, source):
    return lax.ppermute(value, AXES, [(place(*source(*spot(i))), i) for i in range(256)])


def along(axis, step):
    def source(x, y, z, core):
        if (core + axis) % 2 == 0:
            return x, y + step, z, core
        if step == 2 and z % 2:
            return x, y, z - 2, core
        return x, y, z + step, core

    return source


def along_x(step):
    return lambda x, y, z, core: (x + step, y, z, core)


def pair_x(x, y, z, core):
    return x ^ 1, y, z, core


def far_z(x, y, z, core):
    return x, y, z + 4, core


def sibling(x, y, z, core):
    return x, y, z, 1 - core


def call(kernel, out_shape, inputs, scratch=(), limit=16, flops=0, smem=0, kept=(), resident=(), anywhere=(), out_space=pltpu.VMEM):
    specs = [pl.BlockSpec(memory_space=pltpu.SMEM)] * smem
    specs += [pl.BlockSpec(memory_space=pltpu.VMEM)] * (len(inputs) - smem + len(resident))
    specs += [pl.BlockSpec(memory_space=pltpu.HBM)] * len(kept)
    specs += [pl.BlockSpec(memory_space=pl.ANY)] * len(anywhere)
    resident = [pltpu.with_memory_space_constraint(v, pltpu.VMEM) for v in resident]
    kept = [pltpu.with_memory_space_constraint(v, pltpu.HBM) for v in kept]
    inputs = (*inputs, *resident, *kept, *anywhere)
    moved = sum(math.prod(v.shape) * v.dtype.itemsize for v in inputs)
    return pl.pallas_call(
        kernel,
        out_shape=out_shape,
        in_specs=specs,
        out_specs=jax.tree.map(
            lambda _: pl.BlockSpec(memory_space=out_space),
            out_shape,
            is_leaf=lambda v: not isinstance(v, tuple),
        ),
        scratch_shapes=list(scratch),
        compiler_params=pltpu.CompilerParams(vmem_limit_bytes=limit << 20),
        cost_estimate=pl.CostEstimate(flops=flops, bytes_accessed=moved, transcendentals=0),
    )(*inputs)


def stacked(value, wide):
    return jnp.concatenate(
        [value[:, k * wide : (k + 1) * wide] for k in range(value.shape[1] // wide)], axis=0
    )


def mixed_of(momentum, gradient):
    return momentum_decay * momentum[0] + gradient[0].astype(F32)


def bands_kernel(
    momentum, gradient, cols_in, rows3, back_rows3, weight_in, exact, rounded, mixed, cols, back, weight, g, r, sems
):
    wide = WIDE * TILE
    steps = momentum.shape[2] // wide
    copies = [
        pltpu.make_async_copy(cols_in, cols, sems.at[2 * steps]),
        pltpu.make_async_copy(rows3, r, sems.at[2 * steps + 1]),
    ]
    for k in range(steps):
        cut = pl.ds(k * wide, wide)
        copies += [
            pltpu.make_async_copy(momentum.at[0, :, cut], mixed.at[k], sems.at[2 * k]),
            pltpu.make_async_copy(gradient.at[0, :, cut], g.at[k], sems.at[2 * k + 1]),
        ]
    copies += [
        pltpu.make_async_copy(back_rows3, back, sems.at[2 * steps + 2]),
        pltpu.make_async_copy(weight_in, weight, sems.at[2 * steps + 3]),
    ]
    for copy in copies:
        copy.start()
    copies[0].wait()
    narrow = []
    for k in range(steps):
        copies[2 * k + 2].wait()
        copies[2 * k + 3].wait()
        value = momentum_decay * mixed[k] + g[k].astype(F32)
        mixed[k] = value
        high, low = split(value)
        narrow.append(dot(high, cols[:wide]) + dot(low, cols[:wide]) + dot(high, cols[wide:]))
    copies[1].wait()
    high, low = split(jnp.concatenate(narrow, axis=1))
    bands = dot(r[...], jnp.concatenate([high, low, high], axis=0))
    exact[...] = bands
    rounded[...] = bands.astype(BF16)
    for copy in copies[-2:]:
        copy.wait()


def restored(bands, back, cols):
    wide = WIDE * TILE
    high, low = split(bands)
    tall = dot(back[...], jnp.concatenate([high, low, high], axis=0))
    high, low = split(stacked(tall, WIDE * BAND))

    def spread(a, b):
        return lax.dot_general(a, b, NT, preferred_element_type=F32)

    return spread(high, cols[:wide]) + spread(low, cols[:wide]) + spread(high, cols[wide:])


def residual_kernel(bands, mixed, cols, back, out):
    low = restored(bands[...], back, cols)
    wide = WIDE * TILE
    for k in range(mixed.shape[0]):
        out[0, :, k * wide : (k + 1) * wide] = mixed[k] - low[k * TILE : (k + 1) * TILE]


def soft_sign(update):
    return update * lax.rsqrt(update * update + soft_width)


def direction_kernel(total, cols, back, direction):
    sign = soft_sign(restored(total[...], back, cols))
    wide = WIDE * TILE
    for k in range(direction.shape[1] // wide):
        direction[:, k * wide : (k + 1) * wide] = sign[k * TILE : (k + 1) * TILE]


def renew_kernel(bands, ahead, behind, ahead_half, behind_half, cols, back, weight, top, bottom):
    wide = WIDE * TILE
    half = TILE // 2
    for f in range(4):
        band = bands[f * BAND : (f + 1) * BAND]
        tall = dot(back[:, BAND:], jnp.concatenate([band, band], axis=0)).astype(BF16)
        move = step_rate * soft_sign(
            lax.dot_general(stacked(tall, WIDE * BAND), cols[:wide], NT, preferred_element_type=F32)
        )
        out, at = (top, bottom)[f // 2], f % 2 * TILE
        raws = ([(weight, 0, TILE)], [(ahead, 0, TILE)], [(ahead_half, 0, half), (behind_half, half, half)])
        for raw, row, count in (*raws, [(behind, 0, TILE)])[f]:
            for k in range(weight.shape[1] // wide):
                cut = slice(k * wide, (k + 1) * wide)
                part = move[k * TILE + row : k * TILE + row + count]
                out[at + row : at + row + count, cut] = (raw[:, cut].astype(F32) - part).astype(BF16)


def forward_kernel(pieces, load, first, *refs):
    groups = len(pieces)
    refs = list(refs)
    sources = [refs.pop(0) for _ in range(2)]
    weights = [refs.pop(0) for _ in range(1 + max(n for group in pieces for n, _ in group))]
    outs = [refs.pop(0) for _ in range(2 * groups)]
    tokens = [refs.pop(0) for _ in range(2)] if load else sources
    fresh = [refs.pop(0) for _ in range(groups)]
    sems, token_sems = refs
    rows = fresh[0].shape[0]
    per = tokens[0].shape[0] // rows
    copies = []
    for g, group in enumerate(pieces):
        for f, (n, row) in enumerate(group):
            at = pl.ds(pl.multiple_of(lax.rem(first[0] + f, 4) * TILE, TILE), TILE)
            copies.append(
                pltpu.make_async_copy(weights[n].at[pl.ds(row, TILE)], fresh[g].at[at], sems.at[g, f])
            )
    token_copies = []
    if load:
        for t in range(2 * per):
            cut = pl.ds(t % per * rows, rows)
            token_copies.append(
                pltpu.make_async_copy(sources[t // per].at[cut], tokens[t // per].at[cut], token_sems.at[t])
            )
    for copy in copies[:4] + token_copies + copies[4:]:
        copy.start()
    for g in range(groups):
        for f in range(4):
            copies[4 * g + f].wait()
        for t in range(2 * per):
            if g == 0 and load:
                token_copies[t].wait()
            cut = slice(t % per * rows, (t % per + 1) * rows)
            product = lax.dot_general(tokens[t // per][cut], fresh[g][...], NT, preferred_element_type=F32)
            outs[2 * g + t // per][cut] = product.astype(BF16)


def far_kernel(first, tokens, upper, lower, out, fresh, sems):
    copies = []
    for f in range(4):
        at = pl.ds(pl.multiple_of(lax.rem(first[0] + f, 4) * TILE, TILE), TILE)
        source = (upper, lower)[f // 2].at[pl.ds(f % 2 * TILE, TILE)]
        copies.append(pltpu.make_async_copy(source, fresh.at[at], sems.at[f]))
        copies[f].start()
    for copy in copies:
        copy.wait()
    own_kernel(tokens, fresh, out)


def own_kernel(tokens, fresh, out):
    rows = fresh.shape[0]
    for t in range(tokens.shape[0] // rows):
        cut = slice(t * rows, (t + 1) * rows)
        product = lax.dot_general(tokens[cut], fresh[...], NT, preferred_element_type=F32)
        out[cut] = product.astype(BF16)


def weave_kernel(where, *refs):
    mine, theirs = refs[:4], refs[4:8]
    out, held, ready, sems = refs[8:]
    copies = []
    core, my_start, their_start = where[0], where[1], where[2]
    for g in range(4):
        held[core, lax.rem(my_start + g, 4)] = mine[g][...]
        held[1 - core, lax.rem(their_start + g, 4)] = theirs[g][...]
    for y in range(4):
        for z in range(4):
            left = held[0, z, :, y * TILE : (y + 1) * TILE]
            right = held[1, y, :, z * TILE : (z + 1) * TILE]
            chip = y * 4 + z
            ready[chip] = jnp.concatenate([left, right], axis=1)
            cut = pl.ds(chip * 2 * TILE, 2 * TILE)
            copies.append(pltpu.make_async_copy(ready.at[chip], out.at[:, cut], sems.at[chip]))
            copies[-1].start()
    for copy in copies:
        copy.wait()


def on_device(momentum, gradient, weight, activations):
    cosines = cosine_rows()
    high, low = halves(cosines)
    eye = np.eye(WIDE)
    cols_hi, cols_lo = (np.kron(eye, np.asarray(h, np.float32).T).astype(jnp.bfloat16) for h in (high, low))
    rows3 = np.concatenate([high, high, low], axis=1)
    back_rows3 = np.concatenate([high.T, high.T, low.T], axis=1)
    width = weight.shape[1]
    narrow = width // TILE * BAND
    rows = weight.shape[0]
    tokens = activations.shape[0]

    core = lax.axis_index("fsdp") % 2
    y = lax.axis_index("fsdp") // 8
    z = lax.axis_index("fsdp") // 2 % 4
    first = jnp.where(core == 0, y, z).astype(jnp.int32)
    second = jnp.where(core == 0, z, y).astype(jnp.int32)

    shape = jax.ShapeDtypeStruct
    steps = width // (WIDE * TILE)
    cols_in = np.concatenate([cols_hi, cols_lo], axis=0)
    exact, rounded, mixed, cols, back, held_weight = call(
        bands_kernel,
        (
            shape((BAND, narrow), F32),
            shape((BAND, narrow), BF16),
            pltpu.VMEM((steps, rows, WIDE * TILE), F32),
            pltpu.VMEM(cols_in.shape, BF16),
            pltpu.VMEM(back_rows3.shape, BF16),
            pltpu.VMEM(weight.shape, BF16),
        ),
        (),
        (
            pltpu.VMEM((steps, rows, WIDE * TILE), BF16),
            pltpu.VMEM(rows3.shape, BF16),
            pltpu.SemaphoreType.DMA((2 * steps + 4,)),
        ),
        kept=(momentum, gradient, cols_in, rows3, back_rows3, weight),
    )

    def after(value, *others):
        return lax.optimization_barrier((value, *others))[0]

    ahead, behind = (fetch(after(weight, rounded), along(0, n)) for n in (1, -1))

    parts = [rounded.astype(F32)] + [fetch(rounded, along_x(n)).astype(F32) for n in (1, 2, -1)]
    sent = ((parts[0] + parts[2]) + (parts[1] + parts[3])).astype(BF16)
    total = sent.astype(F32) + fetch(after(sent, ahead, behind), far_z).astype(F32)
    halves_across = [fetch(ahead[: rows // 2], along(0, 1)), fetch(behind[rows // 2 :], along(0, -1))]

    sent = total.astype(BF16)
    line = jnp.concatenate([sent] + [fetch(sent, along(0, n)) for n in (1, 2, -1)], axis=0)
    direction = call(
        direction_kernel,
        shape((rows, width), F32),
        (total,),
        resident=(cols, back),
    )
    half_rows = shape((2 * rows, width), BF16)
    top, bottom = call(
        renew_kernel,
        (half_rows, half_rows),
        (line, ahead, behind, *halves_across),
        resident=(cols, back, held_weight),
    )
    other = fetch(after(activations, top), sibling)
    new_momentum = call(
        residual_kernel,
        shape(momentum.shape, F32),
        (after(exact, top),),
        resident=(mixed, cols, back),
    )

    next_top, last_bottom = fetch(top, along(1, 1)), fetch(bottom, along(1, -1))
    next_bottom, last_top = fetch(bottom, along(1, 1)), fetch(top, along(1, -1))
    far_top, far_bottom = fetch(next_top, along(1, 1)), fetch(last_bottom, along(1, -1))
    lines = [
        [(a, row) for a in pair for row in (0, TILE)]
        for pair in (
            (after(top, new_momentum, direction), bottom),
            (next_top, next_bottom),
            (far_top, far_bottom),
            (last_top, last_bottom),
        )
    ]

    block = shape((tokens, 4 * rows), BF16)

    def forward(order, load):
        used, pieces = [], []
        for g in order:
            pieces.append([])
            for value, row in lines[g]:
                found = [n for n, v in enumerate(used) if v is value]
                if not found:
                    used.append(value)
                pieces[-1].append((found[0] if found else len(used) - 1, row))
        count = len(order)
        held = pltpu.VMEM(activations.shape, BF16)
        return call(
            lambda *refs: forward_kernel(pieces, load, *refs),
            (*[block] * (2 * count), *([held] * 2 if load else [])),
            [first[None]],
            (
                *[pltpu.VMEM((4 * rows, width), BF16)] * count,
                pltpu.SemaphoreType.DMA((count, 4)),
                pltpu.SemaphoreType.DMA((4,)),
            ),
            limit=24,
            flops=count * 2 * 2 * tokens * 4 * rows * width,
            smem=1,
            resident=() if load else (activations_in, other_in),
            kept=[activations] if load else [],
            anywhere=([other] if load else []) + used,
        )

    *results, activations_in, other_in = forward([0], True)
    results += forward([3, 1], False)
    flops = 2 * tokens * 4 * rows * width
    far_other, fresh = call(
        far_kernel,
        (block, pltpu.VMEM((4 * rows, width), BF16)),
        [first[None]],
        (pltpu.SemaphoreType.DMA((4,)),),
        flops=flops,
        smem=1,
        resident=(other_in,),
        anywhere=(far_top, far_bottom),
    )
    far_own = call(own_kernel, block, (), flops=flops, resident=(activations_in, fresh))
    results += (far_own, far_other)
    mine, theirs = [None] * 4, [None] * 4
    for n, g in enumerate((0, 3, 1, 2)):
        mine[g] = results[2 * n]
        theirs[g] = fetch(results[2 * n + 1], sibling)
    where = jnp.stack([core.astype(jnp.int32), second, first])
    projected = call(
        weave_kernel,
        shape((tokens, 32 * rows), BF16),
        (where, *mine, *theirs),
        (
            pltpu.VMEM((2, 4, tokens, 4 * rows), BF16),
            pltpu.VMEM((16, tokens, 2 * rows), BF16),
            pltpu.SemaphoreType.DMA((16,)),
        ),
        smem=1,
        out_space=pl.ANY,
    )
    return (new_momentum, direction, projected)


def solution(mesh):
    return jax.shard_map(
        on_device,
        mesh=mesh,
        in_specs=(
            P("rep", "fsdp", None),
            P("rep", "fsdp", None),
            P("fsdp", None),
            P(("rep", "fsdp"), None),
        ),
        out_specs=(P("rep", "fsdp", None), P("fsdp", None), P(("rep", "fsdp"), None)),
        check_vma=False,
    )
```

```python
import math

import jax
import jax.numpy as jnp
import numpy as np
from jax import lax
from jax.experimental import pallas as pl
from jax.experimental.pallas import tpu as pltpu
from jax.sharding import PartitionSpec as P

TILE = 64
BAND = 16
WIDE = 8
AXES = ("rep", "fsdp")

momentum_decay = 0.9
step_rate = 0.02
soft_width = 0.25

F32 = jnp.float32
BF16 = jnp.bfloat16
NT = (((1,), (1,)), ((), ()))


def cosine_rows():
    freq = np.arange(BAND, dtype=np.float64)[:, None]
    place = np.arange(TILE, dtype=np.float64)[None, :]
    factor = np.where(freq == 0.0, math.sqrt(1.0 / TILE), math.sqrt(2.0 / TILE))
    return factor * np.cos(math.pi * (2.0 * place + 1.0) * freq / (2.0 * TILE))


def halves(array):
    high = np.asarray(array, np.float32).astype(jnp.bfloat16)
    low = (np.asarray(array, np.float64) - high.astype(np.float64)).astype(jnp.bfloat16)
    return high, low


def split(value):
    high = value.astype(BF16)
    return high, (value - high.astype(F32)).astype(BF16)


def dot(a, b):
    return jnp.dot(a, b, preferred_element_type=F32)


def spot(index):
    rep, rest = divmod(index, 32)
    high, x = divmod(rep, 4)
    y, rest = divmod(rest, 8)
    low, core = divmod(rest, 2)
    return x, y, high * 4 + low, core


def place(x, y, z, core):
    x, y, z = x % 4, y % 4, z % 8
    return ((z // 4) * 4 + x) * 32 + y * 8 + (z % 4) * 2 + core


def fetch(value, source):
    return lax.ppermute(value, AXES, [(place(*source(*spot(i))), i) for i in range(256)])


def along(axis, step):
    def source(x, y, z, core):
        if (core + axis) % 2 == 0:
            return x, y + step, z, core
        if step == 2 and z % 2:
            return x, y, z - 2, core
        return x, y, z + step, core

    return source


def along_x(step):
    return lambda x, y, z, core: (x + step, y, z, core)


def pair_x(x, y, z, core):
    return x ^ 1, y, z, core


def far_z(x, y, z, core):
    return x, y, z + 4, core


def sibling(x, y, z, core):
    return x, y, z, 1 - core


def call(kernel, out_shape, inputs, scratch=(), limit=10, flops=0, smem=0, kept=(), resident=(), anywhere=(), out_space=pltpu.VMEM):
    specs = [pl.BlockSpec(memory_space=pltpu.SMEM)] * smem
    specs += [pl.BlockSpec(memory_space=pltpu.VMEM)] * (len(inputs) - smem + len(resident))
    specs += [pl.BlockSpec(memory_space=pltpu.HBM)] * len(kept)
    specs += [pl.BlockSpec(memory_space=pl.ANY)] * len(anywhere)
    resident = [pltpu.with_memory_space_constraint(v, pltpu.VMEM) for v in resident]
    kept = [pltpu.with_memory_space_constraint(v, pltpu.HBM) for v in kept]
    inputs = (*inputs, *resident, *kept, *anywhere)
    moved = sum(math.prod(v.shape) * v.dtype.itemsize for v in inputs)
    return pl.pallas_call(
        kernel,
        out_shape=out_shape,
        in_specs=specs,
        out_specs=jax.tree.map(
            lambda _: pl.BlockSpec(memory_space=out_space),
            out_shape,
            is_leaf=lambda v: not isinstance(v, tuple),
        ),
        scratch_shapes=list(scratch),
        compiler_params=pltpu.CompilerParams(vmem_limit_bytes=limit << 20),
        cost_estimate=pl.CostEstimate(flops=flops, bytes_accessed=moved, transcendentals=0),
    )(*inputs)


def stacked(value, wide):
    return jnp.concatenate(
        [value[:, k * wide : (k + 1) * wide] for k in range(value.shape[1] // wide)], axis=0
    )


def mixed_of(momentum, gradient):
    return momentum_decay * momentum[0] + gradient[0].astype(F32)


def bands_kernel(
    momentum, gradient, cols_in, rows3, back_rows3, weight_in, exact, rounded, mixed, cols, back, weight, g, r, sems
):
    wide = WIDE * TILE
    steps = momentum.shape[2] // wide
    copies = [
        pltpu.make_async_copy(cols_in, cols, sems.at[2 * steps]),
        pltpu.make_async_copy(rows3, r, sems.at[2 * steps + 1]),
    ]
    for k in range(steps):
        cut = pl.ds(k * wide, wide)
        copies += [
            pltpu.make_async_copy(momentum.at[0, :, cut], mixed.at[k], sems.at[2 * k]),
            pltpu.make_async_copy(gradient.at[0, :, cut], g.at[k], sems.at[2 * k + 1]),
        ]
    copies += [
        pltpu.make_async_copy(back_rows3, back, sems.at[2 * steps + 2]),
        pltpu.make_async_copy(weight_in, weight, sems.at[2 * steps + 3]),
    ]
    for copy in copies:
        copy.start()
    copies[0].wait()
    narrow = []
    for k in range(steps):
        copies[2 * k + 2].wait()
        copies[2 * k + 3].wait()
        value = momentum_decay * mixed[k] + g[k].astype(F32)
        mixed[k] = value
        high, low = split(value)
        narrow.append(dot(high, cols[:wide]) + dot(low, cols[:wide]) + dot(high, cols[wide:]))
    copies[1].wait()
    high, low = split(jnp.concatenate(narrow, axis=1))
    bands = dot(r[...], jnp.concatenate([high, low, high], axis=0))
    exact[...] = bands
    rounded[...] = bands.astype(BF16)
    for copy in copies[-2:]:
        copy.wait()


def restored(bands, back, cols):
    wide = WIDE * TILE
    high, low = split(bands)
    tall = dot(back[...], jnp.concatenate([high, low, high], axis=0))
    high, low = split(stacked(tall, WIDE * BAND))

    def spread(a, b):
        return lax.dot_general(a, b, NT, preferred_element_type=F32)

    return spread(high, cols[:wide]) + spread(low, cols[:wide]) + spread(high, cols[wide:])


def residual_kernel(bands, mixed, cols, back, out):
    low = restored(bands[...], back, cols)
    wide = WIDE * TILE
    for k in range(mixed.shape[0]):
        out[0, :, k * wide : (k + 1) * wide] = mixed[k] - low[k * TILE : (k + 1) * TILE]


def soft_sign(update):
    return update * lax.rsqrt(update * update + soft_width)


def direction_kernel(total, cols, back, direction):
    sign = soft_sign(restored(total[...], back, cols))
    wide = WIDE * TILE
    for k in range(direction.shape[1] // wide):
        direction[:, k * wide : (k + 1) * wide] = sign[k * TILE : (k + 1) * TILE]


def renew_kernel(bands, ahead, behind, ahead_half, behind_half, cols, back, weight, top, bottom):
    wide = WIDE * TILE
    half = TILE // 2
    for f in range(4):
        band = bands[f * BAND : (f + 1) * BAND]
        tall = dot(back[:, BAND:], jnp.concatenate([band, band], axis=0)).astype(BF16)
        move = step_rate * soft_sign(
            lax.dot_general(stacked(tall, WIDE * BAND), cols[:wide], NT, preferred_element_type=F32)
        )
        out, at = (top, bottom)[f // 2], f % 2 * TILE
        raws = ([(weight, 0, TILE)], [(ahead, 0, TILE)], [(ahead_half, 0, half), (behind_half, half, half)])
        for raw, row, count in (*raws, [(behind, 0, TILE)])[f]:
            for k in range(weight.shape[1] // wide):
                cut = slice(k * wide, (k + 1) * wide)
                part = move[k * TILE + row : k * TILE + row + count]
                out[at + row : at + row + count, cut] = (raw[:, cut].astype(F32) - part).astype(BF16)


def forward_kernel(pieces, load, first, *refs):
    groups = len(pieces)
    refs = list(refs)
    sources = [refs.pop(0) for _ in range(2)]
    weights = [refs.pop(0) for _ in range(1 + max(n for group in pieces for n, _ in group))]
    outs = [refs.pop(0) for _ in range(2 * groups)]
    tokens = [refs.pop(0) for _ in range(2)] if load else sources
    fresh = [refs.pop(0) for _ in range(groups)]
    sems, token_sems = refs
    rows = fresh[0].shape[0]
    per = tokens[0].shape[0] // rows
    copies = []
    for g, group in enumerate(pieces):
        for f, (n, row) in enumerate(group):
            at = pl.ds(pl.multiple_of(lax.rem(first[0] + f, 4) * TILE, TILE), TILE)
            copies.append(
                pltpu.make_async_copy(weights[n].at[pl.ds(row, TILE)], fresh[g].at[at], sems.at[g, f])
            )
    token_copies = []
    if load:
        for t in range(2 * per):
            cut = pl.ds(t % per * rows, rows)
            token_copies.append(
                pltpu.make_async_copy(sources[t // per].at[cut], tokens[t // per].at[cut], token_sems.at[t])
            )
    for copy in copies[:4] + token_copies + copies[4:]:
        copy.start()
    for g in range(groups):
        for f in range(4):
            copies[4 * g + f].wait()
        for t in range(2 * per):
            if g == 0 and load:
                token_copies[t].wait()
            cut = slice(t % per * rows, (t % per + 1) * rows)
            product = lax.dot_general(tokens[t // per][cut], fresh[g][...], NT, preferred_element_type=F32)
            outs[2 * g + t // per][cut] = product.astype(BF16)


def far_kernel(first, tokens, upper, lower, out, fresh, sems):
    copies = []
    for f in range(4):
        at = pl.ds(pl.multiple_of(lax.rem(first[0] + f, 4) * TILE, TILE), TILE)
        source = (upper, lower)[f // 2].at[pl.ds(f % 2 * TILE, TILE)]
        copies.append(pltpu.make_async_copy(source, fresh.at[at], sems.at[f]))
        copies[f].start()
    for copy in copies:
        copy.wait()
    own_kernel(tokens, fresh, out)


def own_kernel(tokens, fresh, out):
    rows = fresh.shape[0]
    for t in range(tokens.shape[0] // rows):
        cut = slice(t * rows, (t + 1) * rows)
        product = lax.dot_general(tokens[cut], fresh[...], NT, preferred_element_type=F32)
        out[cut] = product.astype(BF16)


def weave_kernel(where, *refs):
    mine, theirs = refs[:4], refs[4:8]
    out, held, ready, sems = refs[8:]
    copies = []
    core, my_start, their_start = where[0], where[1], where[2]
    for g in range(4):
        held[core, lax.rem(my_start + g, 4)] = mine[g][...]
        held[1 - core, lax.rem(their_start + g, 4)] = theirs[g][...]
    for y in range(4):
        for z in range(4):
            left = held[0, z, :, y * TILE : (y + 1) * TILE]
            right = held[1, y, :, z * TILE : (z + 1) * TILE]
            chip = y * 4 + z
            ready[chip] = jnp.concatenate([left, right], axis=1)
            cut = pl.ds(chip * 2 * TILE, 2 * TILE)
            copies.append(pltpu.make_async_copy(ready.at[chip], out.at[:, cut], sems.at[chip]))
            copies[-1].start()
    for copy in copies:
        copy.wait()


def on_device(momentum, gradient, weight, activations):
    cosines = cosine_rows()
    high, low = halves(cosines)
    eye = np.eye(WIDE)
    cols_hi, cols_lo = (np.kron(eye, np.asarray(h, np.float32).T).astype(jnp.bfloat16) for h in (high, low))
    rows3 = np.concatenate([high, high, low], axis=1)
    back_rows3 = np.concatenate([high.T, high.T, low.T], axis=1)
    width = weight.shape[1]
    narrow = width // TILE * BAND
    rows = weight.shape[0]
    tokens = activations.shape[0]

    core = lax.axis_index("fsdp") % 2
    y = lax.axis_index("fsdp") // 8
    z = lax.axis_index("fsdp") // 2 % 4
    first = jnp.where(core == 0, y, z).astype(jnp.int32)
    second = jnp.where(core == 0, z, y).astype(jnp.int32)

    shape = jax.ShapeDtypeStruct
    steps = width // (WIDE * TILE)
    cols_in = np.concatenate([cols_hi, cols_lo], axis=0)
    exact, rounded, mixed, cols, back, held_weight = call(
        bands_kernel,
        (
            shape((BAND, narrow), F32),
            shape((BAND, narrow), BF16),
            pltpu.VMEM((steps, rows, WIDE * TILE), F32),
            pltpu.VMEM(cols_in.shape, BF16),
            pltpu.VMEM(back_rows3.shape, BF16),
            pltpu.VMEM(weight.shape, BF16),
        ),
        (),
        (
            pltpu.VMEM((steps, rows, WIDE * TILE), BF16),
            pltpu.VMEM(rows3.shape, BF16),
            pltpu.SemaphoreType.DMA((2 * steps + 4,)),
        ),
        kept=(momentum, gradient, cols_in, rows3, back_rows3, weight),
    )

    def after(value, *others):
        return lax.optimization_barrier((value, *others))[0]

    ahead, behind = (fetch(after(weight, rounded), along(0, n)) for n in (1, -1))

    parts = [rounded.astype(F32)] + [fetch(rounded, along_x(n)).astype(F32) for n in (1, 2, -1)]
    sent = ((parts[0] + parts[2]) + (parts[1] + parts[3])).astype(BF16)
    total = sent.astype(F32) + fetch(after(sent, ahead, behind), far_z).astype(F32)
    halves_across = [fetch(ahead[: rows // 2], along(0, 1)), fetch(behind[rows // 2 :], along(0, -1))]

    sent = total.astype(BF16)
    line = jnp.concatenate([sent] + [fetch(sent, along(0, n)) for n in (1, 2, -1)], axis=0)
    direction = call(
        direction_kernel,
        shape((rows, width), F32),
        (total,),
        resident=(cols, back),
    )
    half_rows = shape((2 * rows, width), BF16)
    top, bottom = call(
        renew_kernel,
        (half_rows, half_rows),
        (line, ahead, behind, *halves_across),
        resident=(cols, back, held_weight),
    )
    other = fetch(after(activations, top), sibling)
    new_momentum = call(
        residual_kernel,
        shape(momentum.shape, F32),
        (after(exact, top),),
        resident=(mixed, cols, back),
    )

    next_top, last_bottom = fetch(top, along(1, 1)), fetch(bottom, along(1, -1))
    next_bottom, last_top = fetch(bottom, along(1, 1)), fetch(top, along(1, -1))
    far_top, far_bottom = fetch(next_top, along(1, 1)), fetch(last_bottom, along(1, -1))
    lines = [
        [(a, row) for a in pair for row in (0, TILE)]
        for pair in (
            (after(top, new_momentum, direction), bottom),
            (next_top, next_bottom),
            (far_top, far_bottom),
            (last_top, last_bottom),
        )
    ]

    block = shape((tokens, 4 * rows), BF16)

    def forward(order, load):
        used, pieces = [], []
        for g in order:
            pieces.append([])
            for value, row in lines[g]:
                found = [n for n, v in enumerate(used) if v is value]
                if not found:
                    used.append(value)
                pieces[-1].append((found[0] if found else len(used) - 1, row))
        count = len(order)
        held = pltpu.VMEM(activations.shape, BF16)
        return call(
            lambda *refs: forward_kernel(pieces, load, *refs),
            (*[block] * (2 * count), *([held] * 2 if load else [])),
            [first[None]],
            (
                *[pltpu.VMEM((4 * rows, width), BF16)] * count,
                pltpu.SemaphoreType.DMA((count, 4)),
                pltpu.SemaphoreType.DMA((4,)),
            ),
            limit=10,
            flops=count * 2 * 2 * tokens * 4 * rows * width,
            smem=1,
            resident=() if load else (activations_in, other_in),
            kept=[activations] if load else [],
            anywhere=([other] if load else []) + used,
        )

    *results, activations_in, other_in = forward([0], True)
    results += forward([3, 1], False)
    flops = 2 * tokens * 4 * rows * width
    far_other, fresh = call(
        far_kernel,
        (block, pltpu.VMEM((4 * rows, width), BF16)),
        [first[None]],
        (pltpu.SemaphoreType.DMA((4,)),),
        flops=flops,
        smem=1,
        resident=(other_in,),
        anywhere=(far_top, far_bottom),
    )
    far_own = call(own_kernel, block, (), flops=flops, resident=(activations_in, fresh))
    results += (far_own, far_other)
    mine, theirs = [None] * 4, [None] * 4
    for n, g in enumerate((0, 3, 1, 2)):
        mine[g] = results[2 * n]
        theirs[g] = fetch(results[2 * n + 1], sibling)
    where = jnp.stack([core.astype(jnp.int32), second, first])
    projected = call(
        weave_kernel,
        shape((tokens, 32 * rows), BF16),
        (where, *mine, *theirs),
        (
            pltpu.VMEM((2, 4, tokens, 4 * rows), BF16),
            pltpu.VMEM((16, tokens, 2 * rows), BF16),
            pltpu.SemaphoreType.DMA((16,)),
        ),
        smem=1,
        out_space=pl.ANY,
    )
    return (new_momentum, direction, projected)


def solution(mesh):
    return jax.shard_map(
        on_device,
        mesh=mesh,
        in_specs=(
            P("rep", "fsdp", None),
            P("rep", "fsdp", None),
            P("fsdp", None),
            P(("rep", "fsdp"), None),
        ),
        out_specs=(P("rep", "fsdp", None), P("fsdp", None), P(("rep", "fsdp"), None)),
        check_vma=False,
    )
```
